32 devices in a mesh: row: 8 (over z, x), col: 4 (over y, core).
Axes of the slice: x: 2, y: 2, z: 4, core: 2. Of those that a mesh axis runs over, the one named last changes fastest.
Arguments:
- features: bfloat16 [8192, 602], P(('row', 'col')), may hold values from -6 to 6
- adjacency: bfloat16 [8192, 8192], P('col', 'row'), may hold values from -0.09375 to 0.09375
- occupancy: int32 [16, 32], P('col', 'row'), may hold values 0 or 1
- labels: int32 [8192], P(('row', 'col')), may hold values from 0 to 40
- train_mask: int32 [8192], P(('row', 'col')), may hold values from 0 to 1, as said below
- node_count: int32 [32], P(('row', 'col')), may hold values from 129 to 256
- weight_one: float32 [602, 256], replicated, may hold values from -0.25 to 0.25
- weight_two: float32 [256, 256], replicated, may hold values from -0.375 to 0.375
- weight_three: float32 [256, 41], replicated, may hold values from -0.375 to 0.375
- biases: float32 [553], replicated, may hold values from -0.6 to 0.6
- first_one: float32 [602, 256], replicated, may hold values from -0.013671875 to 0.013671875
- first_two: float32 [256, 256], replicated, may hold values from -0.013671875 to 0.013671875
- first_three: float32 [256, 41], replicated, may hold values from -0.013671875 to 0.013671875
- first_bias: float32 [553], replicated, may hold values from -0.013671875 to 0.013671875
- second_one: float32 [602, 256], replicated, as said below
- second_two: float32 [256, 256], replicated, as said below
- second_three: float32 [256, 41], replicated, as said below
- second_bias: float32 [553], replicated, as said below
Outputs:
- new_first_one: float32 [602, 256], replicated
- new_second_one: float32 [602, 256], replicated
- new_weight_one: float32 [602, 256], replicated
- new_first_two: float32 [256, 256], replicated
- new_second_two: float32 [256, 256], replicated
- new_weight_two: float32 [256, 256], replicated
- new_first_three: float32 [256, 41], replicated
- new_second_three: float32 [256, 41], replicated
- new_weight_three: float32 [256, 41], replicated
- new_first_bias: float32 [553], replicated
- new_second_bias: float32 [553], replicated
- new_biases: float32 [553], replicated
- loss_sum: float32 [], replicated
- train_count: float32 [], replicated
The draws below stay inside these ranges and needn't reach their ends.
Inputs may be any that keep to these rules, and one draw needn't show every extreme that they name: `train_mask`: 0 or 1; the share of training nodes differs between blocks. `second_one`: positive. `second_two`: positive. `second_three`: positive. `second_bias`: positive.
All inputs are finite; a program needn't handle non-finite values. No bound on the sum of `occupancy` on one device may be relied on, other than what follows from the above.
Results may differ from the reference program's by a relative error of at most 0.0095.
Values may be sent and summed in bfloat16 or wider, within the bound.
A program may use at most 192 MiB of HBM per device.

```python
import jax
import jax.numpy as jnp
from jax import lax

FEAT = 602
HID = 256
CLASSES = 41
NODE_DEV = 256
SUB = 512
STEP = 5
NODES = 8192
NBLK = 32
BIAS = 553
N_ROW = 8
N_COL = 4


def moment_scale(key, shape):
    return 0.04 / NODES * jax.random.uniform(key, shape, jnp.float32, 1.0, 4.0)


def draw_train_mask(key, part):
    key = jax.random.fold_in(key, 3)
    node = jnp.arange(NODES, dtype=jnp.int32)
    block = node // NODE_DEV
    row_place = block // N_COL
    col_place = block % N_COL
    limit = 8 * (N_ROW - 1 + 2 * row_place) * (N_COL - 1 + 2 * col_place) // ((N_ROW - 1) * (N_COL - 1))
    drawn = jax.random.randint(key, (NODES,), 0, 100)
    return (drawn < limit).astype(jnp.int32)


def draw_node_count(key, part):
    key = jax.random.fold_in(key, 5)
    counts = NODE_DEV - jax.random.randint(key, (NBLK,), 0, NODE_DEV // 2)
    fullest = jax.random.randint(jax.random.fold_in(key, 1), (), 0, NBLK)
    least = (fullest + 1 + jax.random.randint(jax.random.fold_in(key, 2), (), 0, NBLK - 1)) % NBLK
    place = jnp.arange(NBLK, dtype=jnp.int32)
    counts = jnp.where(place == least, NODE_DEV - NODE_DEV // 2 + 1, counts)
    return jnp.where(place == fullest, NODE_DEV, counts).astype(jnp.int32)


def draw_second_one(key, part):
    key = jax.random.fold_in(key, 11)
    return moment_scale(key, (FEAT, HID))


def draw_second_two(key, part):
    key = jax.random.fold_in(key, 12)
    return moment_scale(key, (HID, HID))


def draw_second_three(key, part):
    key = jax.random.fold_in(key, 13)
    return moment_scale(key, (HID, CLASSES))


def draw_second_bias(key, part):
    key = jax.random.fold_in(key, 14)
    return moment_scale(key, (BIAS,))


def plant(values, stream_key, low, top_value):
    longest = values.shape.index(max(values.shape))
    spots = []
    for shift in (0, 1):
        where = [jax.random.randint(jax.random.fold_in(stream_key, axis), (), 0, length) for axis, length in enumerate(values.shape)]
        where[longest] = (where[longest] + shift) % values.shape[longest]
        spots.append(tuple(where))
    return values.at[spots[0]].set(low).at[spots[1]].set(top_value)


def levels(stream_key, extent, cuts, low, high):
    loudness = 1.0
    for position, shards_of in cuts:
        steps = jax.random.uniform(jax.random.fold_in(jax.random.fold_in(stream_key, 6), position), (shards_of,), jnp.float32, low / len(cuts), high / len(cuts))
        loudness = loudness * jnp.repeat(jnp.exp(steps), extent[position] // shards_of).reshape((-1,) + (1,) * (len(extent) - 1 - position))
    return loudness


def scatter_about(key, dims, scale, bound, shards=(), kind=jnp.bfloat16):
    factor_of = levels(key, dims, shards, -0.22, 0.18) if shards else 1.0
    values = jax.random.normal(key, dims, jnp.float32) * scale * factor_of
    return jnp.minimum(jnp.maximum(values, -bound), bound).astype(kind)


def setup_inputs(seed: int = 0) -> dict:
    splits = jax.random.split(jax.random.key(seed), 19)
    features = scatter_about(splits[0], (NODES, FEAT), 1.0, 6.0, ((0, 32),))
    adjacency = scatter_about(splits[1], (NODES, NODES), (NODES // 2) ** -0.5, 0.09375, ((0, 4), (1, 8)))
    occupancy = plant((jax.random.randint(splits[2], (NODES // SUB, NBLK), 0, 2) < 1).astype(jnp.int32), jax.random.fold_in(splits[2], 1), 0, 1)
    labels = plant(jax.random.randint(splits[3], (NODES,), 0, CLASSES), jax.random.fold_in(splits[3], 1), 0, CLASSES - 1).astype(jnp.int32)
    train_mask = draw_train_mask(jax.random.fold_in(splits[18], 71), 0)
    node_count = draw_node_count(jax.random.fold_in(splits[18], 71), 0)
    weight_one = scatter_about(splits[6], (FEAT, HID), FEAT ** -0.5, 0.25, (), jnp.float32)
    weight_two = scatter_about(splits[7], (HID, HID), HID ** -0.5, 0.375, (), jnp.float32)
    weight_three = scatter_about(splits[8], (HID, CLASSES), HID ** -0.5, 0.375, (), jnp.float32)
    biases = scatter_about(splits[9], (BIAS,), 0.1, 0.6, (), jnp.float32)
    first_one = scatter_about(splits[10], (FEAT, HID), (25 * NODES) ** -0.5, 0.013671875, (), jnp.float32)
    first_two = scatter_about(splits[11], (HID, HID), (25 * NODES) ** -0.5, 0.013671875, (), jnp.float32)
    first_three = scatter_about(splits[12], (HID, CLASSES), (25 * NODES) ** -0.5, 0.013671875, (), jnp.float32)
    first_bias = scatter_about(splits[13], (BIAS,), (25 * NODES) ** -0.5, 0.013671875, (), jnp.float32)
    second_one = draw_second_one(jax.random.fold_in(splits[18], 71), 0)
    second_two = draw_second_two(jax.random.fold_in(splits[18], 71), 0)
    second_three = draw_second_three(jax.random.fold_in(splits[18], 71), 0)
    second_bias = draw_second_bias(jax.random.fold_in(splits[18], 71), 0)
    return {"features": features, "adjacency": adjacency, "occupancy": occupancy, "labels": labels, "train_mask": train_mask, "node_count": node_count, "weight_one": weight_one, "weight_two": weight_two, "weight_three": weight_three, "biases": biases, "first_one": first_one, "first_two": first_two, "first_three": first_three, "first_bias": first_bias, "second_one": second_one, "second_two": second_two, "second_three": second_three, "second_bias": second_bias}


B_ONE = 0.5
B_TWO = 0.5
RATE = 0.05
DECAY = 0.01
EPSILON = 1e-08
SMOOTH = 0.1
HIGH = lax.Precision.HIGHEST

@jax.custom_vjp
def low(v):
    return lax.optimization_barrier(v.astype(jnp.bfloat16)).astype(jnp.float32)

@jax.custom_vjp
def low_back(v):
    return v

def low_keep(v):
    return (low(v), None)

def low_pass(kept, grad):
    return (grad,)

def back_keep(v):
    return (v, None)

def back_low(kept, grad):
    return (low(grad),)
low.defvjp(low_keep, low_pass)
low_back.defvjp(back_keep, back_low)

def adam_update(weight, first, second, grad):
    first_new = B_ONE * first + (1.0 - B_ONE) * grad
    second_new = B_TWO * second + (1.0 - B_TWO) * grad * grad
    fix_one = 1.0 - B_ONE ** STEP
    fix_two = 1.0 - B_TWO ** STEP
    step_size = first_new / fix_one / (jnp.sqrt(second_new / fix_two) + EPSILON) + DECAY * weight
    return (first_new, second_new, weight - RATE * step_size)

def reference(features, adjacency, occupancy, labels, train_mask, node_count, weight_one, weight_two, weight_three, biases, first_one, first_two, first_three, first_bias, second_one, second_two, second_three, second_bias):
    node = jnp.arange(NODES, dtype=jnp.int32)
    valid = (node % NODE_DEV < node_count[node // NODE_DEV]).astype(jnp.float32)
    counted = train_mask.astype(jnp.float32) * valid
    train_count = jnp.sum(counted)
    cover = jnp.repeat(jnp.repeat(occupancy.astype(jnp.float32), SUB, axis=0), NODE_DEV, axis=1)
    entries = adjacency.astype(jnp.float32) * cover
    operator = entries.reshape(N_COL, N_ROW, NODE_DEV, NODES).transpose(1, 0, 2, 3).reshape(NODES, NODES)
    inputs = features.astype(jnp.float32) * valid[:, None]
    target = (1.0 - SMOOTH) * jax.nn.one_hot(labels, CLASSES, dtype=jnp.float32) + SMOOTH / CLASSES

    def hop(values):
        return jnp.dot(operator, values, precision=HIGH) + values

    def forward(w_one, w_two, w_three, bias_all):
        hidden = low(inputs)
        for weight, bias in ((w_one, bias_all[:HID]), (w_two, bias_all[HID:2 * HID])):
            mixed = low_back(low(jnp.dot(hidden, low(weight), precision=HIGH)))
            summed = low_back(hop(mixed) + bias)
            hidden = low(jax.nn.gelu(summed)) * valid[:, None]
        pooled = low_back(low(hop(hidden)))
        logits = low_back(jnp.dot(pooled, low(w_three), precision=HIGH) + bias_all[2 * HID:])
        logp = jax.nn.log_softmax(logits, axis=1)
        return jnp.sum(-lax.optimization_barrier(jnp.sum(target * logp, axis=1)) * counted)
    loss_sum, pull = jax.vjp(forward, weight_one, weight_two, weight_three, biases)
    grad_one, grad_two, grad_three, grad_bias = pull(jnp.ones((), jnp.float32) / train_count)
    m_one, v_one, w_one = adam_update(weight_one, first_one, second_one, grad_one)
    m_two, v_two, w_two = adam_update(weight_two, first_two, second_two, grad_two)
    m_three, v_three, w_three = adam_update(weight_three, first_three, second_three, grad_three)
    m_bias, v_bias, w_bias = adam_update(biases, first_bias, second_bias, grad_bias)
    return (m_one, v_one, w_one, m_two, v_two, w_two, m_three, v_three, w_three, m_bias, v_bias, w_bias, loss_sum, train_count)
```

```python
import functools
import math

import jax
import jax.numpy as jnp
from jax import lax
from jax.experimental import pallas as pl
from jax.experimental.pallas import tpu as pltpu
from jax.sharding import PartitionSpec as P

SUB = 512
STEP = 5


B_ONE = 0.5
B_TWO = 0.5
RATE = 0.05
DECAY = 0.01
EPSILON = 1e-08
SMOOTH = 0.1

MESH = pl.DeviceIdType.MESH
LOW = jnp.bfloat16
FULL = jnp.float32
GELU_A = 0.7978845608028654
GELU_B = 0.044715


def adam_update(weight, first, second, grad):
    first_new = B_ONE * first + (1.0 - B_ONE) * grad
    second_new = B_TWO * second + (1.0 - B_TWO) * grad * grad
    fix_one = 1.0 - B_ONE**STEP
    fix_two = 1.0 - B_TWO**STEP
    step_size = first_new / fix_one / (jnp.sqrt(second_new / fix_two) + EPSILON) + DECAY * weight
    return (first_new, second_new, weight - RATE * step_size)


def up(value, unit):
    return -(-value // unit) * unit


def dot(left, right):
    return jnp.dot(left, right, preferred_element_type=FULL)


def dot_nt(left, right):
    return lax.dot_general(left, right, (((1,), (1,)), ((), ())), preferred_element_type=FULL)


def gelu_both(z):
    t = jnp.tanh(GELU_A * (z + GELU_B * z * z * z))
    half = 0.5 * (1.0 + t)
    slope = half + 0.5 * z * (1.0 - t * t) * (GELU_A * (1.0 + 3.0 * GELU_B * z * z))
    return z * half, slope


class Sizes:
    def __init__(self, n_row, n_col, own, feat, width, classes):
        self.n_row, self.n_col = n_row, n_col
        self.nk = 2 if n_col % 2 == 0 else 1
        self.ny = n_col // self.nk
        self.nx = self.ny if n_row % self.ny == 0 else 1
        self.nz = n_row // self.nx
        self.own, self.feat, self.width, self.classes = own, feat, width, classes
        self.feat_up = up(feat, 128)
        self.cls = up(classes, 16)
        self.plane = self.nx * self.ny
        self.one_rows = up(feat, 16 * self.plane)
        self.two_rows = up(width + self.cls, 16 * self.plane)
        self.grad_rows = self.one_rows + self.two_rows
        self.lanes = width // self.nk
        self.sends = 4 * (n_row + n_col) + 4 * self.plane
        self.arrivals = 6 * n_row + 8 * n_col + 8 * self.plane + 16


def kernel(
    s,
    xt_ref,
    adj_ref,
    occ_ref,
    lab_ref,
    mask_ref,
    cnt_ref,
    w1_ref,
    w2_ref,
    w3t_ref,
    bias_ref,
    grad_ref,
    misc_ref,
    tile,
    w1b,
    w3t,
    xt_all,
    v_all,
    pool,
    xsend,
    zsend,
    zrecv,
    v3_all,
    p3send,
    p3recv,
    dl_all,
    q3send,
    q3recv,
    acc,
    half_send,
    half_recv,
    half,
    plane_recv,
    quarter,
    fin,
    misc_k,
    misc_p,
    misc_z,
    ssem,
    rsem,
    lsem,
):
    nx, ny, nz, nk = s.nx, s.ny, s.nz, s.nk
    own, width = s.own, s.width
    r, c = lax.axis_index("row"), lax.axis_index("col")
    z, x = r // nx, r % nx
    y, k = c // nk, c % nk

    def at(zz, xx, yy, kk):
        return (zz * nx + xx, yy * nk + kk)

    def xs(d):
        return lax.rem(x + d, nx)

    def ys(d):
        return lax.rem(y + d, ny)

    def zs(d):
        if nz & (nz - 1):
            return lax.rem(z + d, nz)
        there, bit = z, 1
        while bit < nz:
            if d & bit:
                there = there + bit - 2 * bit * lax.rem(there // bit, 2)
            bit *= 2
        return there

    def zback(d):
        return zs(d) if not nz & (nz - 1) else lax.rem(z + nz - d, nz)

    sibling = at(z, x, y, 1 - k)

    rows, cols = tile.shape
    n_sub = rows // SUB
    loads = [
        pltpu.make_async_copy(
            adj_ref.at[pl.ds(a * SUB, SUB)], tile.at[pl.ds(a * SUB, SUB)], lsem.at[a]
        )
        for a in range(n_sub)
    ]
    for load in loads:
        load.start()

    peers = []
    for d in range(1, s.n_row):
        peers.append((lax.rem(r + d, s.n_row), c))
    for d in range(1, s.n_col):
        peers.append((r, lax.rem(c + d, s.n_col)))
    for dx in range(1, nx):
        for dy in range(1, ny):
            peers.append(at(z, xs(dx), ys(dy), k))
    barrier = pltpu.get_barrier_semaphore()
    for peer in peers:
        pl.semaphore_signal(barrier, inc=1, device_id=peer, device_id_type=MESH)

    free = list(range(s.sends))
    pending = []

    def send(src, dst, recv_slot, device, of=None):
        if not free:
            settle(len(pending) - 1)
        copy = pltpu.make_async_remote_copy(
            src_ref=src,
            dst_ref=dst,
            send_sem=ssem.at[free[0]],
            recv_sem=rsem.at[recv_slot],
            device_id=device,
            device_id_type=MESH,
        )
        copy.start()
        pending.append((copy, free.pop(0), of))

    def arrived(dst, recv_slot):
        pltpu.make_async_remote_copy(
            src_ref=dst,
            dst_ref=dst,
            send_sem=ssem.at[0],
            recv_sem=rsem.at[recv_slot],
            device_id=sibling,
            device_id_type=MESH,
        ).wait_recv()

    def settle(keep=0, of=None):
        done = [p for p in pending if p[2] == of] if of else pending[: len(pending) - keep]
        for item in done:
            item[0].wait_send()
            free.append(item[1])
        left = [p for p in pending if all(p is not q for q in done)]
        pending[:] = left

    rcount = [0]

    def rslots(n):
        rcount[0] += n
        return rcount[0] - n

    def row_block(index):
        return pl.ds(pl.multiple_of(index * own, own), own)

    nh = 2
    cut = own // nh

    def row_part(index, q):
        return pl.ds(pl.multiple_of(index * own + q * cut, cut), cut)

    def part(q):
        return pl.ds(q * cut, cut)

    valid_col = (lax.broadcasted_iota(jnp.int32, (own, width), 0) < cnt_ref[0]).astype(FULL)
    valid_low = valid_col.astype(LOW)
    valid_row = (lax.broadcasted_iota(jnp.int32, (1, own), 1) < cnt_ref[0]).astype(FULL)
    counted = mask_ref[...].astype(FULL) * valid_row

    pad = s.feat_up - up(s.feat, 16) + 16
    own_xt = xt_all.at[c]
    own_xt[s.feat_up - pad :, :] = jnp.zeros((pad, own), LOW)
    w1b[s.feat_up - pad :, :] = jnp.zeros((pad, width), LOW)
    x_valid = (lax.broadcasted_iota(jnp.int32, (s.feat, own), 1) < cnt_ref[0]).astype(LOW)
    own_xt[: s.feat, :] = xt_ref[...] * x_valid
    w1b[: s.feat, :] = w1_ref[...].astype(LOW)
    y1 = lax.dot_general(
        own_xt[...], w1b[...], (((0,), (0,)), ((), ())), preferred_element_type=FULL
    ).astype(LOW)

    wide = [rslots(s.n_row * nh) for _ in range(2)]
    gbase = [rslots(s.n_col * nh) for _ in range(2)]

    def start_gather(hop, q, values):
        mine = v_all.at[hop, row_part(c, q)]
        mine[...] = values
        for d in range(1, ny):
            send(mine, mine, gbase[hop] + c * nh + q, at(z, x, ys(d), k))
        if nk > 1:
            send(mine, mine, gbase[hop] + c * nh + q, sibling)

    def complete_gather(hop):
        for q in range(nh):
            for d in range(1, ny):
                source = ys(ny - d) * nk + k
                block = v_all.at[hop, row_part(source, q)]
                arrived(block, gbase[hop] + source * nh + q)
                if nk > 1:
                    send(block, block, gbase[hop] + source * nh + q, sibling)
        if nk > 1:
            for q in range(nh):
                for d in range(ny):
                    source = ys(d) * nk + 1 - k
                    arrived(
                        v_all.at[hop, row_part(source, q)], gbase[hop] + source * nh + q
                    )

    pl.semaphore_wait(barrier, len(peers))
    for q in range(nh):
        start_gather(0, q, y1[q * cut : (q + 1) * cut])

    w3t[...] = jnp.zeros_like(w3t)
    w3t[: s.classes, :] = w3t_ref[...].astype(LOW)
    w2 = w2_ref[...].astype(LOW)
    for a in range(n_sub):
        loads[a].wait()
        for b in range(cols // own):
            piece = tile[pl.ds(a * SUB, SUB), pl.ds(b * own, own)]
            cover = jnp.full((SUB, own), occ_ref[a, b].astype(FULL), FULL).astype(LOW)
            tile[pl.ds(a * SUB, SUB), pl.ds(b * own, own)] = piece * cover

    def spread(hop, finish):
        settle(of="hop")
        with jax.named_scope("gather_y"):
            complete_gather(hop)
        zbase = wide[hop]
        xbase = zbase + nz * nh
        order = list(range(nz - 1, -1, -1))

        def send_x(dz, dx, q):
            place = (dx - 1) * nz + dz
            send(
                xsend.at[place, part(q)],
                pool.at[hop * s.n_row + place, part(q)],
                xbase + place * nh + q,
                at(z, xs(dx), y, k),
                "hop",
            )

        with jax.named_scope("send_x"):
            for dz in order:
                for dx in range(1, nx):
                    place = (dx - 1) * nz + dz
                    rt = zs(dz) * nx + xs(dx)
                    xsend[place] = dot(tile[row_block(rt), :], v_all[hop]).astype(LOW)
                    send_x(dz, dx, 0)
            for q in range(1, nh):
                for dz in order:
                    for dx in range(1, nx):
                        send_x(dz, dx, q)
            for dz in order:
                acc[:, dz * own : (dz + 1) * own] = dot(
                    tile[row_block(zs(dz) * nx + x), :], v_all[hop]
                )

        def send_z(dz, q):
            rows_q = slice(q * cut, (q + 1) * cut)
            total = acc[rows_q, dz * own : (dz + 1) * own]
            for dx in range(1, nx):
                place = (dx - 1) * nz + dz
                arrived(pool.at[hop * s.n_row + place, part(q)], xbase + place * nh + q)
                total = total + pool[hop * s.n_row + place, rows_q, :].astype(FULL)
            if dz:
                zsend[dz - 1, rows_q, :] = total.astype(LOW)
                send(
                    zsend.at[dz - 1, part(q)],
                    zrecv.at[hop, dz - 1, part(q)],
                    zbase + dz * nh + q,
                    at(zs(dz), x, y, k),
                    "hop",
                )
            return total

        totals = [None] * nh

        def sum_z(q):
            total = totals[q]
            rows_q = slice(q * cut, (q + 1) * cut)
            for dz in range(1, nz):
                arrived(zrecv.at[hop, dz - 1, part(q)], zbase + dz * nh + q)
                total = total + zrecv[hop, dz - 1, rows_q, :].astype(FULL)
            finish(q, total)

        with jax.named_scope("send_z"):
            for q in range(nh):
                for i, dz in enumerate(order):
                    totals[q] = send_z(dz, q)
                    if q and i == nz // 2 - 1:
                        with jax.named_scope("sum_z0"):
                            sum_z(q - 1)
        with jax.named_scope("sum_z1"):
            sum_z(nh - 1)

    bias = [bias_ref[i * width : (i + 1) * width].reshape(1, width) for i in range(2)]
    slopes, acts = [None] * nh, [None] * nh

    def first_done(q, total):
        rows_q = slice(q * cut, (q + 1) * cut)
        z1 = total + v_all[0, row_part(c, q), :].astype(FULL) + bias[0]
        act, slope = gelu_both(z1)
        h1 = act.astype(LOW) * valid_low[rows_q]
        start_gather(1, q, dot(h1, w2).astype(LOW))
        acts[q], slopes[q] = h1, slope * valid_col[rows_q]

    spread(0, first_done)
    h1t = jnp.concatenate(acts, axis=0).astype(FULL).T.astype(LOW)
    slope1t = jnp.concatenate(slopes, axis=0).T

    xt_base = rslots(s.n_col)

    def second_done(q, total):
        rows_q = slice(q * cut, (q + 1) * cut)
        z2 = total + v_all[1, row_part(c, q), :].astype(FULL) + bias[1]
        act, slope = gelu_both(z2)
        acts[q] = act.astype(LOW) * valid_low[rows_q]
        slopes[q] = slope * valid_col[rows_q]

    spread(1, second_done)
    h2 = jnp.concatenate(acts, axis=0)
    y3t = dot_nt(w3t[...], h2).astype(LOW)

    with jax.named_scope("hop3_gather"):
        base = rslots(s.n_col)
        mine = v3_all.at[c]
        mine[...] = y3t
        for d in range(1, s.n_col):
            send(mine, mine, base + c, (r, lax.rem(c + d, s.n_col)))
        slope2t = jnp.concatenate(slopes, axis=0).T
        settle(s.n_col - 1)
        for d in range(1, s.n_col):
            source = lax.rem(c + d, s.n_col)
            arrived(v3_all.at[source], base + source)
    with jax.named_scope("hop3_sum"):
        pbase = rslots(s.n_row)
        v3 = jnp.concatenate([v3_all[i] for i in range(s.n_col)], axis=1)
        for d in range(s.n_row - 1, -1, -1):
            rt = lax.rem(r + d, s.n_row)
            here = dot_nt(v3, tile[row_block(rt), :])
            if d:
                p3send[d - 1] = here.astype(LOW)
                send(p3send.at[d - 1], p3recv.at[d - 1], pbase + d, (rt, c))
            else:
                total = here
        for d in range(1, s.n_row):
            arrived(p3recv.at[d - 1], pbase + d)
            total = total + p3recv[d - 1].astype(FULL)
    total = total + y3t.astype(FULL)

    place = lax.broadcasted_iota(jnp.int32, (s.cls, own), 0)
    real = place < s.classes
    on_diag = lax.broadcasted_iota(jnp.int32, (s.cls, s.classes), 0) == lax.broadcasted_iota(
        jnp.int32, (s.cls, s.classes), 1
    )
    bias3 = jnp.sum(
        jnp.where(on_diag, bias_ref[2 * width :].reshape(1, s.classes), 0.0), axis=1, keepdims=True
    )
    logits = jnp.where(real, total + bias3, -1e30)
    shifted = logits - jnp.max(logits, axis=0, keepdims=True)
    weight = jnp.where(real, jnp.exp(shifted), 0.0)
    norm = jnp.sum(weight, axis=0, keepdims=True)
    logp = shifted - jnp.log(norm)
    target = jnp.where(place == lab_ref[...], 1.0 - SMOOTH, 0.0) + SMOOTH / s.classes
    target = jnp.where(real, target, 0.0)
    row_loss = -jnp.sum(jnp.where(real, target * logp, 0.0), axis=0, keepdims=True)
    loss = jnp.sum(row_loss * counted, axis=1, keepdims=True)
    number = jnp.sum(counted, axis=1, keepdims=True)
    dlt = ((weight / norm - target) * counted).astype(LOW)

    with jax.named_scope("back3_gather"):
        base = rslots(s.n_row)
        mine = dl_all.at[r]
        mine[...] = dlt
        for d in range(s.n_row - 1, 0, -1):
            send(mine, mine, base + r, (lax.rem(r + d, s.n_row), c))
        here = dot(dlt, tile[row_block(r), :])
        for d in range(1, s.n_row):
            source = lax.rem(r + d, s.n_row)
            arrived(dl_all.at[source], base + source)
            here = here + dot(dl_all[source], tile[row_block(source), :])
        acc[: s.cls, :cols] = here
    with jax.named_scope("back3_sum"):
        qbase = rslots(s.n_col)
        total = dlt.astype(FULL)
        for d in range(s.n_col - 1, -1, -1):
            ct = lax.rem(c + d, s.n_col)
            here = acc[: s.cls, row_block(ct)]
            if d:
                q3send[d - 1] = here.astype(LOW)
                send(q3send.at[d - 1], q3recv.at[d - 1], qbase + d, (r, ct))
            else:
                total = total + here
        for d in range(1, s.n_col):
            arrived(q3recv.at[d - 1], qbase + d)
            total = total + q3recv[d - 1].astype(FULL)
    qt = total.astype(LOW)
    dh2t = lax.dot_general(
        w3t[...], qt, (((0,), (0,)), ((), ())), preferred_element_type=FULL
    )
    step_cols = min(cols, 1024)

    def gained(values, block, fresh=False):
        for j in range(0, cols, step_cols):
            here = dot(values, tile[block, j : j + step_cols])
            if fresh:
                acc[:, j : j + step_cols] = here
            else:
                acc[:, j : j + step_cols] += here

    def receive(hop, values, meanwhile=None):
        base = wide[hop]
        first = hop * s.n_row
        pool[first] = values
        for q in range(nh):
            mine = pool.at[first, part(q)]
            for dz in range(nz - 1, 0, -1):
                send(
                    mine,
                    pool.at[first + dz, part(q)],
                    base + dz * nh + q,
                    at(zs(dz), x, y, k),
                )
            for dx in range(1, nx):
                place = dx * nz
                send(
                    mine,
                    pool.at[first + place, part(q)],
                    base + place * nh + q,
                    at(z, xs(dx), y, k),
                )

        def source(dz, dx):
            return row_block(zback(dz) * nx + xs(nx - dx))

        gained(values, row_block(r), fresh=True)
        if meanwhile is not None:
            meanwhile()
        for q in range(nh):
            for dz in range(1, nz):
                arrived(pool.at[first + dz, part(q)], base + dz * nh + q)
                for dx in range(1, nx):
                    place = dx * nz + dz
                    send(
                        pool.at[first + dz, part(q)],
                        pool.at[first + place, part(q)],
                        base + place * nh + q,
                        at(z, xs(dx), y, k),
                    )
                if q == nh - 1:
                    gained(pool[first + dz], source(dz, 0))
        for dz in range(nz):
            for dx in range(1, nx):
                place = dx * nz + dz
                for q in range(nh):
                    arrived(pool.at[first + place, part(q)], base + place * nh + q)
                gained(pool[first + place], source(dz, dx))

    dz2t = (dh2t * slope2t).astype(LOW)

    def features_out():
        for d in range(1, ny):
            send(own_xt, own_xt, xt_base + c, at(z, x, ys(d), k))
        if nk > 1:
            send(own_xt, own_xt, xt_base + c, sibling)

    with jax.named_scope("back2_rows"):
        settle()
        receive(0, dz2t, features_out)
    with jax.named_scope("back2_cols"):
        cbase = rslots(ny)
        ybase = rslots(ny)

        def crecv(dy):
            return v_all.at[0, dy * own : (dy + 1) * own]

        def yrecv(dy):
            return crecv(dy + (ny if nk > 1 else 0))

        for dy in range(ny - 1, -1, -1):
            if nk > 1:
                xsend[dy] = acc[:, row_block(ys(dy) * nk + 1 - k)].astype(LOW)
                send(xsend.at[dy], crecv(dy), cbase + dy, sibling)
        total = dz2t.astype(FULL)
        for dy in range(ny - 1, -1, -1):
            here = acc[:, row_block(ys(dy) * nk + k)]
            if nk > 1:
                arrived(crecv(dy), cbase + dy)
                here = here + crecv(dy)[...].astype(FULL)
            if dy:
                xsend[ny + dy] = here.astype(LOW)
                send(xsend.at[ny + dy], yrecv(dy), ybase + dy, at(z, x, ys(dy), k))
            else:
                total = total + here
        for d in range(1, ny):
            source = ys(ny - d) * nk + k
            arrived(xt_all.at[source], xt_base + source)
            if nk > 1:
                send(xt_all.at[source], xt_all.at[source], xt_base + source, sibling)
        for dy in range(1, ny):
            arrived(yrecv(dy), ybase + dy)
            total = total + yrecv(dy)[...].astype(FULL)
    dy2t = total.astype(LOW)
    dz1t = (dot(w2, dy2t) * slope1t).astype(LOW)

    lanes, plane = s.lanes, s.plane
    me = y * nx + x
    others = [(dx, dy) for dx in range(nx) for dy in range(ny) if dx or dy]

    def lane_block(index):
        return pl.ds(pl.multiple_of(index * lanes, lanes), lanes)

    class Total:
        def __init__(self, start, rows):
            self.all = pl.ds(start, rows)
            self.start, self.rows = start, rows
            self.n = rows // plane
            self.short = pl.ds(start // plane, self.n)
            self.base = rslots(1 + 3 * plane + nz)

        def piece(self, index):
            return pl.ds(pl.multiple_of(self.start + index * self.n, 16), self.n)

        def core_send(self, other):
            if nk > 1:
                half_send[self.all, :] = other.astype(LOW)
                send(half_send.at[self.all], half_recv.at[self.all], self.base, sibling)

        def plane_send(self, mine):
            if nk > 1:
                arrived(half_recv.at[self.all], self.base)
                mine = mine + half_recv[self.all, :].astype(FULL)
            half[self.all, :] = mine.astype(LOW)
            base = self.base + 1
            for dx, dy in others:
                there = ys(dy) * nx + xs(dx)
                send(
                    half.at[self.piece(there)],
                    plane_recv.at[me, self.short],
                    base + me,
                    at(z, xs(dx), ys(dy), k),
                )
            plane_recv[me, self.short, :] = half[self.piece(me), :]

        def line_send(self):
            base = self.base + 1
            for dx, dy in others:
                there = ys(dy) * nx + xs(dx)
                arrived(plane_recv.at[there, self.short], base + there)
            total = plane_recv[0, self.short, :].astype(FULL)
            for i in range(1, plane):
                total = total + plane_recv[i, self.short, :].astype(FULL)
            quarter[z, self.short, :] = total.astype(LOW)
            mine = quarter.at[z, self.short]
            base = self.base + 1 + plane
            for dz in range(nz - 1, 0, -1):
                send(mine, mine, base + z, at(zs(dz), x, y, k))

        def back_send(self):
            base = self.base + 1 + plane
            for dz in range(1, nz):
                arrived(quarter.at[zback(dz), self.short], base + zback(dz))
            total = quarter[0, self.short, :].astype(FULL)
            for i in range(1, nz):
                total = total + quarter[i, self.short, :].astype(FULL)
            base = self.base + 1 + plane + nz
            mine = fin.at[k, self.piece(me)]
            mine[...] = total.astype(LOW)
            for dx, dy in others:
                send(mine, mine, base + me, at(z, xs(dx), ys(dy), k))
            if nk > 1:
                send(mine, mine, base + plane + me, sibling)

        def back_forward(self):
            base = self.base + 1 + plane + nz
            for dx, dy in others:
                there = ys(dy) * nx + xs(dx)
                block = fin.at[k, self.piece(there)]
                arrived(block, base + there)
                if nk > 1:
                    send(block, block, base + plane + there, sibling)

        def end(self):
            base = self.base + 1 + plane + nz
            if nk > 1:
                for i in range(plane):
                    arrived(fin.at[1 - k, self.piece(i)], base + plane + i)

    one = Total(0, s.one_rows)
    two = Total(s.one_rows, s.two_rows)
    tail = s.two_rows - width - s.cls

    def early():
        grad3t = dot(qt, h2)
        grad2 = dot_nt(h1t, dy2t)
        acc_two = jnp.concatenate(
            [grad2, grad3t] + ([jnp.zeros((tail, width), FULL)] if tail else []), axis=0
        )
        if nk > 1:
            first, second = acc_two[:, :lanes], acc_two[:, lanes:]
            low_core = (k == 0).astype(FULL)
            two.core_send(second * low_core + first * (1.0 - low_core))
            two.plane_send(first * low_core + second * (1.0 - low_core))
        else:
            two.plane_send(acc_two)

    with jax.named_scope("back1_rows"):
        receive(1, dz1t, early)
    with jax.named_scope("grad1"):
        two.line_send()
        acc[:, row_block(c)] += dz1t.astype(FULL)
        if nk > 1:
            for d in range(ny):
                source = ys(d) * nk + 1 - k
                arrived(xt_all.at[source], xt_base + source)

        def grad_one(index):
            total = None
            for i in range(s.n_col):
                here = acc[pl.ds(pl.multiple_of(index * lanes, lanes), lanes), :]
                here = dot_nt(xt_all[i], here[:, i * own : (i + 1) * own].astype(LOW))
                total = here if total is None else total + here
            if s.one_rows <= s.feat_up:
                return total[: s.one_rows]
            return jnp.concatenate(
                [total, jnp.zeros((s.one_rows - s.feat_up, lanes), FULL)], axis=0
            )

        if nk > 1:
            one.core_send(grad_one(1 - k))
        mine_one = grad_one(k)
        ones = jnp.ones((8, own), LOW)
        line = lax.broadcasted_iota(jnp.int32, (8, width), 0)
        lane = lax.broadcasted_iota(jnp.int32, (8, width), 1)
        bias_three = jnp.concatenate([dlt, jnp.zeros((width - s.cls, own), LOW)], axis=0)
        misc = jnp.where(line == 0, dot_nt(ones, dz1t), 0.0)
        misc = jnp.where(line == 1, dot_nt(ones, dz2t), misc)
        misc = jnp.where(line == 2, dot_nt(ones, bias_three), misc)
        misc = jnp.where((line == 3) & (lane == 0), loss, misc)
        misc = jnp.where((line == 3) & (lane == 1), number, misc)
        mbase = rslots(1 + plane + nz)
        misc_k[0] = misc
        if nk > 1:
            send(misc_k.at[0], misc_k.at[1], mbase, sibling)

    with jax.named_scope("sum_plane"):
        one.plane_send(mine_one)
        if nk > 1:
            arrived(misc_k.at[1], mbase)
            misc = misc_k[0] + misc_k[1]
        misc_p[me] = misc
        mbase = mbase + 1
        for dx, dy in others:
            send(misc_p.at[me], misc_p.at[me], mbase + me, at(z, xs(dx), ys(dy), k))
        left = len(pending)
        two.back_send()
    with jax.named_scope("sum_line"):
        one.line_send()
        for dx, dy in others:
            there = ys(dy) * nx + xs(dx)
            arrived(misc_p.at[there], mbase + there)
        misc = misc_p[0]
        for i in range(1, plane):
            misc = misc + misc_p[i]
        mbase = mbase + plane
        misc_z[z] = misc
        for dz in range(1, nz):
            send(misc_z.at[z], misc_z.at[z], mbase + z, at(zs(dz), x, y, k))
        two.back_forward()
        two.end()
        settle(len(pending) - left)
    with jax.named_scope("back_line"):
        one.back_send()
        for dz in range(1, nz):
            arrived(misc_z.at[zback(dz)], mbase + zback(dz))
        misc = misc_z[0]
        for i in range(1, nz):
            misc = misc + misc_z[i]
        misc_ref[...] = jnp.where(line == 4, 1.0 / misc[3:4, 1:2], misc)
        grad_ref[:, s.one_rows :, :] = fin[:, s.one_rows :, :]
    with jax.named_scope("back_plane"):
        one.back_forward()
        one.end()
        grad_ref[:, : s.one_rows, :] = fin[:, : s.one_rows, :]
    with jax.named_scope("settle"):
        settle()
    assert rcount[0] <= s.arrivals


def adam_kernel(
    s, grad_ref, misc_ref, *refs
):
    ins, outs = refs[:12], refs[12:]
    width, classes, f = s.width, s.classes, s.one_rows
    total = misc_ref[3:4, 1:2]
    scale = misc_ref[4:5, 0:1]
    lanes = s.lanes

    def update(place, rows, lane, grad):
        weight, first, second = (ins[3 * place + i][rows, lane] for i in range(3))
        new = adam_update(weight, first, second, grad * scale)
        for i in range(3):
            outs[3 * place + i][rows, lane] = new[i]

    for i in range(s.nk):
        lane = slice(i * lanes, (i + 1) * lanes)
        update(0, slice(0, s.feat), lane, grad_ref[i, : s.feat, :].astype(FULL))
        update(1, slice(0, width), lane, grad_ref[i, f : f + width, :].astype(FULL))
        update(
            2,
            slice(0, classes),
            lane,
            grad_ref[i, f + width : f + width + s.cls, :].astype(FULL)[:classes],
        )
    for i, size in enumerate((width, width, classes)):
        span = slice(i * width, i * width + size)
        weight, first, second = (ins[9 + j][span] for j in range(3))
        new = adam_update(weight, first, second, misc_ref[i, :size] * misc_ref[4, :size])
        for j in range(3):
            outs[9 + j][span] = new[j]
    outs[12][...] = misc_ref[3:4, 0:1]
    outs[13][...] = total


def shards(
    sizes,
    features,
    adjacency,
    occupancy,
    labels,
    train_mask,
    node_count,
    weight_one,
    weight_two,
    weight_three,
    biases,
    first_one,
    first_two,
    first_three,
    first_bias,
    second_one,
    second_two,
    second_three,
    second_bias,
):
    own, feat = features.shape
    width = weight_two.shape[0]
    classes = weight_three.shape[1]
    s = sizes(own, feat, width, classes)
    rows, cols = adjacency.shape
    lanes = s.lanes
    vmem = pl.BlockSpec(memory_space=pltpu.VMEM)
    smem = pl.BlockSpec(memory_space=pltpu.SMEM)
    block = (own, width)
    small = (s.cls, own)
    shapes = [
        ((rows, cols), LOW),
        ((s.feat_up, width), LOW),
        ((s.cls, width), LOW),
        ((s.n_col, s.feat_up, own), LOW),
        ((2, s.n_col * own, width), LOW),
        ((2 * s.n_row, *block), LOW),
        ((max(2 * s.ny, s.n_row - s.nz), *block), LOW),
        ((max(1, s.nz - 1), *block), LOW),
        ((2, max(1, s.nz - 1), *block), LOW),
        ((s.n_col, *small), LOW),
        ((s.n_row, *small), LOW),
        ((s.n_row, *small), LOW),
        ((s.n_row, *small), LOW),
        ((s.n_col, *small), LOW),
        ((s.n_col, *small), LOW),
        ((width, max(cols, s.nz * own)), FULL),
        ((s.grad_rows, lanes), LOW),
        ((s.grad_rows, lanes), LOW),
        ((s.grad_rows, lanes), LOW),
        ((s.plane, s.grad_rows // s.plane, lanes), LOW),
        ((s.nz, s.grad_rows // s.plane, lanes), LOW),
        ((s.nk, s.grad_rows, lanes), LOW),
        ((2, 8, width), FULL),
        ((s.plane, 8, width), FULL),
        ((s.nz, 8, width), FULL),
    ]
    bytes_held = sum(math.prod(shape) * jnp.dtype(kind).itemsize for shape, kind in shapes)
    limit = 62 * 2**20
    grads, misc = pl.pallas_call(
        functools.partial(kernel, s),
        out_shape=(
            jax.ShapeDtypeStruct((s.nk, s.grad_rows, lanes), LOW),
            jax.ShapeDtypeStruct((8, width), FULL),
        ),
        in_specs=[
            vmem,
            pl.BlockSpec(memory_space=pl.ANY),
            smem,
            vmem,
            vmem,
            smem,
            vmem,
            vmem,
            vmem,
            vmem,
        ],
        out_specs=(vmem, vmem),
        scratch_shapes=[
            *[pltpu.VMEM(shape, kind) for shape, kind in shapes],
            pltpu.SemaphoreType.DMA((s.sends,)),
            pltpu.SemaphoreType.DMA((s.arrivals,)),
            pltpu.SemaphoreType.DMA((rows // SUB,)),
        ],
        compiler_params=pltpu.CompilerParams(
            collective_id=0, has_side_effects=True, vmem_limit_bytes=limit
        ),
        cost_estimate=pl.CostEstimate(
            flops=12 * rows * cols * width, bytes_accessed=2 * rows * cols, transcendentals=0
        ),
        name="step",
    )(
        features.T,
        adjacency,
        occupancy,
        labels.reshape(1, own),
        train_mask.reshape(1, own),
        node_count,
        weight_one,
        weight_two,
        weight_three.T,
        biases,
    )
    state = (
        weight_one,
        first_one,
        second_one,
        weight_two,
        first_two,
        second_two,
        weight_three.T,
        first_three.T,
        second_three.T,
        biases,
        first_bias,
        second_bias,
    )
    new = pl.pallas_call(
        functools.partial(adam_kernel, s),
        out_shape=(
            *[jax.ShapeDtypeStruct(a.shape, FULL) for a in state],
            jax.ShapeDtypeStruct((1, 1), FULL),
            jax.ShapeDtypeStruct((1, 1), FULL),
        ),
        in_specs=[vmem] * 14,
        out_specs=(vmem,) * 14,
        compiler_params=pltpu.CompilerParams(vmem_limit_bytes=62 * 2**20),
        name="update",
    )(grads, misc, *state)
    return (
        *new[:6],
        *[a.T for a in new[6:9]],
        *new[9:12],
        new[12].reshape(()),
        new[13].reshape(()),
    )


def solution(mesh):
    placed = (
        P(("row", "col"), None),
        P("col", "row"),
        P("col", "row"),
        P(("row", "col")),
        P(("row", "col")),
        P(("row", "col")),
        *[P()] * 12,
    )
    sizes = functools.partial(Sizes, mesh.shape["row"], mesh.shape["col"])
    return jax.shard_map(
        functools.partial(shards, sizes),
        mesh=mesh,
        in_specs=placed,
        out_specs=(P(),) * 14,
        check_vma=False,
    )
```

```python
import functools
import math

import jax
import jax.numpy as jnp
from jax import lax
from jax.experimental import pallas as pl
from jax.experimental.pallas import tpu as pltpu
from jax.sharding import PartitionSpec as P

SUB = 512
STEP = 5


B_ONE = 0.5
B_TWO = 0.5
RATE = 0.05
DECAY = 0.01
EPSILON = 1e-08
SMOOTH = 0.1

MESH = pl.DeviceIdType.MESH
LOW = jnp.bfloat16
FULL = jnp.float32
GELU_A = 0.7978845608028654
GELU_B = 0.044715


def adam_update(weight, first, second, grad):
    first_new = B_ONE * first + (1.0 - B_ONE) * grad
    second_new = B_TWO * second + (1.0 - B_TWO) * grad * grad
    fix_one = 1.0 - B_ONE**STEP
    fix_two = 1.0 - B_TWO**STEP
    step_size = first_new / fix_one / (jnp.sqrt(second_new / fix_two) + EPSILON) + DECAY * weight
    return (first_new, second_new, weight - RATE * step_size)


def up(value, unit):
    return -(-value // unit) * unit


def dot(left, right):
    return jnp.dot(left, right, preferred_element_type=FULL)


def dot_nt(left, right):
    return lax.dot_general(left, right, (((1,), (1,)), ((), ())), preferred_element_type=FULL)


def gelu_both(z):
    t = jnp.tanh(GELU_A * (z + GELU_B * z * z * z))
    half = 0.5 * (1.0 + t)
    slope = half + 0.5 * z * (1.0 - t * t) * (GELU_A * (1.0 + 3.0 * GELU_B * z * z))
    return z * half, slope


class Sizes:
    def __init__(self, n_row, n_col, own, feat, width, classes):
        self.n_row, self.n_col = n_row, n_col
        self.nk = 2 if n_col % 2 == 0 else 1
        self.ny = n_col // self.nk
        self.nx = self.ny if n_row % self.ny == 0 else 1
        self.nz = n_row // self.nx
        self.own, self.feat, self.width, self.classes = own, feat, width, classes
        self.feat_up = up(feat, 128)
        self.cls = up(classes, 16)
        self.plane = self.nx * self.ny
        self.one_rows = up(feat, 16 * self.plane)
        self.two_rows = up(width + self.cls, 16 * self.plane)
        self.grad_rows = self.one_rows + self.two_rows
        self.lanes = width // self.nk
        units = self.one_rows // (16 * self.plane)
        self.cut_rows = (units + 1) // 2 * 16 * self.plane
        self.nh = 4
        self.sends = 3 * (n_row + n_col) + 3 * self.plane
        wide = 2 * self.nh * (n_row + n_col)
        self.arrivals = wide + 2 * (n_row + n_col) + n_col + 4 * self.ny
        self.arrivals += 3 * (1 + 3 * self.plane + self.nz) + 1 + self.plane + self.nz


def kernel(
    s,
    xt_ref,
    adj_ref,
    occ_ref,
    lab_ref,
    mask_ref,
    cnt_ref,
    w1_ref,
    w2_ref,
    w3t_ref,
    bias_ref,
    grad_ref,
    misc_ref,
    tile,
    w1b,
    w3t,
    xt_all,
    v_all,
    pool,
    xsend,
    zsend,
    zrecv,
    v3_all,
    p3send,
    p3recv,
    dl_all,
    q3send,
    q3recv,
    acc,
    half_send,
    half_recv,
    half,
    plane_recv,
    quarter,
    fin,
    misc_k,
    misc_p,
    misc_z,
    ssem,
    rsem,
    lsem,
):
    nx, ny, nz, nk = s.nx, s.ny, s.nz, s.nk
    own, width = s.own, s.width
    r, c = lax.axis_index("row"), lax.axis_index("col")
    z, x = r // nx, r % nx
    y, k = c // nk, c % nk

    def at(zz, xx, yy, kk):
        return (zz * nx + xx, yy * nk + kk)

    def xs(d):
        return lax.rem(x + d, nx)

    def ys(d):
        return lax.rem(y + d, ny)

    def zs(d):
        if nz & (nz - 1):
            return lax.rem(z + d, nz)
        there, bit = z, 1
        while bit < nz:
            if d & bit:
                there = there + bit - 2 * bit * lax.rem(there // bit, 2)
            bit *= 2
        return there

    def zback(d):
        return zs(d) if not nz & (nz - 1) else lax.rem(z + nz - d, nz)

    sibling = at(z, x, y, 1 - k)

    rows, cols = tile.shape
    n_sub = rows // SUB
    loads = [
        pltpu.make_async_copy(
            adj_ref.at[pl.ds(a * SUB, SUB)], tile.at[pl.ds(a * SUB, SUB)], lsem.at[a]
        )
        for a in range(n_sub)
    ]
    for load in loads:
        load.start()

    peers = []
    for d in range(1, s.n_row):
        peers.append((lax.rem(r + d, s.n_row), c))
    for d in range(1, s.n_col):
        peers.append((r, lax.rem(c + d, s.n_col)))
    for dx in range(1, nx):
        for dy in range(1, ny):
            peers.append(at(z, xs(dx), ys(dy), k))
    barrier = pltpu.get_barrier_semaphore()
    for peer in peers:
        pl.semaphore_signal(barrier, inc=1, device_id=peer, device_id_type=MESH)

    free = list(range(s.sends))
    pending = []

    def send(src, dst, recv_slot, device, of=None, when=None):
        if not free:
            settle(len(pending) - 1)
        copy = pltpu.make_async_remote_copy(
            src_ref=src,
            dst_ref=dst,
            send_sem=ssem.at[free[0]],
            recv_sem=rsem.at[recv_slot],
            device_id=device,
            device_id_type=MESH,
        )
        if when is None:
            copy.start()
        else:
            pl.when(when)(copy.start)
        pending.append((copy, free.pop(0), of, when))

    def arrived(dst, recv_slot):
        pltpu.make_async_remote_copy(
            src_ref=dst,
            dst_ref=dst,
            send_sem=ssem.at[0],
            recv_sem=rsem.at[recv_slot],
            device_id=sibling,
            device_id_type=MESH,
        ).wait_recv()

    def settle(keep=0, of=None):
        done = [p for p in pending if p[2] == of] if of else pending[: len(pending) - keep]
        for item in done:
            if item[3] is None:
                item[0].wait_send()
            else:
                pl.when(item[3])(item[0].wait_send)
            free.append(item[1])
        left = [p for p in pending if all(p is not q for q in done)]
        pending[:] = left

    rcount = [0]

    def rslots(n):
        rcount[0] += n
        return rcount[0] - n

    def row_block(index):
        return pl.ds(pl.multiple_of(index * own, own), own)

    nh = s.nh
    cut = own // nh

    def row_part(index, q):
        return pl.ds(pl.multiple_of(index * own + q * cut, cut), cut)

    def part(q):
        return pl.ds(q * cut, cut)

    valid_col = (lax.broadcasted_iota(jnp.int32, (own, width), 0) < cnt_ref[0]).astype(FULL)
    valid_low = valid_col.astype(LOW)
    valid_row = (lax.broadcasted_iota(jnp.int32, (1, own), 1) < cnt_ref[0]).astype(FULL)
    counted = mask_ref[...].astype(FULL) * valid_row

    prologue = jax.named_scope("prologue")
    prologue.__enter__()
    pad = s.feat_up - up(s.feat, 16) + 16
    own_xt = xt_all.at[c]
    own_xt[s.feat_up - pad :, :] = jnp.zeros((pad, own), LOW)
    w1b[s.feat_up - pad :, :] = jnp.zeros((pad, width), LOW)
    x_valid = (lax.broadcasted_iota(jnp.int32, (s.feat, own), 1) < cnt_ref[0]).astype(LOW)
    own_xt[: s.feat, :] = xt_ref[...] * x_valid
    w1b[: s.feat, :] = w1_ref[...].astype(LOW)
    y1 = lax.dot_general(
        own_xt[...], w1b[...], (((0,), (0,)), ((), ())), preferred_element_type=FULL
    ).astype(LOW)

    wide = [rslots(s.n_row * nh) for _ in range(2)]
    gbase = [rslots(s.n_col * nh) for _ in range(2)]
    prologue.__exit__(None, None, None)

    def start_gather(hop, q, values):
        mine = v_all.at[hop, row_part(c, q)]
        mine[...] = values
        for d in range(1, ny):
            send(mine, mine, gbase[hop] + c * nh + q, at(z, x, ys(d), k))
        if nk > 1:
            send(mine, mine, gbase[hop] + c * nh + q, sibling)

    def complete_gather(hop):
        for q in range(nh):
            for d in range(1, ny):
                source = ys(ny - d) * nk + k
                block = v_all.at[hop, row_part(source, q)]
                arrived(block, gbase[hop] + source * nh + q)
                if nk > 1:
                    send(block, block, gbase[hop] + source * nh + q, sibling)
        if nk > 1:
            for q in range(nh):
                for d in range(ny):
                    source = ys(d) * nk + 1 - k
                    arrived(
                        v_all.at[hop, row_part(source, q)], gbase[hop] + source * nh + q
                    )

    with jax.named_scope("barrier"):
        pl.semaphore_wait(barrier, len(peers))
    for q in range(nh):
        start_gather(0, q, y1[q * cut : (q + 1) * cut])

    w3t[...] = jnp.zeros_like(w3t)
    w3t[: s.classes, :] = w3t_ref[...].astype(LOW)
    w2 = w2_ref[...].astype(LOW)
    for a in range(n_sub):
        loads[a].wait()
        for b in range(cols // own):
            piece = tile[pl.ds(a * SUB, SUB), pl.ds(b * own, own)]
            cover = jnp.full((SUB, own), occ_ref[a, b].astype(FULL), FULL).astype(LOW)
            tile[pl.ds(a * SUB, SUB), pl.ds(b * own, own)] = piece * cover

    def spread(hop, finish):
        settle(of="hop")
        with jax.named_scope("gather_y"):
            complete_gather(hop)
        zbase = wide[hop]
        xbase = zbase + nz * nh
        order = list(range(nz - 1, -1, -1))

        def send_x(dz, dx, q):
            place = (dx - 1) * nz + dz
            send(
                xsend.at[place, part(q)],
                pool.at[hop * s.n_row + place, part(q)],
                xbase + place * nh + q,
                at(z, xs(dx), y, k),
                "hop",
            )

        sequence = []
        for q in range(nh):
            sequence += [(dz, q) for dz in order if dz]
            if q:
                sequence.append((0, q - 1))
        sequence.append((0, nh - 1))
        ready = set()
        with jax.named_scope("send_x"):
            for dz, q in sequence:
                for dx in range(1, nx):
                    if (dz, dx) not in ready:
                        ready.add((dz, dx))
                        rt = zs(dz) * nx + xs(dx)
                        xsend[(dx - 1) * nz + dz] = dot(
                            tile[row_block(rt), :], v_all[hop]
                        ).astype(LOW)
                    send_x(dz, dx, q)
            for dz in order:
                acc[:, dz * own : (dz + 1) * own] = dot(
                    tile[row_block(zs(dz) * nx + x), :], v_all[hop]
                )

        def send_z(dz, q):
            rows_q = slice(q * cut, (q + 1) * cut)
            total = acc[rows_q, dz * own : (dz + 1) * own]
            for dx in range(1, nx):
                place = (dx - 1) * nz + dz
                arrived(pool.at[hop * s.n_row + place, part(q)], xbase + place * nh + q)
                total = total + pool[hop * s.n_row + place, rows_q, :].astype(FULL)
            if dz:
                zsend[dz - 1, rows_q, :] = total.astype(LOW)
                send(
                    zsend.at[dz - 1, part(q)],
                    zrecv.at[hop, dz - 1, part(q)],
                    zbase + dz * nh + q,
                    at(zs(dz), x, y, k),
                    "hop",
                )
            return total

        totals = [None] * nh

        def sum_z(q):
            total = totals[q]
            rows_q = slice(q * cut, (q + 1) * cut)
            for dz in range(1, nz):
                arrived(zrecv.at[hop, dz - 1, part(q)], zbase + dz * nh + q)
                total = total + zrecv[hop, dz - 1, rows_q, :].astype(FULL)
            finish(q, total)

        with jax.named_scope("send_z"):
            for dz, q in sequence[:-1]:
                totals[q] = send_z(dz, q)
                if not dz:
                    with jax.named_scope("sum_z0"):
                        sum_z(q)
        with jax.named_scope("sum_z1"):
            totals[nh - 1] = send_z(0, nh - 1)
            sum_z(nh - 1)

    bias = [bias_ref[i * width : (i + 1) * width].reshape(1, width) for i in range(2)]
    slopes, acts = [None] * nh, [None] * nh

    def first_done(q, total):
        rows_q = slice(q * cut, (q + 1) * cut)
        z1 = total + v_all[0, row_part(c, q), :].astype(FULL) + bias[0]
        act, slope = gelu_both(z1)
        h1 = act.astype(LOW) * valid_low[rows_q]
        start_gather(1, q, dot(h1, w2).astype(LOW))
        acts[q], slopes[q] = h1, slope * valid_col[rows_q]

    spread(0, first_done)
    h1t = jnp.concatenate(acts, axis=0).astype(FULL).T.astype(LOW)
    slope1t = jnp.concatenate(slopes, axis=0).T

    xt_base = rslots(s.n_col)

    def second_done(q, total):
        rows_q = slice(q * cut, (q + 1) * cut)
        z2 = total + v_all[1, row_part(c, q), :].astype(FULL) + bias[1]
        act, slope = gelu_both(z2)
        acts[q] = act.astype(LOW) * valid_low[rows_q]
        slopes[q] = slope * valid_col[rows_q]

    spread(1, second_done)
    h2 = jnp.concatenate(acts, axis=0)
    y3t = dot_nt(w3t[...], h2).astype(LOW)

    with jax.named_scope("hop3_gather"):
        base = rslots(s.n_col)
        mine = v3_all.at[c]
        mine[...] = y3t
        for d in range(1, s.n_col):
            send(mine, mine, base + c, (r, lax.rem(c + d, s.n_col)))
        slope2t = jnp.concatenate(slopes, axis=0).T
        settle(s.n_col - 1)
        for d in range(1, s.n_col):
            source = lax.rem(c + d, s.n_col)
            arrived(v3_all.at[source], base + source)
    with jax.named_scope("hop3_sum"):
        pbase = rslots(s.n_row)
        v3 = jnp.concatenate([v3_all[i] for i in range(s.n_col)], axis=1)
        for d in range(s.n_row - 1, -1, -1):
            rt = lax.rem(r + d, s.n_row)
            here = dot_nt(v3, tile[row_block(rt), :])
            if d:
                p3send[d - 1] = here.astype(LOW)
                send(p3send.at[d - 1], p3recv.at[d - 1], pbase + d, (rt, c))
            else:
                total = here
        for d in range(1, s.n_row):
            arrived(p3recv.at[d - 1], pbase + d)
            total = total + p3recv[d - 1].astype(FULL)
    total = total + y3t.astype(FULL)

    place = lax.broadcasted_iota(jnp.int32, (s.cls, own), 0)
    real = place < s.classes
    on_diag = lax.broadcasted_iota(jnp.int32, (s.cls, s.classes), 0) == lax.broadcasted_iota(
        jnp.int32, (s.cls, s.classes), 1
    )
    bias3 = jnp.sum(
        jnp.where(on_diag, bias_ref[2 * width :].reshape(1, s.classes), 0.0), axis=1, keepdims=True
    )
    logits = jnp.where(real, total + bias3, -1e30)
    shifted = logits - jnp.max(logits, axis=0, keepdims=True)
    weight = jnp.where(real, jnp.exp(shifted), 0.0)
    norm = jnp.sum(weight, axis=0, keepdims=True)
    logp = shifted - jnp.log(norm)
    target = jnp.where(place == lab_ref[...], 1.0 - SMOOTH, 0.0) + SMOOTH / s.classes
    target = jnp.where(real, target, 0.0)
    row_loss = -jnp.sum(jnp.where(real, target * logp, 0.0), axis=0, keepdims=True)
    loss = jnp.sum(row_loss * counted, axis=1, keepdims=True)
    number = jnp.sum(counted, axis=1, keepdims=True)
    dlt = ((weight / norm - target) * counted).astype(LOW)

    with jax.named_scope("back3_gather"):
        base = rslots(s.n_row)
        mine = dl_all.at[r]
        mine[...] = dlt
        for d in range(s.n_row - 1, 0, -1):
            send(mine, mine, base + r, (lax.rem(r + d, s.n_row), c))
        here = dot(dlt, tile[row_block(r), :])
        for d in range(1, s.n_row):
            source = lax.rem(r + d, s.n_row)
            arrived(dl_all.at[source], base + source)
            here = here + dot(dl_all[source], tile[row_block(source), :])
        acc[: s.cls, :cols] = here
    with jax.named_scope("back3_sum"):
        qbase = rslots(s.n_col)
        total = dlt.astype(FULL)
        for d in range(s.n_col - 1, -1, -1):
            ct = lax.rem(c + d, s.n_col)
            here = acc[: s.cls, row_block(ct)]
            if d:
                q3send[d - 1] = here.astype(LOW)
                send(q3send.at[d - 1], q3recv.at[d - 1], qbase + d, (r, ct))
            else:
                total = total + here
        for d in range(1, s.n_col):
            arrived(q3recv.at[d - 1], qbase + d)
            total = total + q3recv[d - 1].astype(FULL)
    qt = total.astype(LOW)
    dh2t = lax.dot_general(
        w3t[...], qt, (((0,), (0,)), ((), ())), preferred_element_type=FULL
    )
    step_cols = min(cols, 1024)

    def gained(values, block, fresh=False):
        for j in range(0, cols, step_cols):
            here = dot(values, tile[block, j : j + step_cols])
            if fresh:
                acc[:, j : j + step_cols] = here
            else:
                acc[:, j : j + step_cols] += here

    def halves(lane, row):
        return (
            pl.ds(row * (width // 2), width // 2),
            pl.ds(lane * (own // 2), own // 2),
        )

    quarters = [(lane, row) for lane in range(2) for row in range(2)]
    relayed = nz == 4
    inner = lax.rem((z + 1) // 2, 2) == 1

    def receive(hop, values, meanwhile=None):
        base = wide[hop]
        first = hop * s.n_row

        def piece(dz, dx, q):
            return pool.at[(first + dx * nz + dz, *halves(*quarters[q]))]

        def to_z(dz, q, when=None):
            send(
                piece(0, 0, q), piece(dz, 0, q), base + dz * nh + q, at(zs(dz), x, y, k), when=when
            )

        def to_x(dz, q):
            for dx in range(1, nx):
                place = dx * nz + dz
                send(piece(dz, 0, q), piece(dz, dx, q), base + place * nh + q, at(z, xs(dx), y, k))

        own_parts = []
        for lane in range(2):
            mine = values(lane)
            own_parts.append(mine)
            pool[first, :, lane * (own // 2) : (lane + 1) * (own // 2)] = mine
            for q in (2 * lane, 2 * lane + 1):
                if relayed:
                    to_z(2, q, jnp.logical_not(inner))
                    to_z(3, q, inner)
                    to_z(1, q)
                else:
                    for dz in range(nz - 1, 0, -1):
                        to_z(dz, q)
                to_x(0, q)

        def source(dz, dx):
            return row_block(zback(dz) * nx + xs(nx - dx))

        gained(jnp.concatenate(own_parts, axis=1), row_block(r), fresh=True)
        if meanwhile is not None:
            meanwhile()

        def step(dz, q):
            arrived(piece(dz, 0, q), base + dz * nh + q)
            if relayed and dz == 2:
                send(piece(2, 0, q), piece(3, 0, q), base + 3 * nh + q, at(zs(1), x, y, k), when=inner)
                to_z(2, q, inner)
            to_x(dz, q)
            if q == nh - 1:
                gained(pool[first + dz], source(dz, 0))

        if relayed:
            for q in range(nh):
                step(1, q)
                step(2, q)
                if q:
                    step(3, q - 1)
            step(3, nh - 1)
        else:
            for q in range(nh):
                for dz in range(1, nz):
                    step(dz, q)
        for dz in range(nz):
            for dx in range(1, nx):
                for q in range(nh):
                    arrived(piece(dz, dx, q), base + (dx * nz + dz) * nh + q)
                gained(pool[first + dx * nz + dz], source(dz, dx))

    dz2t = (dh2t * slope2t).astype(LOW)
    half_own = own // 2

    def features_out():
        for d in range(1, ny):
            send(own_xt, own_xt, xt_base + c, at(z, x, ys(d), k))
        if nk > 1:
            send(own_xt, own_xt, xt_base + c, sibling)

    with jax.named_scope("back2_rows"):
        settle()
        receive(0, lambda lane: dz2t[:, lane * half_own : (lane + 1) * half_own], features_out)
    cbase = rslots(2 * ny)
    ybase = rslots(2 * ny)

    def lane_part(index, lane):
        return pl.ds(pl.multiple_of(index * own + lane * half_own, half_own), half_own)

    def held(place, lane):
        return xsend.at[place, :, pl.ds(lane * half_own, half_own)]

    def crecv(dy, lane):
        return v_all.at[0, dy * own : (dy + 1) * own, pl.ds(lane * half_own, half_own)]

    def yrecv(dy, lane):
        return crecv(dy + (ny if nk > 1 else 0), lane)

    column_totals = [None, None]
    with jax.named_scope("back2_cols"):
        for lane in range(2):
            for dy in range(ny - 1, -1, -1):
                if nk > 1:
                    there = held(dy, lane)
                    there[...] = acc[:, lane_part(ys(dy) * nk + 1 - k, lane)].astype(LOW)
                    send(there, crecv(dy, lane), cbase + 2 * dy + lane, sibling)
        for lane in range(2):
            for dy in range(ny - 1, -1, -1):
                here = acc[:, lane_part(ys(dy) * nk + k, lane)]
                if nk > 1:
                    arrived(crecv(dy, lane), cbase + 2 * dy + lane)
                    here = here + crecv(dy, lane)[...].astype(FULL)
                if dy:
                    there = held(ny + dy, lane)
                    there[...] = here.astype(LOW)
                    send(
                        there, yrecv(dy, lane), ybase + 2 * dy + lane, at(z, x, ys(dy), k)
                    )
                else:
                    column_totals[lane] = here
        for d in range(1, ny):
            source = ys(ny - d) * nk + k
            arrived(xt_all.at[source], xt_base + source)
            if nk > 1:
                send(xt_all.at[source], xt_all.at[source], xt_base + source, sibling)

    dy2_parts, dz1_parts = [], []

    def first_slopes(lane):
        lanes_q = slice(lane * half_own, (lane + 1) * half_own)
        total = column_totals[lane] + dz2t[:, lanes_q].astype(FULL)
        with jax.named_scope("y_wait"):
            for dy in range(1, ny):
                arrived(yrecv(dy, lane), ybase + 2 * dy + lane)
                total = total + yrecv(dy, lane)[...].astype(FULL)
        dy2_parts.append(total.astype(LOW))
        dz1_parts.append((dot(w2, dy2_parts[lane]) * slope1t[:, lanes_q]).astype(LOW))
        return dz1_parts[lane]

    lanes, plane = s.lanes, s.plane
    me = y * nx + x
    others = [(dx, dy) for dx in range(nx) for dy in range(ny) if dx or dy]

    def lane_block(index):
        return pl.ds(pl.multiple_of(index * lanes, lanes), lanes)

    class Total:
        def __init__(self, start, rows):
            self.all = pl.ds(start, rows)
            self.start, self.rows = start, rows
            self.n = rows // plane
            self.short = pl.ds(start // plane, self.n)
            self.base = rslots(1 + 3 * plane + nz)

        def piece(self, index):
            return pl.ds(pl.multiple_of(self.start + index * self.n, 16), self.n)

        def core_send(self, other):
            if nk > 1:
                half_send[self.all, :] = other.astype(LOW)
                send(half_send.at[self.all], half_recv.at[self.all], self.base, sibling)

        def plane_send(self, mine):
            if nk > 1:
                arrived(half_recv.at[self.all], self.base)
                mine = mine + half_recv[self.all, :].astype(FULL)
            half[self.all, :] = mine.astype(LOW)
            base = self.base + 1
            for dx, dy in others:
                there = ys(dy) * nx + xs(dx)
                send(
                    half.at[self.piece(there)],
                    plane_recv.at[me, self.short],
                    base + me,
                    at(z, xs(dx), ys(dy), k),
                )
            plane_recv[me, self.short, :] = half[self.piece(me), :]

        def line_send(self):
            base = self.base + 1
            for dx, dy in others:
                there = ys(dy) * nx + xs(dx)
                arrived(plane_recv.at[there, self.short], base + there)
            total = plane_recv[0, self.short, :].astype(FULL)
            for i in range(1, plane):
                total = total + plane_recv[i, self.short, :].astype(FULL)
            quarter[z, self.short, :] = total.astype(LOW)
            mine = quarter.at[z, self.short]
            base = self.base + 1 + plane
            for dz in range(nz - 1, 0, -1):
                send(mine, mine, base + z, at(zs(dz), x, y, k))

        def back_send(self):
            base = self.base + 1 + plane
            for dz in range(1, nz):
                arrived(quarter.at[zback(dz), self.short], base + zback(dz))
            total = quarter[0, self.short, :].astype(FULL)
            for i in range(1, nz):
                total = total + quarter[i, self.short, :].astype(FULL)
            base = self.base + 1 + plane + nz
            mine = fin.at[k, self.piece(me)]
            mine[...] = total.astype(LOW)
            for dx, dy in others:
                send(mine, mine, base + me, at(z, xs(dx), ys(dy), k))
            if nk > 1:
                send(mine, mine, base + plane + me, sibling)

        def back_forward(self):
            base = self.base + 1 + plane + nz
            for dx, dy in others:
                there = ys(dy) * nx + xs(dx)
                block = fin.at[k, self.piece(there)]
                arrived(block, base + there)
                if nk > 1:
                    send(block, block, base + plane + there, sibling)

        def end(self):
            base = self.base + 1 + plane + nz
            if nk > 1:
                for i in range(plane):
                    arrived(fin.at[1 - k, self.piece(i)], base + plane + i)

    one_a = Total(0, s.cut_rows)
    one_b = Total(s.cut_rows, s.one_rows - s.cut_rows)
    two = Total(s.one_rows, s.two_rows)
    tail = s.two_rows - width - s.cls

    def early():
        grad3t = dot(qt, h2)
        dy2t = jnp.concatenate(dy2_parts, axis=1)
        grad2 = dot_nt(h1t, dy2t)
        acc_two = jnp.concatenate(
            [grad2, grad3t] + ([jnp.zeros((tail, width), FULL)] if tail else []), axis=0
        )
        if nk > 1:
            first, second = acc_two[:, :lanes], acc_two[:, lanes:]
            low_core = (k == 0).astype(FULL)
            two.core_send(second * low_core + first * (1.0 - low_core))
            two.plane_send(first * low_core + second * (1.0 - low_core))
        else:
            two.plane_send(acc_two)

    with jax.named_scope("back1_rows"):
        receive(1, first_slopes, early)
    with jax.named_scope("grad1"):
        two.line_send()
        dz1t = jnp.concatenate(dz1_parts, axis=1)
        acc[:, row_block(c)] += dz1t.astype(FULL)
        if nk > 1:
            for d in range(ny):
                source = ys(d) * nk + 1 - k
                arrived(xt_all.at[source], xt_base + source)

        def grad_one(index, start, stop):
            total = None
            end = min(stop, s.feat_up)
            for i in range(s.n_col):
                here = acc[pl.ds(pl.multiple_of(index * lanes, lanes), lanes), :]
                here = dot_nt(
                    xt_all[i, start:end, :], here[:, i * own : (i + 1) * own].astype(LOW)
                )
                total = here if total is None else total + here
            if end < stop:
                total = jnp.concatenate([total, jnp.zeros((stop - end, lanes), FULL)], axis=0)
            return total

        if nk > 1:
            one_a.core_send(grad_one(1 - k, 0, s.cut_rows))
            one_b.core_send(grad_one(1 - k, s.cut_rows, s.one_rows))
        one_a.plane_send(grad_one(k, 0, s.cut_rows))
        one_b.plane_send(grad_one(k, s.cut_rows, s.one_rows))
        ones = jnp.ones((8, own), LOW)
        line = lax.broadcasted_iota(jnp.int32, (8, width), 0)
        lane = lax.broadcasted_iota(jnp.int32, (8, width), 1)
        bias_three = jnp.concatenate([dlt, jnp.zeros((width - s.cls, own), LOW)], axis=0)
        misc = jnp.where(line == 0, dot_nt(ones, dz1t), 0.0)
        misc = jnp.where(line == 1, dot_nt(ones, dz2t), misc)
        misc = jnp.where(line == 2, dot_nt(ones, bias_three), misc)
        misc = jnp.where((line == 3) & (lane == 0), loss, misc)
        misc = jnp.where((line == 3) & (lane == 1), number, misc)
        mbase = rslots(1 + plane + nz)
        misc_k[0] = misc
        if nk > 1:
            send(misc_k.at[0], misc_k.at[1], mbase, sibling)

    with jax.named_scope("sum_plane"):
        if nk > 1:
            arrived(misc_k.at[1], mbase)
            misc = misc_k[0] + misc_k[1]
        misc_p[me] = misc
        mbase = mbase + 1
        for dx, dy in others:
            send(misc_p.at[me], misc_p.at[me], mbase + me, at(z, xs(dx), ys(dy), k))
        left = len(pending)
        two.back_send()
    with jax.named_scope("sum_line"):
        one_a.line_send()
        one_b.line_send()
        for dx, dy in others:
            there = ys(dy) * nx + xs(dx)
            arrived(misc_p.at[there], mbase + there)
        misc = misc_p[0]
        for i in range(1, plane):
            misc = misc + misc_p[i]
        mbase = mbase + plane
        misc_z[z] = misc
        for dz in range(1, nz):
            send(misc_z.at[z], misc_z.at[z], mbase + z, at(zs(dz), x, y, k))
        two.back_forward()
        two.end()
        settle(len(pending) - left)
    with jax.named_scope("back_line"):
        one_a.back_send()
        one_b.back_send()
        for dz in range(1, nz):
            arrived(misc_z.at[zback(dz)], mbase + zback(dz))
        misc = misc_z[0]
        for i in range(1, nz):
            misc = misc + misc_z[i]
        misc_ref[...] = jnp.where(line == 4, 1.0 / misc[3:4, 1:2], misc)
        grad_ref[:, s.one_rows :, :] = fin[:, s.one_rows :, :]
    with jax.named_scope("back_plane"):
        one_a.back_forward()
        one_b.back_forward()
        one_a.end()
        one_b.end()
        grad_ref[:, : s.one_rows, :] = fin[:, : s.one_rows, :]
    with jax.named_scope("settle"):
        settle()
    assert rcount[0] <= s.arrivals


def update_pieces(s):
    middle = up(s.feat // 2, 8)
    return (
        (0, 0, middle),
        (0, middle, s.feat - middle),
        (1, 0, s.width),
        (2, 0, s.classes),
    )


def adam_kernel(s, grad_hbm, misc_hbm, *refs):
    ins, outs, scratch = refs[:12], refs[12:26], refs[26:]
    grad_ref, misc_ref, bias_in, bias_out, ends, *held = scratch[:-2]
    sem_in, sem_out = scratch[-2:]
    pieces = update_pieces(s)
    width, classes, lanes = s.width, s.classes, s.lanes
    grad_at = (0, s.one_rows, s.one_rows + width)

    misc_load = pltpu.make_async_copy(misc_hbm, misc_ref, sem_in.at[0])
    grad_load = pltpu.make_async_copy(grad_hbm, grad_ref, sem_in.at[1])
    misc_load.start()
    grad_load.start()
    loads, count = [], 2
    for n, (which, start, rows) in enumerate(pieces):
        mine = []
        for i in range(3):
            mine.append(
                pltpu.make_async_copy(
                    ins[3 * which + i].at[pl.ds(start, rows)], held[2 * n].at[i], sem_in.at[count]
                )
            )
            count += 1
            mine[-1].start()
        loads.append(mine)
    bias_loads = []
    for i in range(3):
        bias_loads.append(
            pltpu.make_async_copy(ins[9 + i], bias_in[i], sem_in.at[count])
        )
        count += 1
        bias_loads[-1].start()

    misc_load.wait()
    grad_load.wait()
    total = misc_ref[3:4, 1:2]
    scale = misc_ref[4:5, 0:1]
    stores, count = [], 2
    ends[0] = misc_ref[3:4, 0:1]
    ends[1] = total
    for i in range(2):
        stores.append(pltpu.make_async_copy(ends.at[i], outs[12 + i], sem_out.at[i]))
        stores[-1].start()
    for n, (which, start, rows) in enumerate(pieces):
        for load in loads[n]:
            load.wait()
        source, target = held[2 * n], held[2 * n + 1]
        for i in range(s.nk):
            lane = slice(i * lanes, (i + 1) * lanes)
            first = grad_at[which] + start
            grad = grad_ref[i, first : first + up(rows, 16), :].astype(FULL)[:rows]
            weight, one, two = (source[j, :, lane] for j in range(3))
            for j, new in enumerate(adam_update(weight, one, two, grad * scale)):
                target[j, :, lane] = new
        for j in range(3):
            stores.append(
                pltpu.make_async_copy(
                    target.at[j], outs[3 * which + j].at[pl.ds(start, rows)], sem_out.at[count]
                )
            )
            count += 1
            stores[-1].start()
    for load in bias_loads:
        load.wait()
    for i, size in enumerate((width, width, classes)):
        span = slice(i * width, i * width + size)
        weight, first, second = (bias_in[j][span] for j in range(3))
        new = adam_update(weight, first, second, misc_ref[i, :size] * misc_ref[4, :size])
        for j in range(3):
            bias_out[j][span] = new[j]
    for j in range(3):
        stores.append(
            pltpu.make_async_copy(bias_out[j], outs[9 + j], sem_out.at[count])
        )
        count += 1
        stores[-1].start()
    for store in stores:
        store.wait()


def shards(
    sizes,
    features,
    adjacency,
    occupancy,
    labels,
    train_mask,
    node_count,
    weight_one,
    weight_two,
    weight_three,
    biases,
    first_one,
    first_two,
    first_three,
    first_bias,
    second_one,
    second_two,
    second_three,
    second_bias,
):
    own, feat = features.shape
    width = weight_two.shape[0]
    classes = weight_three.shape[1]
    s = sizes(own, feat, width, classes)
    rows, cols = adjacency.shape
    lanes = s.lanes
    vmem = pl.BlockSpec(memory_space=pltpu.VMEM)
    smem = pl.BlockSpec(memory_space=pltpu.SMEM)
    anywhere = pl.BlockSpec(memory_space=pl.ANY)
    block = (own, width)
    small = (s.cls, own)
    shapes = [
        ((rows, cols), LOW),
        ((s.feat_up, width), LOW),
        ((s.cls, width), LOW),
        ((s.n_col, s.feat_up, own), LOW),
        ((2, s.n_col * own, width), LOW),
        ((2 * s.n_row, *block), LOW),
        ((max(2 * s.ny, s.n_row - s.nz), *block), LOW),
        ((max(1, s.nz - 1), *block), LOW),
        ((2, max(1, s.nz - 1), *block), LOW),
        ((s.n_col, *small), LOW),
        ((s.n_row, *small), LOW),
        ((s.n_row, *small), LOW),
        ((s.n_row, *small), LOW),
        ((s.n_col, *small), LOW),
        ((s.n_col, *small), LOW),
        ((width, max(cols, s.nz * own)), FULL),
        ((s.grad_rows, lanes), LOW),
        ((s.grad_rows, lanes), LOW),
        ((s.grad_rows, lanes), LOW),
        ((s.plane, s.grad_rows // s.plane, lanes), LOW),
        ((s.nz, s.grad_rows // s.plane, lanes), LOW),
        ((s.nk, s.grad_rows, lanes), LOW),
        ((2, 8, width), FULL),
        ((s.plane, 8, width), FULL),
        ((s.nz, 8, width), FULL),
    ]
    bytes_held = sum(math.prod(shape) * jnp.dtype(kind).itemsize for shape, kind in shapes)
    limit = 62 * 2**20
    grads, misc = pl.pallas_call(
        functools.partial(kernel, s),
        out_shape=(
            jax.ShapeDtypeStruct((s.nk, s.grad_rows, lanes), LOW),
            jax.ShapeDtypeStruct((8, width), FULL),
        ),
        in_specs=[
            vmem,
            anywhere,
            smem,
            vmem,
            vmem,
            smem,
            vmem,
            vmem,
            vmem,
            vmem,
        ],
        out_specs=(vmem, vmem),
        scratch_shapes=[
            *[pltpu.VMEM(shape, kind) for shape, kind in shapes],
            pltpu.SemaphoreType.DMA((s.sends,)),
            pltpu.SemaphoreType.DMA((s.arrivals,)),
            pltpu.SemaphoreType.DMA((rows // SUB,)),
        ],
        compiler_params=pltpu.CompilerParams(
            collective_id=0, has_side_effects=True, vmem_limit_bytes=limit
        ),
        cost_estimate=pl.CostEstimate(
            flops=12 * rows * cols * width, bytes_accessed=2 * rows * cols, transcendentals=0
        ),
        name="step",
    )(
        features.T,
        adjacency,
        occupancy,
        labels.reshape(1, own),
        train_mask.reshape(1, own),
        node_count,
        weight_one,
        weight_two,
        weight_three.T,
        biases,
    )
    state = (
        weight_one,
        first_one,
        second_one,
        weight_two,
        first_two,
        second_two,
        weight_three.T,
        first_three.T,
        second_three.T,
        biases,
        first_bias,
        second_bias,
    )
    new = pl.pallas_call(
        functools.partial(adam_kernel, s),
        out_shape=(
            *[jax.ShapeDtypeStruct(a.shape, FULL) for a in state],
            jax.ShapeDtypeStruct((1, 1), FULL),
            jax.ShapeDtypeStruct((1, 1), FULL),
        ),
        in_specs=[anywhere] * 14,
        out_specs=(anywhere,) * 14,
        scratch_shapes=[
            pltpu.VMEM(grads.shape, LOW),
            pltpu.VMEM(misc.shape, FULL),
            [pltpu.VMEM(biases.shape, FULL)] * 3,
            [pltpu.VMEM(biases.shape, FULL)] * 3,
            pltpu.VMEM((2, 1, 1), FULL),
            *[
                pltpu.VMEM((3, rows, width), FULL)
                for _, _, rows in update_pieces(s)
                for _ in range(2)
            ],
            pltpu.SemaphoreType.DMA((17,)),
            pltpu.SemaphoreType.DMA((17,)),
        ],
        compiler_params=pltpu.CompilerParams(vmem_limit_bytes=62 * 2**20),
        name="update",
    )(grads, misc, *state)
    return (
        *new[:6],
        *[a.T for a in new[6:9]],
        *new[9:12],
        new[12].reshape(()),
        new[13].reshape(()),
    )


def solution(mesh):
    placed = (
        P(("row", "col"), None),
        P("col", "row"),
        P("col", "row"),
        P(("row", "col")),
        P(("row", "col")),
        P(("row", "col")),
        *[P()] * 12,
    )
    sizes = functools.partial(Sizes, mesh.shape["row"], mesh.shape["col"])
    return jax.shard_map(
        functools.partial(shards, sizes),
        mesh=mesh,
        in_specs=placed,
        out_specs=(P(),) * 14,
        check_vma=False,
    )
```

```python
import functools
import math

import jax
import jax.numpy as jnp
from jax import lax
from jax.experimental import pallas as pl
from jax.experimental.pallas import tpu as pltpu
from jax.sharding import PartitionSpec as P

SUB = 512
STEP = 5


B_ONE = 0.5
B_TWO = 0.5
RATE = 0.05
DECAY = 0.01
EPSILON = 1e-08
SMOOTH = 0.1

MESH = pl.DeviceIdType.MESH
LOW = jnp.bfloat16
FULL = jnp.float32
GELU_A = 0.7978845608028654
GELU_B = 0.044715


def adam_update(weight, first, second, grad):
    first_new = B_ONE * first + (1.0 - B_ONE) * grad
    second_new = B_TWO * second + (1.0 - B_TWO) * grad * grad
    fix_one = 1.0 - B_ONE**STEP
    fix_two = 1.0 - B_TWO**STEP
    step_size = first_new / fix_one / (jnp.sqrt(second_new / fix_two) + EPSILON) + DECAY * weight
    return (first_new, second_new, weight - RATE * step_size)


def up(value, unit):
    return -(-value // unit) * unit


def dot(left, right):
    return jnp.dot(left, right, preferred_element_type=FULL)


def dot_nt(left, right):
    return lax.dot_general(left, right, (((1,), (1,)), ((), ())), preferred_element_type=FULL)


def gelu_both(z):
    t = jnp.tanh(GELU_A * (z + GELU_B * z * z * z))
    half = 0.5 * (1.0 + t)
    slope = half + 0.5 * z * (1.0 - t * t) * (GELU_A * (1.0 + 3.0 * GELU_B * z * z))
    return z * half, slope


class Sizes:
    def __init__(self, n_row, n_col, own, feat, width, classes):
        self.n_row, self.n_col = n_row, n_col
        self.nk = 2 if n_col % 2 == 0 else 1
        self.ny = n_col // self.nk
        self.nx = self.ny if n_row % self.ny == 0 else 1
        self.nz = n_row // self.nx
        self.own, self.feat, self.width, self.classes = own, feat, width, classes
        self.feat_up = up(feat, 128)
        self.cls = up(classes, 16)
        self.plane = self.nx * self.ny
        self.one_rows = up(feat, 16 * self.plane)
        self.two_rows = up(width + self.cls, 16 * self.plane)
        self.grad_rows = self.one_rows + self.two_rows
        self.lanes = width // self.nk
        units = self.one_rows // (16 * self.plane)
        self.cut_rows = (units + 1) // 2 * 16 * self.plane
        self.nh = 4
        self.relayed = self.nz == 4
        self.sends = 3 * (n_row + n_col) + 3 * self.plane
        wide = 2 * self.nh * (n_row + n_col)
        self.arrivals = wide + 3 * (1 + 3 * self.plane + self.nz) + 1 + self.plane + self.nz


def kernel(
    s,
    xt_ref,
    adj_ref,
    occ_ref,
    lab_ref,
    mask_ref,
    cnt_ref,
    w1_ref,
    w2_ref,
    w3t_ref,
    bias_ref,
    grad_ref,
    misc_ref,
    tile,
    w1b,
    w3t,
    xt_all,
    v_all,
    pool,
    xsend,
    zsend,
    zrecv,
    v3_all,
    p3send,
    p3recv,
    dl_all,
    q3send,
    q3recv,
    acc,
    half_send,
    half_recv,
    half,
    plane_recv,
    quarter,
    fin,
    misc_k,
    misc_p,
    misc_z,
    ssem,
    rsem,
    lsem,
):
    nx, ny, nz, nk = s.nx, s.ny, s.nz, s.nk
    own, width = s.own, s.width
    r, c = lax.axis_index("row"), lax.axis_index("col")
    z, x = r // nx, r % nx
    y, k = c // nk, c % nk

    def at(zz, xx, yy, kk):
        return (zz * nx + xx, yy * nk + kk)

    def xs(d):
        return lax.rem(x + d, nx)

    def ys(d):
        return lax.rem(y + d, ny)

    def zs(d):
        if nz & (nz - 1):
            return lax.rem(z + d, nz)
        there, bit = z, 1
        while bit < nz:
            if d & bit:
                there = there + bit - 2 * bit * lax.rem(there // bit, 2)
            bit *= 2
        return there

    def zback(d):
        return zs(d) if not nz & (nz - 1) else lax.rem(z + nz - d, nz)

    sibling = at(z, x, y, 1 - k)
    relayed = s.relayed
    is_inner = lax.rem((z + 1) // 2, 2)
    inner = is_inner == 1
    outer = is_inner == 0
    line = [dz for dz in range(nz - 1, -1, -1)]
    row_far = [(dz, dx) for dz in line for dx in range(nx - 1, -1, -1) if dz or dx]
    col_far = [(dy, dk) for dy in range(ny - 1, -1, -1) for dk in range(nk - 1, -1, -1) if dy or dk]

    def ks(d):
        return lax.rem(k + d, nk)


    rows, cols = tile.shape
    n_sub = rows // SUB
    loads = [
        pltpu.make_async_copy(
            adj_ref.at[pl.ds(a * SUB, SUB)], tile.at[pl.ds(a * SUB, SUB)], lsem.at[a]
        )
        for a in range(n_sub)
    ]
    for load in loads:
        load.start()

    peers = []
    for d in range(1, s.n_row):
        peers.append((lax.rem(r + d, s.n_row), c))
    for d in range(1, s.n_col):
        peers.append((r, lax.rem(c + d, s.n_col)))
    for dx in range(1, nx):
        for dy in range(1, ny):
            peers.append(at(z, xs(dx), ys(dy), k))
    barrier = pltpu.get_barrier_semaphore()
    for peer in peers:
        pl.semaphore_signal(barrier, inc=1, device_id=peer, device_id_type=MESH)

    free = list(range(s.sends))
    pending = []

    def send(src, dst, recv_slot, device, of=None, when=None, start=True):
        if not free:
            settle(len(pending) - 1)
        copy = pltpu.make_async_remote_copy(
            src_ref=src,
            dst_ref=dst,
            send_sem=ssem.at[free[0]],
            recv_sem=rsem.at[recv_slot],
            device_id=device,
            device_id_type=MESH,
        )
        if start:
            if when is None:
                copy.start()
            else:
                pl.when(when)(copy.start)
        pending.append((copy, free.pop(0), of, when))
        return copy

    def arrived(dst, recv_slot):
        pltpu.make_async_remote_copy(
            src_ref=dst,
            dst_ref=dst,
            send_sem=ssem.at[0],
            recv_sem=rsem.at[recv_slot],
            device_id=sibling,
            device_id_type=MESH,
        ).wait_recv()

    def settle(keep=0, of=None):
        done = [p for p in pending if p[2] == of] if of else pending[: len(pending) - keep]
        for item in done:
            if item[3] is None:
                item[0].wait_send()
            else:
                pl.when(item[3])(item[0].wait_send)
            free.append(item[1])
        left = [p for p in pending if all(p is not q for q in done)]
        pending[:] = left

    rcount = [0]

    def rslots(n):
        rcount[0] += n
        return rcount[0] - n

    def row_block(index):
        return pl.ds(pl.multiple_of(index * own, own), own)

    nh = s.nh
    cut = own // nh

    def row_part(index, q):
        return pl.ds(pl.multiple_of(index * own + q * cut, cut), cut)

    def part(q):
        return pl.ds(q * cut, cut)

    valid_col = (lax.broadcasted_iota(jnp.int32, (own, width), 0) < cnt_ref[0]).astype(FULL)
    valid_low = valid_col.astype(LOW)
    valid_row = (lax.broadcasted_iota(jnp.int32, (1, own), 1) < cnt_ref[0]).astype(FULL)
    counted = mask_ref[...].astype(FULL) * valid_row

    prologue = jax.named_scope("prologue")
    prologue.__enter__()
    pad = s.feat_up - up(s.feat, 16) + 16
    own_xt = xt_all.at[c]
    own_xt[s.feat_up - pad :, :] = jnp.zeros((pad, own), LOW)
    w1b[s.feat_up - pad :, :] = jnp.zeros((pad, width), LOW)
    x_valid = (lax.broadcasted_iota(jnp.int32, (s.feat, own), 1) < cnt_ref[0]).astype(LOW)
    own_xt[: s.feat, :] = xt_ref[...] * x_valid
    w1b[: s.feat, :] = w1_ref[...].astype(LOW)
    y1 = lax.dot_general(
        own_xt[...], w1b[...], (((0,), (0,)), ((), ())), preferred_element_type=FULL
    ).astype(LOW)

    wide = [rslots(s.n_row * nh) for _ in range(2)]
    gbase = [rslots(s.n_col * nh) for _ in range(2)]
    prologue.__exit__(None, None, None)

    def start_gather(hop, q, values):
        mine = v_all.at[hop, row_part(c, q)]
        mine[...] = values
        for d in range(1, ny):
            send(mine, mine, gbase[hop] + c * nh + q, at(z, x, ys(d), k))
        if nk > 1:
            send(mine, mine, gbase[hop] + c * nh + q, sibling)

    def complete_gather(hop):
        for q in range(nh):
            for d in range(1, ny):
                source = ys(ny - d) * nk + k
                block = v_all.at[hop, row_part(source, q)]
                arrived(block, gbase[hop] + source * nh + q)
                if nk > 1:
                    send(block, block, gbase[hop] + source * nh + q, sibling)
        if nk > 1:
            for q in range(nh):
                for d in range(ny):
                    source = ys(d) * nk + 1 - k
                    arrived(
                        v_all.at[hop, row_part(source, q)], gbase[hop] + source * nh + q
                    )

    with jax.named_scope("barrier"):
        pl.semaphore_wait(barrier, len(peers))
    for q in range(nh):
        start_gather(0, q, y1[q * cut : (q + 1) * cut])

    if relayed:

        @pl.when(outer)
        def _():
            zrecv[:, 2] = jnp.zeros((2, own, width), LOW)

    w3t[...] = jnp.zeros_like(w3t)
    w3t[: s.classes, :] = w3t_ref[...].astype(LOW)
    w2 = w2_ref[...].astype(LOW)
    for a in range(n_sub):
        loads[a].wait()
        for b in range(cols // own):
            piece = tile[pl.ds(a * SUB, SUB), pl.ds(b * own, own)]
            cover = jnp.full((SUB, own), occ_ref[a, b].astype(FULL), FULL).astype(LOW)
            tile[pl.ds(a * SUB, SUB), pl.ds(b * own, own)] = piece * cover

    def spread(hop, finish):
        settle(of="hop")
        with jax.named_scope("gather_y"):
            complete_gather(hop)
        zbase = wide[hop]
        xbase = zbase + nz * nh
        order = list(range(nz - 1, -1, -1))

        def send_x(dz, dx, q):
            place = (dx - 1) * nz + dz
            send(
                xsend.at[place, part(q)],
                pool.at[hop * s.n_row + place, part(q)],
                xbase + place * nh + q,
                at(z, xs(dx), y, k),
                "hop",
            )

        sequence = []
        if relayed:
            for q in range(nh):
                sequence.append((3, q))
                if q:
                    sequence.append((2, q - 1))
            sequence += [(dz, q) for dz, q in ((2, nh - 1),)]
            sequence += [(dz, q) for dz in (1, 0) for q in range(nh)]
        else:
            for q in range(nh):
                sequence += [(dz, q) for dz in order if dz]
                if q:
                    sequence.append((0, q - 1))
            sequence.append((0, nh - 1))
        ready = set()
        with jax.named_scope("send_x"):
            for dz, q in sequence:
                for dx in range(1, nx):
                    if (dz, dx) not in ready:
                        ready.add((dz, dx))
                        rt = zs(dz) * nx + xs(dx)
                        xsend[(dx - 1) * nz + dz] = dot(
                            tile[row_block(rt), :], v_all[hop]
                        ).astype(LOW)
                    send_x(dz, dx, q)
            for dz in order:
                acc[:, dz * own : (dz + 1) * own] = dot(
                    tile[row_block(zs(dz) * nx + x), :], v_all[hop]
                )

        def send_z(dz, q):
            rows_q = slice(q * cut, (q + 1) * cut)
            total = acc[rows_q, dz * own : (dz + 1) * own]
            for dx in range(1, nx):
                place = (dx - 1) * nz + dz
                arrived(pool.at[hop * s.n_row + place, part(q)], xbase + place * nh + q)
                total = total + pool[hop * s.n_row + place, rows_q, :].astype(FULL)
            if not dz:
                return total
            there, slot, mark = zs(dz), dz - 1, zbase + dz * nh + q
            if relayed and dz == 3:
                there = is_inner * zs(3) + (1 - is_inner) * zs(1)
                slot, mark = 3 - is_inner, zbase + 3 * nh * is_inner + q
            if relayed and dz == 2:

                @pl.when(inner)
                def _():
                    arrived(zrecv.at[hop, 3, part(q)], zbase + q)
                    handed = zrecv[hop, 3, rows_q, :].astype(FULL)
                    zsend[dz - 1, rows_q, :] = (total + handed).astype(LOW)

                @pl.when(outer)
                def _():
                    zsend[dz - 1, rows_q, :] = total.astype(LOW)

            else:
                zsend[dz - 1, rows_q, :] = total.astype(LOW)
            send(
                zsend.at[dz - 1, part(q)],
                zrecv.at[hop, slot, part(q)],
                mark,
                at(there, x, y, k),
                "hop",
            )
            return total

        totals = [None] * nh

        def sum_z(q):
            total = totals[q]
            rows_q = slice(q * cut, (q + 1) * cut)
            for dz in range(1, nz):
                there, mark = zrecv.at[hop, dz - 1, part(q)], zbase + dz * nh + q
                if relayed and dz == 3:
                    pl.when(inner)(functools.partial(arrived, there, mark))
                else:
                    arrived(there, mark)
                total = total + zrecv[hop, dz - 1, rows_q, :].astype(FULL)
            finish(q, total)

        with jax.named_scope("send_z"):
            for dz, q in sequence[:-1]:
                totals[q] = send_z(dz, q)
                if not dz:
                    with jax.named_scope("sum_z0"):
                        sum_z(q)
        with jax.named_scope("sum_z1"):
            totals[nh - 1] = send_z(0, nh - 1)
            sum_z(nh - 1)

    bias = [bias_ref[i * width : (i + 1) * width].reshape(1, width) for i in range(2)]
    slopes, acts = [None] * nh, [None] * nh

    def first_done(q, total):
        rows_q = slice(q * cut, (q + 1) * cut)
        z1 = total + v_all[0, row_part(c, q), :].astype(FULL) + bias[0]
        act, slope = gelu_both(z1)
        h1 = act.astype(LOW) * valid_low[rows_q]
        start_gather(1, q, dot(h1, w2).astype(LOW))
        acts[q], slopes[q] = h1, slope * valid_col[rows_q]

    spread(0, first_done)
    h1t = jnp.concatenate(acts, axis=0).astype(FULL).T.astype(LOW)
    slope1t = jnp.concatenate(slopes, axis=0).T

    xt_base = gbase[1] + s.n_col

    def second_done(q, total):
        rows_q = slice(q * cut, (q + 1) * cut)
        z2 = total + v_all[1, row_part(c, q), :].astype(FULL) + bias[1]
        act, slope = gelu_both(z2)
        acts[q] = act.astype(LOW) * valid_low[rows_q]
        slopes[q] = slope * valid_col[rows_q]

    spread(1, second_done)
    h2 = jnp.concatenate(acts, axis=0)
    y3t = dot_nt(w3t[...], h2).astype(LOW)

    with jax.named_scope("hop3_gather"):
        base = gbase[0]
        mine = v3_all.at[c]
        mine[...] = y3t
        for dy, dk in col_far:
            send(mine, mine, base + c, (r, ys(dy) * nk + ks(dk)))
        slope2t = jnp.concatenate(slopes, axis=0).T
        settle(s.n_col - 1)
        for dy, dk in reversed(col_far):
            source = ys(ny - dy) * nk + ks(nk - dk)
            arrived(v3_all.at[source], base + source)
    with jax.named_scope("hop3_sum"):
        pbase = wide[0]
        v3 = jnp.concatenate([v3_all[i] for i in range(s.n_col)], axis=1)
        for dz, dx in row_far:
            place = dz * nx + dx
            rt = zs(dz) * nx + xs(dx)
            p3send[place] = dot_nt(v3, tile[row_block(rt), :]).astype(LOW)
            send(p3send.at[place], p3recv.at[place], pbase + place, (rt, c))
        total = dot_nt(v3, tile[row_block(r), :])
        for dz, dx in reversed(row_far):
            place = dz * nx + dx
            arrived(p3recv.at[place], pbase + place)
            total = total + p3recv[place].astype(FULL)
    total = total + y3t.astype(FULL)

    place = lax.broadcasted_iota(jnp.int32, (s.cls, own), 0)
    real = place < s.classes
    on_diag = lax.broadcasted_iota(jnp.int32, (s.cls, s.classes), 0) == lax.broadcasted_iota(
        jnp.int32, (s.cls, s.classes), 1
    )
    bias3 = jnp.sum(
        jnp.where(on_diag, bias_ref[2 * width :].reshape(1, s.classes), 0.0), axis=1, keepdims=True
    )
    logits = jnp.where(real, total + bias3, -1e30)
    shifted = logits - jnp.max(logits, axis=0, keepdims=True)
    weight = jnp.where(real, jnp.exp(shifted), 0.0)
    norm = jnp.sum(weight, axis=0, keepdims=True)
    logp = shifted - jnp.log(norm)
    target = jnp.where(place == lab_ref[...], 1.0 - SMOOTH, 0.0) + SMOOTH / s.classes
    target = jnp.where(real, target, 0.0)
    row_loss = -jnp.sum(jnp.where(real, target * logp, 0.0), axis=0, keepdims=True)
    loss = jnp.sum(row_loss * counted, axis=1, keepdims=True)
    number = jnp.sum(counted, axis=1, keepdims=True)
    dlt = ((weight / norm - target) * counted).astype(LOW)

    with jax.named_scope("back3_gather"):
        base = wide[1]
        mine = dl_all.at[r]
        mine[...] = dlt
        for dz, dx in row_far:
            send(mine, mine, base + r, (zs(dz) * nx + xs(dx), c))
        here = dot(dlt, tile[row_block(r), :])
        for dz, dx in reversed(row_far):
            source = zback(dz) * nx + xs(nx - dx)
            arrived(dl_all.at[source], base + source)
            here = here + dot(dl_all[source], tile[row_block(source), :])
        acc[: s.cls, :cols] = here
    with jax.named_scope("back3_sum"):
        qbase = gbase[1]
        for dy, dk in col_far:
            place = dy * nk + dk
            ct = ys(dy) * nk + ks(dk)
            q3send[place] = acc[: s.cls, row_block(ct)].astype(LOW)
            send(q3send.at[place], q3recv.at[place], qbase + place, (r, ct))
        total = dlt.astype(FULL) + acc[: s.cls, row_block(c)]
        for dy, dk in reversed(col_far):
            place = dy * nk + dk
            arrived(q3recv.at[place], qbase + place)
            total = total + q3recv[place].astype(FULL)
    qt = total.astype(LOW)
    dh2t = lax.dot_general(
        w3t[...], qt, (((0,), (0,)), ((), ())), preferred_element_type=FULL
    )
    step_cols = min(cols, 1024)

    def gained(values, block, fresh=False):
        for j in range(0, cols, step_cols):
            here = dot(values, tile[block, j : j + step_cols])
            if fresh:
                acc[:, j : j + step_cols] = here
            else:
                acc[:, j : j + step_cols] += here

    def halves(lane, row):
        return (
            pl.ds(row * (width // 2), width // 2),
            pl.ds(lane * (own // 2), own // 2),
        )

    quarters = [(lane, row) for lane in range(2) for row in range(2)]
    def receive(hop, values, meanwhile=None, late=None):
        base = wide[hop]
        first = hop * s.n_row

        def piece(dz, dx, q):
            return pool.at[(first + dx * nz + dz, *halves(*quarters[q]))]

        def to_z(dz, q, when=None, start=True):
            return send(
                piece(0, 0, q),
                piece(dz, 0, q),
                base + dz * nh + q,
                at(zs(dz), x, y, k),
                when=when,
                start=start,
            )

        def to_x(dz, q, start=True):
            return [
                send(
                    piece(dz, 0, q),
                    piece(dz, dx, q),
                    base + (dx * nz + dz) * nh + q,
                    at(z, xs(dx), y, k),
                    start=start,
                )
                for dx in range(1, nx)
            ]

        own_parts = []
        for lane in range(2):
            mine = values(lane)
            own_parts.append(mine)
            pool[first, :, lane * (own // 2) : (lane + 1) * (own // 2)] = mine
            for q in (2 * lane, 2 * lane + 1):
                if relayed:
                    to_z(2, q)
                    to_z(1, q)
                else:
                    for dz in range(nz - 1, 0, -1):
                        to_z(dz, q)
                to_x(0, q)

        def source(dz, dx):
            return row_block(zback(dz) * nx + xs(nx - dx))

        gained(jnp.concatenate(own_parts, axis=1), row_block(r), fresh=True)
        if meanwhile is not None:
            meanwhile()

        passing = {
            (dz, q): to_x(dz, q, start=False) for q in range(nh) for dz in range(1, nz)
        }

        def step(dz, q):
            arrived(piece(dz, 0, q), base + dz * nh + q)
            for copy in passing[dz, q]:
                copy.start()

        if relayed:
            relays = [
                send(
                    piece(2, 0, q),
                    piece(3, 0, q),
                    base + 3 * nh + q,
                    at(zs(1), x, y, k),
                    when=inner,
                    start=False,
                )
                for q in range(nh)
            ]
            paced = [to_z(3, q, inner, start=False) for q in range(nh)]

            @pl.when(inner)
            def _():
                for q in range(nh):
                    arrived(piece(2, 0, q), base + 2 * nh + q)
                    relays[q].start()
                    paced[q].start()
                    for copy in passing[2, q]:
                        copy.start()
                    step(1, q)
                    if q > 1:
                        step(3, q - 2)
                for q in range(nh - 2, nh):
                    step(3, q)

            @pl.when(outer)
            def _():
                for q in range(nh + 2):
                    if q < nh:
                        step(1, q)
                    if 0 < q <= nh:
                        step(2, q - 1)
                    if q > 2:
                        step(3, q - 3)
                for q in range(nh - 1, nh):
                    step(3, q)
        else:
            for q in range(nh):
                for dz in range(1, nz):
                    step(dz, q)
        for dz in range(1, nz):
            gained(pool[first + dz], source(dz, 0))
        if late is not None:
            late()
        for dz in range(nz):
            for dx in range(1, nx):
                for q in range(nh):
                    arrived(piece(dz, dx, q), base + (dx * nz + dz) * nh + q)
                gained(pool[first + dx * nz + dz], source(dz, dx))

    dz2t = (dh2t * slope2t).astype(LOW)
    half_own = own // 2

    def features_out():
        for d in range(1, ny):
            send(own_xt, own_xt, xt_base + c, at(z, x, ys(d), k))
        if nk > 1:
            send(own_xt, own_xt, xt_base + c, sibling)

    with jax.named_scope("back2_rows"):
        settle()
        receive(0, lambda lane: dz2t[:, lane * half_own : (lane + 1) * half_own], features_out)
    cbase = gbase[0] + s.n_col
    ybase = gbase[1] + 2 * s.n_col

    def lane_part(index, lane):
        return pl.ds(pl.multiple_of(index * own + lane * half_own, half_own), half_own)

    def held(place, lane):
        return xsend.at[place, :, pl.ds(lane * half_own, half_own)]

    def crecv(dy, lane):
        return v_all.at[0, dy * own : (dy + 1) * own, pl.ds(lane * half_own, half_own)]

    def yrecv(dy, lane):
        return crecv(dy + (ny if nk > 1 else 0), lane)

    column_totals = [None, None]
    with jax.named_scope("back2_cols"):
        for lane in range(2):
            for dy in range(ny - 1, -1, -1):
                if nk > 1:
                    there = held(dy, lane)
                    there[...] = acc[:, lane_part(ys(dy) * nk + 1 - k, lane)].astype(LOW)
                    send(there, crecv(dy, lane), cbase + 2 * dy + lane, sibling)
        for lane in range(2):
            for dy in range(ny - 1, -1, -1):
                here = acc[:, lane_part(ys(dy) * nk + k, lane)]
                if nk > 1:
                    arrived(crecv(dy, lane), cbase + 2 * dy + lane)
                    here = here + crecv(dy, lane)[...].astype(FULL)
                if dy:
                    there = held(ny + dy, lane)
                    there[...] = here.astype(LOW)
                    send(
                        there, yrecv(dy, lane), ybase + 2 * dy + lane, at(z, x, ys(dy), k)
                    )
                else:
                    column_totals[lane] = here
        for d in range(1, ny):
            source = ys(ny - d) * nk + k
            arrived(xt_all.at[source], xt_base + source)
            if nk > 1:
                send(xt_all.at[source], xt_all.at[source], xt_base + source, sibling)

    dy2_parts, dz1_parts = [], []

    def first_slopes(lane):
        lanes_q = slice(lane * half_own, (lane + 1) * half_own)
        total = column_totals[lane] + dz2t[:, lanes_q].astype(FULL)
        with jax.named_scope("y_wait"):
            for dy in range(1, ny):
                arrived(yrecv(dy, lane), ybase + 2 * dy + lane)
                total = total + yrecv(dy, lane)[...].astype(FULL)
        dy2_parts.append(total.astype(LOW))
        dz1_parts.append((dot(w2, dy2_parts[lane]) * slope1t[:, lanes_q]).astype(LOW))
        return dz1_parts[lane]

    lanes, plane = s.lanes, s.plane
    me = y * nx + x
    others = [(dx, dy) for dx in range(nx) for dy in range(ny) if dx or dy]

    def lane_block(index):
        return pl.ds(pl.multiple_of(index * lanes, lanes), lanes)

    class Total:
        def __init__(self, start, rows):
            self.all = pl.ds(start, rows)
            self.start, self.rows = start, rows
            self.n = rows // plane
            self.short = pl.ds(start // plane, self.n)
            self.base = rslots(1 + 3 * plane + nz)

        def piece(self, index):
            return pl.ds(pl.multiple_of(self.start + index * self.n, 16), self.n)

        def core_send(self, other):
            if nk > 1:
                half_send[self.all, :] = other.astype(LOW)
                send(half_send.at[self.all], half_recv.at[self.all], self.base, sibling)

        def plane_send(self, mine):
            if nk > 1:
                arrived(half_recv.at[self.all], self.base)
                mine = mine + half_recv[self.all, :].astype(FULL)
            half[self.all, :] = mine.astype(LOW)
            base = self.base + 1
            for dx, dy in others:
                there = ys(dy) * nx + xs(dx)
                send(
                    half.at[self.piece(there)],
                    plane_recv.at[me, self.short],
                    base + me,
                    at(z, xs(dx), ys(dy), k),
                )
            plane_recv[me, self.short, :] = half[self.piece(me), :]

        def line_send(self):
            base = self.base + 1
            for dx, dy in others:
                there = ys(dy) * nx + xs(dx)
                arrived(plane_recv.at[there, self.short], base + there)
            total = plane_recv[0, self.short, :].astype(FULL)
            for i in range(1, plane):
                total = total + plane_recv[i, self.short, :].astype(FULL)
            quarter[z, self.short, :] = total.astype(LOW)
            mine = quarter.at[z, self.short]
            base = self.base + 1 + plane
            for dz in range(nz - 1, 0, -1):
                send(mine, mine, base + z, at(zs(dz), x, y, k))

        def back_send(self):
            base = self.base + 1 + plane
            for dz in range(1, nz):
                arrived(quarter.at[zback(dz), self.short], base + zback(dz))
            total = quarter[0, self.short, :].astype(FULL)
            for i in range(1, nz):
                total = total + quarter[i, self.short, :].astype(FULL)
            base = self.base + 1 + plane + nz
            mine = fin.at[k, self.piece(me)]
            mine[...] = total.astype(LOW)
            for dx, dy in others:
                send(mine, mine, base + me, at(z, xs(dx), ys(dy), k))
            if nk > 1:
                send(mine, mine, base + plane + me, sibling)

        def back_forward(self):
            base = self.base + 1 + plane + nz
            for dx, dy in others:
                there = ys(dy) * nx + xs(dx)
                block = fin.at[k, self.piece(there)]
                arrived(block, base + there)
                if nk > 1:
                    send(block, block, base + plane + there, sibling)

        def end(self):
            base = self.base + 1 + plane + nz
            if nk > 1:
                for i in range(plane):
                    arrived(fin.at[1 - k, self.piece(i)], base + plane + i)

    written = []

    def write(start, count):
        rows_w = pl.ds(start, count)
        copy = pltpu.make_async_copy(
            fin.at[:, rows_w], grad_ref.at[:, rows_w], lsem.at[n_sub + len(written)]
        )
        copy.start()
        written.append(copy)

    one_a = Total(0, s.cut_rows)
    one_b = Total(s.cut_rows, s.one_rows - s.cut_rows)
    two = Total(s.one_rows, s.two_rows)
    tail = s.two_rows - width - s.cls

    def early():
        grad3t = dot(qt, h2)
        dy2t = jnp.concatenate(dy2_parts, axis=1)
        grad2 = dot_nt(h1t, dy2t)
        acc_two = jnp.concatenate(
            [grad2, grad3t] + ([jnp.zeros((tail, width), FULL)] if tail else []), axis=0
        )
        if nk > 1:
            first, second = acc_two[:, :lanes], acc_two[:, lanes:]
            low_core = (k == 0).astype(FULL)
            two.core_send(second * low_core + first * (1.0 - low_core))
            two.plane_send(first * low_core + second * (1.0 - low_core))
        else:
            two.plane_send(acc_two)

    with jax.named_scope("back1_rows"):
        receive(1, first_slopes, early, two.line_send)
    with jax.named_scope("grad1"):
        dz1t = jnp.concatenate(dz1_parts, axis=1)
        acc[:, row_block(c)] += dz1t.astype(FULL)
        if nk > 1:
            for d in range(ny):
                source = ys(d) * nk + 1 - k
                arrived(xt_all.at[source], xt_base + source)

        def grad_one(index, start, stop):
            total = None
            end = min(stop, s.feat_up)
            for i in range(s.n_col):
                here = acc[pl.ds(pl.multiple_of(index * lanes, lanes), lanes), :]
                here = dot_nt(
                    xt_all[i, start:end, :], here[:, i * own : (i + 1) * own].astype(LOW)
                )
                total = here if total is None else total + here
            if end < stop:
                total = jnp.concatenate([total, jnp.zeros((stop - end, lanes), FULL)], axis=0)
            return total

        if nk > 1:
            one_a.core_send(grad_one(1 - k, 0, s.cut_rows))
            one_b.core_send(grad_one(1 - k, s.cut_rows, s.one_rows))
        one_a.plane_send(grad_one(k, 0, s.cut_rows))
        one_b.plane_send(grad_one(k, s.cut_rows, s.one_rows))
        ones = jnp.ones((8, own), LOW)
        row = lax.broadcasted_iota(jnp.int32, (8, width), 0)
        lane = lax.broadcasted_iota(jnp.int32, (8, width), 1)
        bias_three = jnp.concatenate([dlt, jnp.zeros((width - s.cls, own), LOW)], axis=0)
        misc = jnp.where(row == 0, dot_nt(ones, dz1t), 0.0)
        misc = jnp.where(row == 1, dot_nt(ones, dz2t), misc)
        misc = jnp.where(row == 2, dot_nt(ones, bias_three), misc)
        misc = jnp.where((row == 3) & (lane == 0), loss, misc)
        misc = jnp.where((row == 3) & (lane == 1), number, misc)
        mbase = rslots(1 + plane + nz)
        misc_k[0] = misc
        if nk > 1:
            send(misc_k.at[0], misc_k.at[1], mbase, sibling)

    with jax.named_scope("sum_plane"):
        if nk > 1:
            arrived(misc_k.at[1], mbase)
            misc = misc_k[0] + misc_k[1]
        misc_p[me] = misc
        mbase = mbase + 1
        for dx, dy in others:
            send(misc_p.at[me], misc_p.at[me], mbase + me, at(z, xs(dx), ys(dy), k))
        left = len(pending)
        two.back_send()
    with jax.named_scope("sum_line"):
        one_a.line_send()
        one_b.line_send()
        for dx, dy in others:
            there = ys(dy) * nx + xs(dx)
            arrived(misc_p.at[there], mbase + there)
        misc = misc_p[0]
        for i in range(1, plane):
            misc = misc + misc_p[i]
        mbase = mbase + plane
        misc_z[z] = misc
        for dz in range(1, nz):
            send(misc_z.at[z], misc_z.at[z], mbase + z, at(zs(dz), x, y, k))
        two.back_forward()
        two.end()
        settle(len(pending) - left)
    with jax.named_scope("back_line"):
        one_a.back_send()
        one_b.back_send()
        for dz in range(1, nz):
            arrived(misc_z.at[zback(dz)], mbase + zback(dz))
        misc = misc_z[0]
        for i in range(1, nz):
            misc = misc + misc_z[i]
        misc_k[0] = jnp.where(row == 4, 1.0 / misc[3:4, 1:2], misc)
        written.append(
            pltpu.make_async_copy(misc_k.at[0], misc_ref.at[pl.ds(0, 8)], lsem.at[n_sub])
        )
        written[0].start()
        write(s.one_rows, s.two_rows)
    with jax.named_scope("back_plane"):
        one_a.back_forward()
        one_b.back_forward()
        one_a.end()
        write(0, s.cut_rows)
        one_b.end()
        write(s.cut_rows, s.one_rows - s.cut_rows)
    with jax.named_scope("settle"):
        settle()
        for copy in written:
            copy.wait()
    assert rcount[0] <= s.arrivals


def update_pieces(s):
    middle = up(s.feat // 2, 8)
    return (
        (0, 0, middle),
        (0, middle, s.feat - middle),
        (1, 0, s.width),
        (2, 0, s.classes),
    )


def adam_kernel(s, grad_hbm, misc_hbm, *refs):
    ins, outs, scratch = refs[:12], refs[12:26], refs[26:]
    grad_ref, misc_ref, bias_in, bias_out, ends, *held = scratch[:-2]
    sem_in, sem_out = scratch[-2:]
    pieces = update_pieces(s)
    width, classes, lanes = s.width, s.classes, s.lanes
    grad_at = (0, s.one_rows, s.one_rows + width)

    misc_load = pltpu.make_async_copy(misc_hbm.at[pl.ds(0, 8)], misc_ref, sem_in.at[0])
    grad_load = pltpu.make_async_copy(
        grad_hbm.at[:, pl.ds(0, s.grad_rows)], grad_ref, sem_in.at[1]
    )
    misc_load.start()
    grad_load.start()
    loads, count = [], 2
    for n, (which, start, rows) in enumerate(pieces):
        mine = []
        for i in range(3):
            mine.append(
                pltpu.make_async_copy(
                    ins[3 * which + i].at[pl.ds(start, rows)], held[2 * n].at[i], sem_in.at[count]
                )
            )
            count += 1
            mine[-1].start()
        loads.append(mine)
    bias_loads = []
    for i in range(3):
        bias_loads.append(
            pltpu.make_async_copy(ins[9 + i], bias_in[i], sem_in.at[count])
        )
        count += 1
        bias_loads[-1].start()

    misc_load.wait()
    grad_load.wait()
    total = misc_ref[3:4, 1:2]
    scale = misc_ref[4:5, 0:1]
    stores, count = [], 2
    ends[0] = misc_ref[3:4, 0:1]
    ends[1] = total
    for i in range(2):
        stores.append(pltpu.make_async_copy(ends.at[i], outs[12 + i], sem_out.at[i]))
        stores[-1].start()
    for n, (which, start, rows) in enumerate(pieces):
        for load in loads[n]:
            load.wait()
        source, target = held[2 * n], held[2 * n + 1]
        for i in range(s.nk):
            lane = slice(i * lanes, (i + 1) * lanes)
            first = grad_at[which] + start
            grad = grad_ref[i, first : first + up(rows, 16), :].astype(FULL)[:rows]
            weight, one, two = (source[j, :, lane] for j in range(3))
            for j, new in enumerate(adam_update(weight, one, two, grad * scale)):
                target[j, :, lane] = new
        for j in range(3):
            stores.append(
                pltpu.make_async_copy(
                    target.at[j], outs[3 * which + j].at[pl.ds(start, rows)], sem_out.at[count]
                )
            )
            count += 1
            stores[-1].start()
    for load in bias_loads:
        load.wait()
    for i, size in enumerate((width, width, classes)):
        span = slice(i * width, i * width + size)
        weight, first, second = (bias_in[j][span] for j in range(3))
        new = adam_update(weight, first, second, misc_ref[i, :size] * misc_ref[4, :size])
        for j in range(3):
            bias_out[j][span] = new[j]
    for j in range(3):
        stores.append(
            pltpu.make_async_copy(bias_out[j], outs[9 + j], sem_out.at[count])
        )
        count += 1
        stores[-1].start()
    for store in stores:
        store.wait()


def shards(
    sizes,
    features,
    adjacency,
    occupancy,
    labels,
    train_mask,
    node_count,
    weight_one,
    weight_two,
    weight_three,
    biases,
    first_one,
    first_two,
    first_three,
    first_bias,
    second_one,
    second_two,
    second_three,
    second_bias,
):
    own, feat = features.shape
    width = weight_two.shape[0]
    classes = weight_three.shape[1]
    s = sizes(own, feat, width, classes)
    rows, cols = adjacency.shape
    lanes = s.lanes
    vmem = pl.BlockSpec(memory_space=pltpu.VMEM)
    smem = pl.BlockSpec(memory_space=pltpu.SMEM)
    anywhere = pl.BlockSpec(memory_space=pl.ANY)
    block = (own, width)
    small = (s.cls, own)
    shapes = [
        ((rows, cols), LOW),
        ((s.feat_up, width), LOW),
        ((s.cls, width), LOW),
        ((s.n_col, s.feat_up, own), LOW),
        ((2, s.n_col * own, width), LOW),
        ((2 * s.n_row, *block), LOW),
        ((max(2 * s.ny, s.n_row - s.nz), *block), LOW),
        ((max(1, s.nz - 1), *block), LOW),
        ((2, s.nz if s.relayed else max(1, s.nz - 1), *block), LOW),
        ((s.n_col, *small), LOW),
        ((s.n_row, *small), LOW),
        ((s.n_row, *small), LOW),
        ((s.n_row, *small), LOW),
        ((s.n_col, *small), LOW),
        ((s.n_col, *small), LOW),
        ((width, max(cols, s.nz * own)), FULL),
        ((s.grad_rows, lanes), LOW),
        ((s.grad_rows, lanes), LOW),
        ((s.grad_rows, lanes), LOW),
        ((s.plane, s.grad_rows // s.plane, lanes), LOW),
        ((s.nz, s.grad_rows // s.plane, lanes), LOW),
        ((s.nk, s.grad_rows, lanes), LOW),
        ((2, 8, width), FULL),
        ((s.plane, 8, width), FULL),
        ((s.nz, 8, width), FULL),
    ]
    bytes_held = sum(math.prod(shape) * jnp.dtype(kind).itemsize for shape, kind in shapes)
    limit = 62 * 2**20
    grads, misc = pl.pallas_call(
        functools.partial(kernel, s),
        out_shape=(
            jax.ShapeDtypeStruct((s.nk, s.grad_rows, lanes), LOW),
            jax.ShapeDtypeStruct((8, width), FULL),
        ),
        in_specs=[
            vmem,
            anywhere,
            smem,
            vmem,
            vmem,
            smem,
            vmem,
            vmem,
            vmem,
            vmem,
        ],
        out_specs=(anywhere, anywhere),
        scratch_shapes=[
            *[pltpu.VMEM(shape, kind) for shape, kind in shapes],
            pltpu.SemaphoreType.DMA((s.sends,)),
            pltpu.SemaphoreType.DMA((s.arrivals,)),
            pltpu.SemaphoreType.DMA((rows // SUB + 4,)),
        ],
        compiler_params=pltpu.CompilerParams(
            collective_id=0, has_side_effects=True, vmem_limit_bytes=limit
        ),
        cost_estimate=pl.CostEstimate(
            flops=12 * rows * cols * width, bytes_accessed=2 * rows * cols, transcendentals=0
        ),
        name="step",
    )(
        features.T,
        adjacency,
        occupancy,
        labels.reshape(1, own),
        train_mask.reshape(1, own),
        node_count,
        weight_one,
        weight_two,
        weight_three.T,
        biases,
    )
    state = (
        weight_one,
        first_one,
        second_one,
        weight_two,
        first_two,
        second_two,
        weight_three.T,
        first_three.T,
        second_three.T,
        biases,
        first_bias,
        second_bias,
    )
    new = pl.pallas_call(
        functools.partial(adam_kernel, s),
        out_shape=(
            *[jax.ShapeDtypeStruct(a.shape, FULL) for a in state],
            jax.ShapeDtypeStruct((1, 1), FULL),
            jax.ShapeDtypeStruct((1, 1), FULL),
        ),
        in_specs=[anywhere] * 14,
        out_specs=(anywhere,) * 14,
        scratch_shapes=[
            pltpu.VMEM((s.nk, s.grad_rows, lanes), LOW),
            pltpu.VMEM((8, width), FULL),
            [pltpu.VMEM(biases.shape, FULL)] * 3,
            [pltpu.VMEM(biases.shape, FULL)] * 3,
            pltpu.VMEM((2, 1, 1), FULL),
            *[
                pltpu.VMEM((3, rows, width), FULL)
                for _, _, rows in update_pieces(s)
                for _ in range(2)
            ],
            pltpu.SemaphoreType.DMA((17,)),
            pltpu.SemaphoreType.DMA((17,)),
        ],
        compiler_params=pltpu.CompilerParams(vmem_limit_bytes=62 * 2**20),
        name="update",
    )(grads, misc, *state)
    return (
        *new[:6],
        *[a.T for a in new[6:9]],
        *new[9:12],
        new[12].reshape(()),
        new[13].reshape(()),
    )


def solution(mesh):
    placed = (
        P(("row", "col"), None),
        P("col", "row"),
        P("col", "row"),
        P(("row", "col")),
        P(("row", "col")),
        P(("row", "col")),
        *[P()] * 12,
    )
    sizes = functools.partial(Sizes, mesh.shape["row"], mesh.shape["col"])
    return jax.shard_map(
        functools.partial(shards, sizes),
        mesh=mesh,
        in_specs=placed,
        out_specs=(P(),) * 14,
        check_vma=False,
    )
```

```python
import functools
import math

import jax
import jax.numpy as jnp
from jax import lax
from jax.experimental import pallas as pl
from jax.experimental.pallas import tpu as pltpu
from jax.sharding import PartitionSpec as P

SUB = 512
STEP = 5


B_ONE = 0.5
B_TWO = 0.5
RATE = 0.05
DECAY = 0.01
EPSILON = 1e-08
SMOOTH = 0.1

MESH = pl.DeviceIdType.MESH
LOW = jnp.bfloat16
FULL = jnp.float32
GELU_A = 0.7978845608028654
GELU_B = 0.044715


def adam_update(weight, first, second, grad):
    first_new = B_ONE * first + (1.0 - B_ONE) * grad
    second_new = B_TWO * second + (1.0 - B_TWO) * grad * grad
    fix_one = 1.0 - B_ONE**STEP
    fix_two = 1.0 - B_TWO**STEP
    scaled = (first_new * (1.0 / fix_one)) / (jnp.sqrt(second_new * (1.0 / fix_two)) + EPSILON)
    return (first_new, second_new, weight - RATE * (scaled + DECAY * weight))


def up(value, unit):
    return -(-value // unit) * unit


def dot(left, right):
    return jnp.dot(left, right, preferred_element_type=FULL)


def dot_nt(left, right):
    return lax.dot_general(left, right, (((1,), (1,)), ((), ())), preferred_element_type=FULL)


def gelu_both(z):
    t = jnp.tanh(GELU_A * (z + GELU_B * z * z * z))
    half = 0.5 * (1.0 + t)
    slope = half + 0.5 * z * (1.0 - t * t) * (GELU_A * (1.0 + 3.0 * GELU_B * z * z))
    return z * half, slope


class Sizes:
    def __init__(self, n_row, n_col, own, feat, width, classes):
        self.n_row, self.n_col = n_row, n_col
        self.nk = 2 if n_col % 2 == 0 else 1
        self.ny = n_col // self.nk
        self.nx = self.ny if n_row % self.ny == 0 else 1
        self.nz = n_row // self.nx
        self.own, self.feat, self.width, self.classes = own, feat, width, classes
        self.feat_up = up(feat, 128)
        self.cls = up(classes, 16)
        self.plane = self.nx * self.ny
        self.one_rows = up(feat, 16 * self.plane)
        self.two_rows = up(width + self.cls, 16 * self.plane)
        self.grad_rows = self.one_rows + self.two_rows
        self.lanes = width // self.nk
        units = self.one_rows // (16 * self.plane)
        self.cut_rows = (units + 1) // 2 * 16 * self.plane
        self.nh = 4
        self.relayed = self.nz == 4
        self.sends = 3 * (n_row + n_col) + 3 * self.plane
        wide = 2 * self.nh * (n_row + n_col)
        self.arrivals = wide + 3 * (1 + 3 * self.plane + self.nz) + 1 + self.plane + self.nz


def kernel(
    s,
    xt_ref,
    adj_ref,
    occ_ref,
    lab_ref,
    mask_ref,
    cnt_ref,
    w1_ref,
    w2_ref,
    w3t_ref,
    bias_ref,
    grad_ref,
    misc_ref,
    tile,
    w1b,
    w3t,
    xt_all,
    v_all,
    pool,
    xsend,
    zsend,
    zrecv,
    v3_all,
    p3send,
    p3recv,
    dl_all,
    q3send,
    q3recv,
    acc,
    half_send,
    half_recv,
    half,
    plane_recv,
    quarter,
    fin,
    misc_k,
    misc_p,
    misc_z,
    ssem,
    rsem,
    lsem,
):
    nx, ny, nz, nk = s.nx, s.ny, s.nz, s.nk
    own, width = s.own, s.width
    r, c = lax.axis_index("row"), lax.axis_index("col")
    z, x = r // nx, r % nx
    y, k = c // nk, c % nk

    def at(zz, xx, yy, kk):
        return (zz * nx + xx, yy * nk + kk)

    def xs(d):
        return lax.rem(x + d, nx)

    def ys(d):
        return lax.rem(y + d, ny)

    def zs(d):
        if nz & (nz - 1):
            return lax.rem(z + d, nz)
        there, bit = z, 1
        while bit < nz:
            if d & bit:
                there = there + bit - 2 * bit * lax.rem(there // bit, 2)
            bit *= 2
        return there

    def zback(d):
        return zs(d) if not nz & (nz - 1) else lax.rem(z + nz - d, nz)

    sibling = at(z, x, y, 1 - k)
    relayed = s.relayed
    is_inner = lax.rem((z + 1) // 2, 2)
    inner = is_inner == 1
    outer = is_inner == 0
    line = [dz for dz in range(nz - 1, -1, -1)]
    row_far = [(dz, dx) for dz in line for dx in range(nx - 1, -1, -1) if dz or dx]
    col_far = [(dy, dk) for dy in range(ny - 1, -1, -1) for dk in range(nk - 1, -1, -1) if dy or dk]

    def ks(d):
        return lax.rem(k + d, nk)


    rows, cols = tile.shape
    n_sub = rows // SUB
    loads = [
        pltpu.make_async_copy(
            adj_ref.at[pl.ds(a * SUB, SUB)], tile.at[pl.ds(a * SUB, SUB)], lsem.at[a]
        )
        for a in range(n_sub)
    ]
    for load in loads:
        load.start()

    peers = []
    for d in range(1, s.n_row):
        peers.append((lax.rem(r + d, s.n_row), c))
    for d in range(1, s.n_col):
        peers.append((r, lax.rem(c + d, s.n_col)))
    for dx in range(1, nx):
        for dy in range(1, ny):
            peers.append(at(z, xs(dx), ys(dy), k))
    barrier = pltpu.get_barrier_semaphore()
    for peer in peers:
        pl.semaphore_signal(barrier, inc=1, device_id=peer, device_id_type=MESH)

    free = list(range(s.sends))
    pending = []

    def send(src, dst, recv_slot, device, of=None, when=None, start=True):
        if not free:
            settle(len(pending) - 1)
        copy = pltpu.make_async_remote_copy(
            src_ref=src,
            dst_ref=dst,
            send_sem=ssem.at[free[0]],
            recv_sem=rsem.at[recv_slot],
            device_id=device,
            device_id_type=MESH,
        )
        if start:
            if when is None:
                copy.start()
            else:
                pl.when(when)(copy.start)
        pending.append((copy, free.pop(0), of, when))
        return copy

    def arrived(dst, recv_slot):
        pltpu.make_async_remote_copy(
            src_ref=dst,
            dst_ref=dst,
            send_sem=ssem.at[0],
            recv_sem=rsem.at[recv_slot],
            device_id=sibling,
            device_id_type=MESH,
        ).wait_recv()

    def settle(keep=0, of=None):
        done = [p for p in pending if p[2] == of] if of else pending[: len(pending) - keep]
        for item in done:
            if item[3] is None:
                item[0].wait_send()
            else:
                pl.when(item[3])(item[0].wait_send)
            free.append(item[1])
        left = [p for p in pending if all(p is not q for q in done)]
        pending[:] = left

    rcount = [0]

    def rslots(n):
        rcount[0] += n
        return rcount[0] - n

    def row_block(index):
        return pl.ds(pl.multiple_of(index * own, own), own)

    nh = s.nh
    cut = own // nh

    def row_part(index, q):
        return pl.ds(pl.multiple_of(index * own + q * cut, cut), cut)

    def part(q):
        return pl.ds(q * cut, cut)

    valid_col = (lax.broadcasted_iota(jnp.int32, (own, width), 0) < cnt_ref[0]).astype(FULL)
    valid_low = valid_col.astype(LOW)
    valid_row = (lax.broadcasted_iota(jnp.int32, (1, own), 1) < cnt_ref[0]).astype(FULL)
    counted = mask_ref[...].astype(FULL) * valid_row

    prologue = jax.named_scope("prologue")
    prologue.__enter__()
    pad = s.feat_up - up(s.feat, 16) + 16
    own_xt = xt_all.at[c]
    own_xt[s.feat_up - pad :, :] = jnp.zeros((pad, own), LOW)
    w1b[s.feat_up - pad :, :] = jnp.zeros((pad, width), LOW)
    x_valid = (lax.broadcasted_iota(jnp.int32, (s.feat, own), 1) < cnt_ref[0]).astype(LOW)
    own_xt[: s.feat, :] = xt_ref[...] * x_valid
    w1b[: s.feat, :] = w1_ref[...].astype(LOW)
    y1 = lax.dot_general(
        own_xt[...], w1b[...], (((0,), (0,)), ((), ())), preferred_element_type=FULL
    ).astype(LOW)

    wide = [rslots(s.n_row * nh) for _ in range(2)]
    gbase = [rslots(s.n_col * nh) for _ in range(2)]
    prologue.__exit__(None, None, None)

    def start_gather(hop, q, values):
        mine = v_all.at[hop, row_part(c, q)]
        mine[...] = values
        for d in range(1, ny):
            send(mine, mine, gbase[hop] + c * nh + q, at(z, x, ys(d), k))
        if nk > 1:
            send(mine, mine, gbase[hop] + c * nh + q, sibling)

    def complete_gather(hop):
        for q in range(nh):
            for d in range(1, ny):
                source = ys(ny - d) * nk + k
                block = v_all.at[hop, row_part(source, q)]
                arrived(block, gbase[hop] + source * nh + q)
                if nk > 1:
                    send(block, block, gbase[hop] + source * nh + q, sibling)
        if nk > 1:
            for q in range(nh):
                for d in range(ny):
                    source = ys(d) * nk + 1 - k
                    arrived(
                        v_all.at[hop, row_part(source, q)], gbase[hop] + source * nh + q
                    )

    with jax.named_scope("barrier"):
        pl.semaphore_wait(barrier, len(peers))
    for q in range(nh):
        start_gather(0, q, y1[q * cut : (q + 1) * cut])

    if relayed:

        @pl.when(outer)
        def _():
            zrecv[:, 2] = jnp.zeros((2, own, width), LOW)

    w3t[...] = jnp.zeros_like(w3t)
    w3t[: s.classes, :] = w3t_ref[...].astype(LOW)
    w2 = w2_ref[...].astype(LOW)
    for a in range(n_sub):
        loads[a].wait()
        for b in range(cols // own):
            piece = tile[pl.ds(a * SUB, SUB), pl.ds(b * own, own)]
            cover = jnp.full((SUB, own), occ_ref[a, b].astype(FULL), FULL).astype(LOW)
            tile[pl.ds(a * SUB, SUB), pl.ds(b * own, own)] = piece * cover

    def spread(hop, finish):
        settle(of="hop")
        with jax.named_scope("gather_y"):
            complete_gather(hop)
        zbase = wide[hop]
        xbase = zbase + nz * nh
        order = list(range(nz - 1, -1, -1))

        def send_x(dz, dx, q):
            place = (dx - 1) * nz + dz
            send(
                xsend.at[place, part(q)],
                pool.at[hop * s.n_row + place, part(q)],
                xbase + place * nh + q,
                at(z, xs(dx), y, k),
                "hop",
            )

        sequence = []
        if relayed:
            for q in range(nh):
                sequence.append((3, q))
                if q:
                    sequence.append((2, q - 1))
                sequence.append((1, q))
            sequence.append((2, nh - 1))
            sequence += [(0, q) for q in range(nh)]
        else:
            for q in range(nh):
                sequence += [(dz, q) for dz in order if dz]
                if q:
                    sequence.append((0, q - 1))
            sequence.append((0, nh - 1))
        ready = set()
        with jax.named_scope("send_x"):
            for dz, q in sequence:
                for dx in range(1, nx):
                    if (dz, dx) not in ready:
                        ready.add((dz, dx))
                        rt = zs(dz) * nx + xs(dx)
                        xsend[(dx - 1) * nz + dz] = dot(
                            tile[row_block(rt), :], v_all[hop]
                        ).astype(LOW)
                    send_x(dz, dx, q)
            for dz in order:
                acc[:, dz * own : (dz + 1) * own] = dot(
                    tile[row_block(zs(dz) * nx + x), :], v_all[hop]
                )

        def send_z(dz, q):
            rows_q = slice(q * cut, (q + 1) * cut)
            total = acc[rows_q, dz * own : (dz + 1) * own]
            for dx in range(1, nx):
                place = (dx - 1) * nz + dz
                arrived(pool.at[hop * s.n_row + place, part(q)], xbase + place * nh + q)
                total = total + pool[hop * s.n_row + place, rows_q, :].astype(FULL)
            if not dz:
                return total
            there, slot, mark = zs(dz), dz - 1, zbase + dz * nh + q
            if relayed and dz == 3:
                there = is_inner * zs(3) + (1 - is_inner) * zs(1)
                slot, mark = 3 - is_inner, zbase + 3 * nh * is_inner + q
            if relayed and dz == 2:

                @pl.when(inner)
                def _():
                    arrived(zrecv.at[hop, 3, part(q)], zbase + q)
                    handed = zrecv[hop, 3, rows_q, :].astype(FULL)
                    zsend[dz - 1, rows_q, :] = (total + handed).astype(LOW)

                @pl.when(outer)
                def _():
                    zsend[dz - 1, rows_q, :] = total.astype(LOW)

            else:
                zsend[dz - 1, rows_q, :] = total.astype(LOW)
            send(
                zsend.at[dz - 1, part(q)],
                zrecv.at[hop, slot, part(q)],
                mark,
                at(there, x, y, k),
                "hop",
            )
            return total

        totals = [None] * nh

        def sum_z(q):
            total = totals[q]
            rows_q = slice(q * cut, (q + 1) * cut)
            for dz in range(1, nz):
                there, mark = zrecv.at[hop, dz - 1, part(q)], zbase + dz * nh + q
                if relayed and dz == 3:
                    pl.when(inner)(functools.partial(arrived, there, mark))
                else:
                    arrived(there, mark)
                total = total + zrecv[hop, dz - 1, rows_q, :].astype(FULL)
            finish(q, total)

        with jax.named_scope("send_z"):
            for dz, q in sequence[:-1]:
                totals[q] = send_z(dz, q)
                if not dz:
                    with jax.named_scope("sum_z0"):
                        sum_z(q)
        with jax.named_scope("sum_z1"):
            totals[nh - 1] = send_z(0, nh - 1)
            sum_z(nh - 1)

    bias = [bias_ref[i * width : (i + 1) * width].reshape(1, width) for i in range(2)]
    slopes, acts = [None] * nh, [None] * nh

    def first_done(q, total):
        rows_q = slice(q * cut, (q + 1) * cut)
        z1 = total + v_all[0, row_part(c, q), :].astype(FULL) + bias[0]
        act, slope = gelu_both(z1)
        h1 = act.astype(LOW) * valid_low[rows_q]
        start_gather(1, q, dot(h1, w2).astype(LOW))
        acts[q], slopes[q] = h1, slope * valid_col[rows_q]

    spread(0, first_done)
    h1t = jnp.concatenate(acts, axis=0).astype(FULL).T.astype(LOW)
    slope1t = jnp.concatenate(slopes, axis=0).T

    xt_base = gbase[1] + s.n_col

    def second_done(q, total):
        rows_q = slice(q * cut, (q + 1) * cut)
        z2 = total + v_all[1, row_part(c, q), :].astype(FULL) + bias[1]
        act, slope = gelu_both(z2)
        acts[q] = act.astype(LOW) * valid_low[rows_q]
        slopes[q] = slope * valid_col[rows_q]
        if (q + 1) % (nh // 2) == 0:
            lane = q // (nh // 2)
            some = jnp.concatenate(acts[lane * (nh // 2) : q + 1], axis=0)
            y3t = dot_nt(w3t[...], some).astype(LOW)
            mine = v3_half(c, lane)
            mine[...] = y3t
            for dy, dk in col_far:
                send(mine, mine, gbase[0] + 2 * c + lane, (r, ys(dy) * nk + ks(dk)))

    def v3_half(index, lane):
        return v3_all.at[index, :, pl.ds(lane * (own // 2), own // 2)]

    spread(1, second_done)
    h2 = jnp.concatenate(acts, axis=0)

    with jax.named_scope("hop3_gather"):
        slope2t = jnp.concatenate(slopes, axis=0).T
        settle(s.n_col - 1)
        for lane in range(2):
            for dy, dk in reversed(col_far):
                source = ys(ny - dy) * nk + ks(nk - dk)
                arrived(v3_half(source, lane), gbase[0] + 2 * source + lane)
    with jax.named_scope("hop3_sum"):
        pbase = wide[0]
        v3 = jnp.concatenate([v3_all[i] for i in range(s.n_col)], axis=1)
        for dz, dx in row_far:
            place = dz * nx + dx
            rt = zs(dz) * nx + xs(dx)
            p3send[place] = dot_nt(v3, tile[row_block(rt), :]).astype(LOW)
            send(p3send.at[place], p3recv.at[place], pbase + place, (rt, c))
        total = dot_nt(v3, tile[row_block(r), :])
        for dz, dx in reversed(row_far):
            place = dz * nx + dx
            arrived(p3recv.at[place], pbase + place)
            total = total + p3recv[place].astype(FULL)
    total = total + v3_all[c].astype(FULL)

    place = lax.broadcasted_iota(jnp.int32, (s.cls, own), 0)
    real = place < s.classes
    on_diag = lax.broadcasted_iota(jnp.int32, (s.cls, s.classes), 0) == lax.broadcasted_iota(
        jnp.int32, (s.cls, s.classes), 1
    )
    bias3 = jnp.sum(
        jnp.where(on_diag, bias_ref[2 * width :].reshape(1, s.classes), 0.0), axis=1, keepdims=True
    )
    logits = jnp.where(real, total + bias3, -1e30)
    shifted = logits - jnp.max(logits, axis=0, keepdims=True)
    weight = jnp.where(real, jnp.exp(shifted), 0.0)
    norm = jnp.sum(weight, axis=0, keepdims=True)
    logp = shifted - jnp.log(norm)
    target = jnp.where(place == lab_ref[...], 1.0 - SMOOTH, 0.0) + SMOOTH / s.classes
    target = jnp.where(real, target, 0.0)
    row_loss = -jnp.sum(jnp.where(real, target * logp, 0.0), axis=0, keepdims=True)
    loss = jnp.sum(row_loss * counted, axis=1, keepdims=True)
    number = jnp.sum(counted, axis=1, keepdims=True)
    dlt = ((weight / norm - target) * counted).astype(LOW)

    with jax.named_scope("back3_gather"):
        base = wide[1]
        mine = dl_all.at[r]
        mine[...] = dlt
        for dz, dx in row_far:
            send(mine, mine, base + r, (zs(dz) * nx + xs(dx), c))
        here = dot(dlt, tile[row_block(r), :])
        for dz, dx in reversed(row_far):
            source = zback(dz) * nx + xs(nx - dx)
            arrived(dl_all.at[source], base + source)
            here = here + dot(dl_all[source], tile[row_block(source), :])
        acc[: s.cls, :cols] = here
    with jax.named_scope("back3_sum"):
        qbase = gbase[1]
        for dy, dk in col_far:
            place = dy * nk + dk
            ct = ys(dy) * nk + ks(dk)
            q3send[place] = acc[: s.cls, row_block(ct)].astype(LOW)
            send(q3send.at[place], q3recv.at[place], qbase + place, (r, ct))
        total = dlt.astype(FULL) + acc[: s.cls, row_block(c)]
        for dy, dk in reversed(col_far):
            place = dy * nk + dk
            arrived(q3recv.at[place], qbase + place)
            total = total + q3recv[place].astype(FULL)
    qt = total.astype(LOW)
    dh2t = lax.dot_general(
        w3t[...], qt, (((0,), (0,)), ((), ())), preferred_element_type=FULL
    )
    step_cols = min(cols, 1024)

    def gained(values, block, fresh=False):
        for j in range(0, cols, step_cols):
            here = dot(values, tile[block, j : j + step_cols])
            if fresh:
                acc[:, j : j + step_cols] = here
            else:
                acc[:, j : j + step_cols] += here

    def halves(lane, row):
        return (
            pl.ds(row * (width // 2), width // 2),
            pl.ds(lane * (own // 2), own // 2),
        )

    quarters = [(lane, row) for lane in range(2) for row in range(2)]
    def receive(hop, values, meanwhile=None, late=None):
        base = wide[hop]
        first = hop * s.n_row

        def piece(dz, dx, q):
            return pool.at[(first + dx * nz + dz, *halves(*quarters[q]))]

        def to_z(dz, q, when=None, start=True):
            return send(
                piece(0, 0, q),
                piece(dz, 0, q),
                base + dz * nh + q,
                at(zs(dz), x, y, k),
                when=when,
                start=start,
            )

        def to_x(dz, q, start=True):
            return [
                send(
                    piece(dz, 0, q),
                    piece(dz, dx, q),
                    base + (dx * nz + dz) * nh + q,
                    at(z, xs(dx), y, k),
                    start=start,
                )
                for dx in range(1, nx)
            ]

        own_parts = []
        for lane in range(2):
            mine = values(lane)
            own_parts.append(mine)
            pool[first, :, lane * (own // 2) : (lane + 1) * (own // 2)] = mine
            for q in (2 * lane, 2 * lane + 1):
                if relayed:
                    to_z(2, q)
                    to_z(1, q)
                else:
                    for dz in range(nz - 1, 0, -1):
                        to_z(dz, q)
                to_x(0, q)

        def source(dz, dx):
            return row_block(zback(dz) * nx + xs(nx - dx))

        gained(jnp.concatenate(own_parts, axis=1), row_block(r), fresh=True)
        if meanwhile is not None:
            meanwhile()

        passing = {
            (dz, q): to_x(dz, q, start=False) for q in range(nh) for dz in range(1, nz)
        }

        def step(dz, q):
            arrived(piece(dz, 0, q), base + dz * nh + q)
            for copy in passing[dz, q]:
                copy.start()

        if relayed:
            relays = [
                send(
                    piece(2, 0, q),
                    piece(3, 0, q),
                    base + 3 * nh + q,
                    at(zs(1), x, y, k),
                    when=inner,
                    start=False,
                )
                for q in range(nh)
            ]
            paced = [to_z(3, q, inner, start=False) for q in range(nh)]

            @pl.when(inner)
            def _():
                for q in range(nh):
                    arrived(piece(2, 0, q), base + 2 * nh + q)
                    relays[q].start()
                    paced[q].start()
                    for copy in passing[2, q]:
                        copy.start()
                    step(1, q)
                    if q > 1:
                        step(3, q - 2)
                for q in range(nh - 2, nh):
                    step(3, q)

            @pl.when(outer)
            def _():
                for q in range(nh + 2):
                    if q < nh:
                        step(1, q)
                    if 0 < q <= nh:
                        step(2, q - 1)
                    if q > 2:
                        step(3, q - 3)
                for q in range(nh - 1, nh):
                    step(3, q)
        else:
            for q in range(nh):
                for dz in range(1, nz):
                    step(dz, q)
        for dz in range(1, nz):
            gained(pool[first + dz], source(dz, 0))
        if late is not None:
            late()
        for dz in range(nz):
            for dx in range(1, nx):
                for q in range(nh):
                    arrived(piece(dz, dx, q), base + (dx * nz + dz) * nh + q)
                gained(pool[first + dx * nz + dz], source(dz, dx))

    dz2t = (dh2t * slope2t).astype(LOW)
    half_own = own // 2

    def features_out():
        for d in range(1, ny):
            send(own_xt, own_xt, xt_base + c, at(z, x, ys(d), k))
        if nk > 1:
            send(own_xt, own_xt, xt_base + c, sibling)

    with jax.named_scope("back2_rows"):
        settle()
        receive(0, lambda lane: dz2t[:, lane * half_own : (lane + 1) * half_own], features_out)
    cbase = gbase[0] + 2 * s.n_col
    ybase = gbase[1] + 2 * s.n_col

    def lane_part(index, lane):
        return pl.ds(pl.multiple_of(index * own + lane * half_own, half_own), half_own)

    def held(place, lane):
        return xsend.at[place, :, pl.ds(lane * half_own, half_own)]

    def crecv(dy, lane):
        return v_all.at[0, dy * own : (dy + 1) * own, pl.ds(lane * half_own, half_own)]

    def yrecv(dy, lane):
        return crecv(dy + (ny if nk > 1 else 0), lane)

    column_totals = [None, None]
    with jax.named_scope("back2_cols"):
        for lane in range(2):
            for dy in range(ny - 1, -1, -1):
                if nk > 1:
                    there = held(dy, lane)
                    there[...] = acc[:, lane_part(ys(dy) * nk + 1 - k, lane)].astype(LOW)
                    send(there, crecv(dy, lane), cbase + 2 * dy + lane, sibling)
        for lane in range(2):
            for dy in range(ny - 1, -1, -1):
                here = acc[:, lane_part(ys(dy) * nk + k, lane)]
                if nk > 1:
                    arrived(crecv(dy, lane), cbase + 2 * dy + lane)
                    here = here + crecv(dy, lane)[...].astype(FULL)
                if dy:
                    there = held(ny + dy, lane)
                    there[...] = here.astype(LOW)
                    send(
                        there, yrecv(dy, lane), ybase + 2 * dy + lane, at(z, x, ys(dy), k)
                    )
                else:
                    column_totals[lane] = here
        for d in range(1, ny):
            source = ys(ny - d) * nk + k
            arrived(xt_all.at[source], xt_base + source)
            if nk > 1:
                send(xt_all.at[source], xt_all.at[source], xt_base + source, sibling)

    dy2_parts, dz1_parts = [], []

    def first_slopes(lane):
        lanes_q = slice(lane * half_own, (lane + 1) * half_own)
        total = column_totals[lane] + dz2t[:, lanes_q].astype(FULL)
        with jax.named_scope("y_wait"):
            for dy in range(1, ny):
                arrived(yrecv(dy, lane), ybase + 2 * dy + lane)
                total = total + yrecv(dy, lane)[...].astype(FULL)
        dy2_parts.append(total.astype(LOW))
        dz1_parts.append((dot(w2, dy2_parts[lane]) * slope1t[:, lanes_q]).astype(LOW))
        return dz1_parts[lane]

    lanes, plane = s.lanes, s.plane
    me = y * nx + x
    others = [(dx, dy) for dx in range(nx) for dy in range(ny) if dx or dy]

    def lane_block(index):
        return pl.ds(pl.multiple_of(index * lanes, lanes), lanes)

    class Total:
        def __init__(self, start, rows):
            self.all = pl.ds(start, rows)
            self.start, self.rows = start, rows
            self.n = rows // plane
            self.short = pl.ds(start // plane, self.n)
            self.base = rslots(1 + 3 * plane + nz)

        def piece(self, index):
            return pl.ds(pl.multiple_of(self.start + index * self.n, 16), self.n)

        def core_send(self, other):
            if nk > 1:
                half_send[self.all, :] = other.astype(LOW)
                send(half_send.at[self.all], half_recv.at[self.all], self.base, sibling)

        def plane_send(self, mine):
            if nk > 1:
                arrived(half_recv.at[self.all], self.base)
                mine = mine + half_recv[self.all, :].astype(FULL)
            half[self.all, :] = mine.astype(LOW)
            base = self.base + 1
            for dx, dy in others:
                there = ys(dy) * nx + xs(dx)
                send(
                    half.at[self.piece(there)],
                    plane_recv.at[me, self.short],
                    base + me,
                    at(z, xs(dx), ys(dy), k),
                )
            plane_recv[me, self.short, :] = half[self.piece(me), :]

        def line_send(self):
            base = self.base + 1
            for dx, dy in others:
                there = ys(dy) * nx + xs(dx)
                arrived(plane_recv.at[there, self.short], base + there)
            total = plane_recv[0, self.short, :].astype(FULL)
            for i in range(1, plane):
                total = total + plane_recv[i, self.short, :].astype(FULL)
            quarter[z, self.short, :] = total.astype(LOW)
            mine = quarter.at[z, self.short]
            base = self.base + 1 + plane
            for dz in range(nz - 1, 0, -1):
                send(mine, mine, base + z, at(zs(dz), x, y, k))

        def back_send(self):
            base = self.base + 1 + plane
            for dz in range(1, nz):
                arrived(quarter.at[zback(dz), self.short], base + zback(dz))
            total = quarter[0, self.short, :].astype(FULL)
            for i in range(1, nz):
                total = total + quarter[i, self.short, :].astype(FULL)
            base = self.base + 1 + plane + nz
            mine = fin.at[k, self.piece(me)]
            mine[...] = total.astype(LOW)
            for dx, dy in others:
                send(mine, mine, base + me, at(z, xs(dx), ys(dy), k))
            if nk > 1:
                send(mine, mine, base + plane + me, sibling)

        def back_forward(self):
            base = self.base + 1 + plane + nz
            for dx, dy in others:
                there = ys(dy) * nx + xs(dx)
                block = fin.at[k, self.piece(there)]
                arrived(block, base + there)
                if nk > 1:
                    send(block, block, base + plane + there, sibling)

        def end(self):
            base = self.base + 1 + plane + nz
            if nk > 1:
                for i in range(plane):
                    arrived(fin.at[1 - k, self.piece(i)], base + plane + i)

    written = []

    def write(start, count):
        rows_w = pl.ds(start, count)
        copy = pltpu.make_async_copy(
            fin.at[:, rows_w], grad_ref.at[:, rows_w], lsem.at[n_sub + len(written)]
        )
        copy.start()
        written.append(copy)

    one_a = Total(0, s.cut_rows)
    one_b = Total(s.cut_rows, s.one_rows - s.cut_rows)
    two = Total(s.one_rows, s.two_rows)
    tail = s.two_rows - width - s.cls

    def early():
        grad3t = dot(qt, h2)
        dy2t = jnp.concatenate(dy2_parts, axis=1)
        grad2 = dot_nt(h1t, dy2t)
        acc_two = jnp.concatenate(
            [grad2, grad3t] + ([jnp.zeros((tail, width), FULL)] if tail else []), axis=0
        )
        if nk > 1:
            first, second = acc_two[:, :lanes], acc_two[:, lanes:]
            low_core = (k == 0).astype(FULL)
            two.core_send(second * low_core + first * (1.0 - low_core))
            two.plane_send(first * low_core + second * (1.0 - low_core))
        else:
            two.plane_send(acc_two)

    with jax.named_scope("back1_rows"):
        receive(1, first_slopes, early, two.line_send)
    with jax.named_scope("grad1"):
        dz1t = jnp.concatenate(dz1_parts, axis=1)
        acc[:, row_block(c)] += dz1t.astype(FULL)
        if nk > 1:
            for d in range(ny):
                source = ys(d) * nk + 1 - k
                arrived(xt_all.at[source], xt_base + source)

        low_core = (k == 0).astype(FULL)

        def grad_one(start, stop):
            total = None
            end = min(stop, s.feat_up)
            for i in range(s.n_col):
                here = acc[:, i * own : (i + 1) * own].astype(LOW)
                here = dot_nt(xt_all[i, start:end, :], here)
                total = here if total is None else total + here
            if end < stop:
                total = jnp.concatenate([total, jnp.zeros((stop - end, width), FULL)], axis=0)
            if nk == 1:
                return None, total
            first, second = total[:, :lanes], total[:, lanes:]
            return (
                second * low_core + first * (1.0 - low_core),
                first * low_core + second * (1.0 - low_core),
            )

        other, mine_a = grad_one(0, s.cut_rows)
        one_a.core_send(other)
        other, mine_b = grad_one(s.cut_rows, s.one_rows)
        one_b.core_send(other)
        one_a.plane_send(mine_a)
        one_b.plane_send(mine_b)
        ones = jnp.ones((8, own), LOW)
        row = lax.broadcasted_iota(jnp.int32, (8, width), 0)
        lane = lax.broadcasted_iota(jnp.int32, (8, width), 1)
        bias_three = jnp.concatenate([dlt, jnp.zeros((width - s.cls, own), LOW)], axis=0)
        misc = jnp.where(row == 0, dot_nt(ones, dz1t), 0.0)
        misc = jnp.where(row == 1, dot_nt(ones, dz2t), misc)
        misc = jnp.where(row == 2, dot_nt(ones, bias_three), misc)
        misc = jnp.where((row == 3) & (lane == 0), loss, misc)
        misc = jnp.where((row == 3) & (lane == 1), number, misc)
        mbase = rslots(1 + plane + nz)
        misc_k[0] = misc
        if nk > 1:
            send(misc_k.at[0], misc_k.at[1], mbase, sibling)

    with jax.named_scope("sum_plane"):
        if nk > 1:
            arrived(misc_k.at[1], mbase)
            misc = misc_k[0] + misc_k[1]
        misc_p[me] = misc
        mbase = mbase + 1
        for dx, dy in others:
            send(misc_p.at[me], misc_p.at[me], mbase + me, at(z, xs(dx), ys(dy), k))
        left = len(pending)
        two.back_send()
    with jax.named_scope("sum_line"):
        one_a.line_send()
        one_b.line_send()
        for dx, dy in others:
            there = ys(dy) * nx + xs(dx)
            arrived(misc_p.at[there], mbase + there)
        misc = misc_p[0]
        for i in range(1, plane):
            misc = misc + misc_p[i]
        mbase = mbase + plane
        misc_z[z] = misc
        for dz in range(1, nz):
            send(misc_z.at[z], misc_z.at[z], mbase + z, at(zs(dz), x, y, k))
        two.back_forward()
        two.end()
        settle(len(pending) - left)
    with jax.named_scope("back_line"):
        one_a.back_send()
        one_b.back_send()
        for dz in range(1, nz):
            arrived(misc_z.at[zback(dz)], mbase + zback(dz))
        misc = misc_z[0]
        for i in range(1, nz):
            misc = misc + misc_z[i]
        misc_k[0] = jnp.where(row == 4, 1.0 / misc[3:4, 1:2], misc)
        written.append(
            pltpu.make_async_copy(misc_k.at[0], misc_ref.at[pl.ds(0, 8)], lsem.at[n_sub])
        )
        written[0].start()
        write(s.one_rows, s.two_rows)
    with jax.named_scope("back_plane"):
        one_a.back_forward()
        one_b.back_forward()
        one_a.end()
        write(0, s.cut_rows)
        one_b.end()
        write(s.cut_rows, s.one_rows - s.cut_rows)
    with jax.named_scope("settle"):
        settle()
        for copy in written:
            copy.wait()
    assert rcount[0] <= s.arrivals


def update_pieces(s):
    some = up(s.feat // 4, 16)
    cuts = [min(i * some, s.feat) for i in range(5)]
    one = [(0, start, stop - start) for start, stop in zip(cuts, cuts[1:]) if stop > start]
    return (*one, (1, 0, s.width), (2, 0, s.classes))


def adam_kernel(s, grad_ref, misc_ref, *refs):
    ins, outs, scratch = refs[:12], refs[12:26], refs[26:]
    bias_out, ends, *held = scratch[:-1]
    sem_out = scratch[-1]
    width, classes, lanes = s.width, s.classes, s.lanes
    grad_at = (0, s.one_rows, s.one_rows + width)

    stores = []

    def store(source, target):
        copy = pltpu.make_async_copy(source, target, sem_out.at[len(stores)])
        copy.start()
        stores.append(copy)

    total = misc_ref[3:4, 1:2]
    scale = misc_ref[4:5, 0:1]
    for (which, start, rows), target in zip(update_pieces(s), held):
        span = slice(start, start + rows)
        for i in range(s.nk):
            lane = slice(i * lanes, (i + 1) * lanes)
            first = grad_at[which] + start
            grad = grad_ref[i, first : first + up(rows, 16), :].astype(FULL)[:rows]
            weight, one, two = (ins[3 * which + j][span, lane] for j in range(3))
            for j, new in enumerate(adam_update(weight, one, two, grad * scale)):
                target[j, :, lane] = new
        for j in range(3):
            store(target.at[j], outs[3 * which + j].at[pl.ds(start, rows)])
    for i, size in enumerate((width, width, classes)):
        span = slice(i * width, i * width + size)
        weight, first, second = (ins[9 + j][span] for j in range(3))
        new = adam_update(weight, first, second, misc_ref[i, :size] * misc_ref[4, :size])
        for j in range(3):
            bias_out[j][span] = new[j]
    for j in range(3):
        store(bias_out[j], outs[9 + j])
    ends[0] = misc_ref[3:4, 0:1]
    ends[1] = total
    for i in range(2):
        store(ends.at[i], outs[12 + i])
    for copy in stores:
        copy.wait()


def shards(
    sizes,
    features,
    adjacency,
    occupancy,
    labels,
    train_mask,
    node_count,
    weight_one,
    weight_two,
    weight_three,
    biases,
    first_one,
    first_two,
    first_three,
    first_bias,
    second_one,
    second_two,
    second_three,
    second_bias,
):
    own, feat = features.shape
    width = weight_two.shape[0]
    classes = weight_three.shape[1]
    s = sizes(own, feat, width, classes)
    rows, cols = adjacency.shape
    lanes = s.lanes
    vmem = pl.BlockSpec(memory_space=pltpu.VMEM)
    smem = pl.BlockSpec(memory_space=pltpu.SMEM)
    anywhere = pl.BlockSpec(memory_space=pl.ANY)
    block = (own, width)
    small = (s.cls, own)
    shapes = [
        ((rows, cols), LOW),
        ((s.feat_up, width), LOW),
        ((s.cls, width), LOW),
        ((s.n_col, s.feat_up, own), LOW),
        ((2, s.n_col * own, width), LOW),
        ((2 * s.n_row, *block), LOW),
        ((max(2 * s.ny, s.n_row - s.nz), *block), LOW),
        ((max(1, s.nz - 1), *block), LOW),
        ((2, s.nz if s.relayed else max(1, s.nz - 1), *block), LOW),
        ((s.n_col, *small), LOW),
        ((s.n_row, *small), LOW),
        ((s.n_row, *small), LOW),
        ((s.n_row, *small), LOW),
        ((s.n_col, *small), LOW),
        ((s.n_col, *small), LOW),
        ((width, max(cols, s.nz * own)), FULL),
        ((s.grad_rows, lanes), LOW),
        ((s.grad_rows, lanes), LOW),
        ((s.grad_rows, lanes), LOW),
        ((s.plane, s.grad_rows // s.plane, lanes), LOW),
        ((s.nz, s.grad_rows // s.plane, lanes), LOW),
        ((s.nk, s.grad_rows, lanes), LOW),
        ((2, 8, width), FULL),
        ((s.plane, 8, width), FULL),
        ((s.nz, 8, width), FULL),
    ]
    bytes_held = sum(math.prod(shape) * jnp.dtype(kind).itemsize for shape, kind in shapes)
    limit = min(62, 16 + bytes_held // 2**20) * 2**20
    grads, misc = pl.pallas_call(
        functools.partial(kernel, s),
        out_shape=(
            pltpu.VMEM((s.nk, s.grad_rows, lanes), LOW),
            pltpu.VMEM((8, width), FULL),
        ),
        in_specs=[
            vmem,
            anywhere,
            smem,
            vmem,
            vmem,
            smem,
            vmem,
            vmem,
            vmem,
            vmem,
        ],
        out_specs=(anywhere, anywhere),
        scratch_shapes=[
            *[pltpu.VMEM(shape, kind) for shape, kind in shapes],
            pltpu.SemaphoreType.DMA((s.sends,)),
            pltpu.SemaphoreType.DMA((s.arrivals,)),
            pltpu.SemaphoreType.DMA((rows // SUB + 4,)),
        ],
        compiler_params=pltpu.CompilerParams(
            collective_id=0, has_side_effects=True, vmem_limit_bytes=limit
        ),
        cost_estimate=pl.CostEstimate(
            flops=12 * rows * cols * width, bytes_accessed=2 * rows * cols, transcendentals=0
        ),
        name="step",
    )(
        *[
            pltpu.with_memory_space_constraint(a, pltpu.HBM)
            for a in (features.T, adjacency)
        ],
        pltpu.with_memory_space_constraint(occupancy, pltpu.HBM),
        *[
            pltpu.with_memory_space_constraint(a, pltpu.HBM)
            for a in (labels.reshape(1, own), train_mask.reshape(1, own))
        ],
        node_count,
        *[
            pltpu.with_memory_space_constraint(a, pltpu.HBM)
            for a in (weight_one, weight_two, weight_three.T, biases)
        ],
    )
    state = (
        weight_one,
        first_one,
        second_one,
        weight_two,
        first_two,
        second_two,
        weight_three.T,
        first_three.T,
        second_three.T,
        biases,
        first_bias,
        second_bias,
    )
    new = pl.pallas_call(
        functools.partial(adam_kernel, s),
        out_shape=(
            *[jax.ShapeDtypeStruct(a.shape, FULL) for a in state],
            jax.ShapeDtypeStruct((1, 1), FULL),
            jax.ShapeDtypeStruct((1, 1), FULL),
        ),
        in_specs=[vmem] * 14,
        out_specs=(anywhere,) * 14,
        scratch_shapes=[
            [pltpu.VMEM(biases.shape, FULL)] * 3,
            pltpu.VMEM((2, 1, 1), FULL),
            *[pltpu.VMEM((3, rows, width), FULL) for _, _, rows in update_pieces(s)],
            pltpu.SemaphoreType.DMA((3 * len(update_pieces(s)) + 5,)),
        ],
        compiler_params=pltpu.CompilerParams(vmem_limit_bytes=32 * 2**20),
        name="update",
    )(grads, misc, *state)
    return (
        *new[:6],
        *[a.T for a in new[6:9]],
        *new[9:12],
        new[12].reshape(()),
        new[13].reshape(()),
    )


def solution(mesh):
    placed = (
        P(("row", "col"), None),
        P("col", "row"),
        P("col", "row"),
        P(("row", "col")),
        P(("row", "col")),
        P(("row", "col")),
        *[P()] * 12,
    )
    sizes = functools.partial(Sizes, mesh.shape["row"], mesh.shape["col"])
    return jax.shard_map(
        functools.partial(shards, sizes),
        mesh=mesh,
        in_specs=placed,
        out_specs=(P(),) * 14,
        check_vma=False,
    )
```

```python
import functools
import math

import jax
import jax.numpy as jnp
from jax import lax
from jax.experimental import pallas as pl
from jax.experimental.pallas import tpu as pltpu
from jax.sharding import PartitionSpec as P

SUB = 512
STEP = 5


B_ONE = 0.5
B_TWO = 0.5
RATE = 0.05
DECAY = 0.01
EPSILON = 1e-08
SMOOTH = 0.1

MESH = pl.DeviceIdType.MESH
LOW = jnp.bfloat16
FULL = jnp.float32
GELU_A = 0.7978845608028654
GELU_B = 0.044715


def adam_update(weight, first, second, grad):
    first_new = B_ONE * first + (1.0 - B_ONE) * grad
    second_new = B_TWO * second + (1.0 - B_TWO) * grad * grad
    fix_one = 1.0 - B_ONE**STEP
    fix_two = 1.0 - B_TWO**STEP
    scaled = (first_new * (1.0 / fix_one)) / (jnp.sqrt(second_new * (1.0 / fix_two)) + EPSILON)
    return (first_new, second_new, weight - RATE * (scaled + DECAY * weight))


def up(value, unit):
    return -(-value // unit) * unit


def dot(left, right):
    return jnp.dot(left, right, preferred_element_type=FULL)


def dot_nt(left, right):
    return lax.dot_general(left, right, (((1,), (1,)), ((), ())), preferred_element_type=FULL)


def gelu_both(z):
    t = jnp.tanh(GELU_A * (z + GELU_B * z * z * z))
    half = 0.5 * (1.0 + t)
    slope = half + 0.5 * z * (1.0 - t * t) * (GELU_A * (1.0 + 3.0 * GELU_B * z * z))
    return z * half, slope


class Sizes:
    def __init__(self, n_row, n_col, own, feat, width, classes):
        self.n_row, self.n_col = n_row, n_col
        self.nk = 2 if n_col % 2 == 0 else 1
        self.ny = n_col // self.nk
        self.nx = self.ny if n_row % self.ny == 0 else 1
        self.nz = n_row // self.nx
        self.own, self.feat, self.width, self.classes = own, feat, width, classes
        self.feat_up = up(feat, 128)
        self.cls = up(classes, 16)
        self.plane = self.nx * self.ny
        self.one_rows = up(feat + 1, 16 * self.plane)
        self.two_rows = up(width + self.cls, 16 * self.plane)
        self.grad_rows = self.one_rows + self.two_rows
        self.lanes = width // self.nk
        units = self.one_rows // (16 * self.plane)
        self.cut_rows = (units + 1) // 2 * 16 * self.plane
        cuts = [own // 4 * i for i in range(5)]
        self.parts = [(start, stop - start) for start, stop in zip(cuts, cuts[1:])]
        self.nh = len(self.parts)
        self.relayed = self.nz == 4
        self.sends = 3 * (n_row + n_col) + 3 * self.plane
        wide = 2 * self.nh * (n_row + n_col)
        self.arrivals = wide + 3 * (1 + 3 * self.plane + self.nz) + 1 + self.plane + self.nz


def kernel(
    s,
    xt_ref,
    adj_ref,
    occ_ref,
    lab_ref,
    mask_ref,
    cnt_ref,
    w1_ref,
    w2_ref,
    w3t_ref,
    bias_ref,
    grad_ref,
    misc_ref,
    tile,
    w1b,
    w3t,
    xt_all,
    v_all,
    pool,
    xsend,
    zsend,
    zrecv,
    v3_all,
    p3send,
    p3recv,
    dl_all,
    q3send,
    q3recv,
    acc,
    half_send,
    half_recv,
    half,
    plane_recv,
    quarter,
    fin,
    misc_k,
    misc_p,
    misc_z,
    ssem,
    rsem,
    lsem,
):
    nx, ny, nz, nk = s.nx, s.ny, s.nz, s.nk
    own, width = s.own, s.width
    r, c = lax.axis_index("row"), lax.axis_index("col")
    z, x = r // nx, r % nx
    y, k = c // nk, c % nk

    def at(zz, xx, yy, kk):
        return (zz * nx + xx, yy * nk + kk)

    def xs(d):
        return lax.rem(x + d, nx)

    def ys(d):
        return lax.rem(y + d, ny)

    def zs(d):
        if nz & (nz - 1):
            return lax.rem(z + d, nz)
        there, bit = z, 1
        while bit < nz:
            if d & bit:
                there = there + bit - 2 * bit * lax.rem(there // bit, 2)
            bit *= 2
        return there

    def zback(d):
        return zs(d) if not nz & (nz - 1) else lax.rem(z + nz - d, nz)

    sibling = at(z, x, y, 1 - k)
    relayed = s.relayed
    is_inner = lax.rem((z + 1) // 2, 2)
    inner = is_inner == 1
    outer = is_inner == 0
    line = [dz for dz in range(nz - 1, -1, -1)]
    row_far = [(dz, dx) for dz in line for dx in range(nx - 1, -1, -1) if dz or dx]
    col_far = [(dy, dk) for dy in range(ny - 1, -1, -1) for dk in range(nk - 1, -1, -1) if dy or dk]

    def ks(d):
        return lax.rem(k + d, nk)


    rows, cols = tile.shape
    n_sub = rows // SUB
    loads = [
        pltpu.make_async_copy(
            adj_ref.at[pl.ds(a * SUB, SUB)], tile.at[pl.ds(a * SUB, SUB)], lsem.at[a]
        )
        for a in range(n_sub)
    ]
    for load in loads:
        load.start()

    peers = []
    for d in range(1, s.n_row):
        peers.append((lax.rem(r + d, s.n_row), c))
    for d in range(1, s.n_col):
        peers.append((r, lax.rem(c + d, s.n_col)))
    for dx in range(1, nx):
        for dy in range(1, ny):
            peers.append(at(z, xs(dx), ys(dy), k))
    barrier = pltpu.get_barrier_semaphore()
    for peer in peers:
        pl.semaphore_signal(barrier, inc=1, device_id=peer, device_id_type=MESH)

    free = list(range(s.sends))
    pending = []

    def send(src, dst, recv_slot, device, of=None, when=None, start=True):
        if not free:
            settle(len(pending) - 1)
        copy = pltpu.make_async_remote_copy(
            src_ref=src,
            dst_ref=dst,
            send_sem=ssem.at[free[0]],
            recv_sem=rsem.at[recv_slot],
            device_id=device,
            device_id_type=MESH,
        )
        if start:
            if when is None:
                copy.start()
            else:
                pl.when(when)(copy.start)
        pending.append((copy, free.pop(0), of, when))
        return copy

    def arrived(dst, recv_slot):
        pltpu.make_async_remote_copy(
            src_ref=dst,
            dst_ref=dst,
            send_sem=ssem.at[0],
            recv_sem=rsem.at[recv_slot],
            device_id=sibling,
            device_id_type=MESH,
        ).wait_recv()

    def settle(keep=0, of=None):
        done = [p for p in pending if p[2] == of] if of else pending[: len(pending) - keep]
        for item in done:
            if item[3] is None:
                item[0].wait_send()
            else:
                pl.when(item[3])(item[0].wait_send)
            free.append(item[1])
        left = [p for p in pending if all(p is not q for q in done)]
        pending[:] = left

    rcount = [0]

    def rslots(n):
        rcount[0] += n
        return rcount[0] - n

    def row_block(index):
        return pl.ds(pl.multiple_of(index * own, own), own)

    nh = s.nh

    def row_part(index, q):
        start, count = s.parts[q]
        return pl.ds(pl.multiple_of(index * own + start, count), count)

    def part(q):
        return pl.ds(*s.parts[q])

    def span_of(q):
        start, count = s.parts[q]
        return slice(start, start + count)

    valid_col = (lax.broadcasted_iota(jnp.int32, (own, width), 0) < cnt_ref[0]).astype(FULL)
    valid_low = valid_col.astype(LOW)
    valid_row = (lax.broadcasted_iota(jnp.int32, (1, own), 1) < cnt_ref[0]).astype(FULL)
    counted = mask_ref[...].astype(FULL) * valid_row

    prologue = jax.named_scope("prologue")
    prologue.__enter__()
    pad = s.feat_up - up(s.feat, 16) + 16
    own_xt = xt_all.at[c]
    own_xt[s.feat_up - pad :, :] = jnp.zeros((pad, own), LOW)
    w1b[s.feat_up - pad :, :] = jnp.zeros((pad, width), LOW)
    x_valid = (lax.broadcasted_iota(jnp.int32, (s.feat, own), 1) < cnt_ref[0]).astype(LOW)
    own_xt[: s.feat, :] = xt_ref[...] * x_valid
    w1b[: s.feat, :] = w1_ref[...].astype(LOW)
    y1 = lax.dot_general(
        own_xt[...], w1b[...], (((0,), (0,)), ((), ())), preferred_element_type=FULL
    ).astype(LOW)

    wide = [rslots(s.n_row * nh) for _ in range(2)]
    gbase = [rslots(s.n_col * nh) for _ in range(2)]
    prologue.__exit__(None, None, None)

    def start_gather(hop, q, values):
        mine = v_all.at[hop, row_part(c, q)]
        mine[...] = values
        for d in range(1, ny):
            send(mine, mine, gbase[hop] + c * nh + q, at(z, x, ys(d), k))
        if nk > 1:
            send(mine, mine, gbase[hop] + c * nh + q, sibling)

    def complete_gather(hop):
        for q in range(nh):
            for d in range(1, ny):
                source = ys(ny - d) * nk + k
                block = v_all.at[hop, row_part(source, q)]
                arrived(block, gbase[hop] + source * nh + q)
                if nk > 1:
                    send(block, block, gbase[hop] + source * nh + q, sibling)
        if nk > 1:
            for q in range(nh):
                for d in range(ny):
                    source = ys(d) * nk + 1 - k
                    arrived(
                        v_all.at[hop, row_part(source, q)], gbase[hop] + source * nh + q
                    )

    with jax.named_scope("barrier"):
        pl.semaphore_wait(barrier, len(peers))
    for q in range(nh):
        start_gather(0, q, y1[span_of(q)])

    if relayed:

        @pl.when(outer)
        def _():
            zrecv[:, 2] = jnp.zeros((2, own, width), LOW)

    w3t[...] = jnp.zeros_like(w3t)
    w3t[: s.classes, :] = w3t_ref[...].astype(LOW)
    w2 = w2_ref[...].astype(LOW)
    for a in range(n_sub):
        loads[a].wait()
        for b in range(cols // own):
            piece = tile[pl.ds(a * SUB, SUB), pl.ds(b * own, own)]
            cover = jnp.full((SUB, own), occ_ref[a, b].astype(FULL), FULL).astype(LOW)
            tile[pl.ds(a * SUB, SUB), pl.ds(b * own, own)] = piece * cover

    def spread(hop, finish):
        settle(of="hop")
        with jax.named_scope("gather_y"):
            complete_gather(hop)
        zbase = wide[hop]
        xbase = zbase + nz * nh
        order = list(range(nz - 1, -1, -1))

        def send_x(dz, dx, q):
            place = (dx - 1) * nz + dz
            send(
                xsend.at[place, part(q)],
                pool.at[hop * s.n_row + place, part(q)],
                xbase + place * nh + q,
                at(z, xs(dx), y, k),
                "hop",
            )

        sequence = []
        if relayed:
            for q in range(nh):
                sequence.append((3, q))
                if q:
                    sequence.append((2, q - 1))
                sequence.append((1, q))
            sequence.append((2, nh - 1))
            sequence += [(0, q) for q in range(nh)]
        else:
            for q in range(nh):
                sequence += [(dz, q) for dz in order if dz]
                if q:
                    sequence.append((0, q - 1))
            sequence.append((0, nh - 1))
        ready = set()
        with jax.named_scope("send_x"):
            for dz, q in sequence:
                for dx in range(1, nx):
                    if (dz, dx) not in ready:
                        ready.add((dz, dx))
                        rt = zs(dz) * nx + xs(dx)
                        xsend[(dx - 1) * nz + dz] = dot(
                            tile[row_block(rt), :], v_all[hop]
                        ).astype(LOW)
                    send_x(dz, dx, q)
            for dz in order:
                acc[:, dz * own : (dz + 1) * own] = dot(
                    tile[row_block(zs(dz) * nx + x), :], v_all[hop]
                )

        def send_z(dz, q):
            rows_q = span_of(q)
            total = acc[rows_q, dz * own : (dz + 1) * own]
            for dx in range(1, nx):
                place = (dx - 1) * nz + dz
                arrived(pool.at[hop * s.n_row + place, part(q)], xbase + place * nh + q)
                total = total + pool[hop * s.n_row + place, rows_q, :].astype(FULL)
            if not dz:
                return total
            there, slot, mark = zs(dz), dz - 1, zbase + dz * nh + q
            if relayed and dz == 3:
                there = is_inner * zs(3) + (1 - is_inner) * zs(1)
                slot, mark = 3 - is_inner, zbase + 3 * nh * is_inner + q
            if relayed and dz == 2:

                @pl.when(inner)
                def _():
                    arrived(zrecv.at[hop, 3, part(q)], zbase + q)
                    handed = zrecv[hop, 3, rows_q, :].astype(FULL)
                    zsend[dz - 1, rows_q, :] = (total + handed).astype(LOW)

                @pl.when(outer)
                def _():
                    zsend[dz - 1, rows_q, :] = total.astype(LOW)

            else:
                zsend[dz - 1, rows_q, :] = total.astype(LOW)
            send(
                zsend.at[dz - 1, part(q)],
                zrecv.at[hop, slot, part(q)],
                mark,
                at(there, x, y, k),
                "hop",
            )
            return total

        totals = [None] * nh

        def sum_z(q):
            total = totals[q]
            rows_q = span_of(q)
            for dz in range(1, nz):
                there, mark = zrecv.at[hop, dz - 1, part(q)], zbase + dz * nh + q
                if relayed and dz == 3:
                    pl.when(inner)(functools.partial(arrived, there, mark))
                else:
                    arrived(there, mark)
                total = total + zrecv[hop, dz - 1, rows_q, :].astype(FULL)
            finish(q, total)

        with jax.named_scope("send_z"):
            for dz, q in sequence[:-1]:
                totals[q] = send_z(dz, q)
                if not dz:
                    with jax.named_scope("sum_z0"):
                        sum_z(q)
        with jax.named_scope("sum_z1"):
            totals[nh - 1] = send_z(0, nh - 1)
            sum_z(nh - 1)

    bias = [bias_ref[i * width : (i + 1) * width].reshape(1, width) for i in range(2)]
    slopes, acts = [None] * nh, [None] * nh

    def first_done(q, total):
        rows_q = span_of(q)
        z1 = total + v_all[0, row_part(c, q), :].astype(FULL) + bias[0]
        act, slope = gelu_both(z1)
        h1 = act.astype(LOW) * valid_low[rows_q]
        start_gather(1, q, dot(h1, w2).astype(LOW))
        acts[q], slopes[q] = h1, slope * valid_col[rows_q]

    spread(0, first_done)
    h1t = jnp.concatenate(acts, axis=0).astype(FULL).T.astype(LOW)
    slope1t = jnp.concatenate(slopes, axis=0).T

    xt_base = gbase[1] + s.n_col

    def second_done(q, total):
        rows_q = span_of(q)
        z2 = total + v_all[1, row_part(c, q), :].astype(FULL) + bias[1]
        act, slope = gelu_both(z2)
        acts[q] = act.astype(LOW) * valid_low[rows_q]
        slopes[q] = slope * valid_col[rows_q]
        ends = span_of(q).stop
        if ends % (own // 2) == 0:
            lane = 2 * ends // own - 1
            some = [act for i, act in enumerate(acts[: q + 1]) if span_of(i).start >= ends - own // 2]
            some = jnp.concatenate(some, axis=0)
            y3t = dot_nt(w3t[...], some).astype(LOW)
            mine = v3_half(c, lane)
            mine[...] = y3t
            for dy, dk in col_far:
                send(mine, mine, gbase[0] + 2 * c + lane, (r, ys(dy) * nk + ks(dk)))

    def v3_half(index, lane):
        return v3_all.at[index, :, pl.ds(lane * (own // 2), own // 2)]

    spread(1, second_done)
    h2 = jnp.concatenate(acts, axis=0)

    with jax.named_scope("hop3_gather"):
        slope2t = jnp.concatenate(slopes, axis=0).T
        settle(s.n_col - 1)
        for lane in range(2):
            for dy, dk in reversed(col_far):
                source = ys(ny - dy) * nk + ks(nk - dk)
                arrived(v3_half(source, lane), gbase[0] + 2 * source + lane)
    with jax.named_scope("hop3_sum"):
        pbase = wide[0]
        v3 = jnp.concatenate([v3_all[i] for i in range(s.n_col)], axis=1)
        for dz, dx in row_far:
            place = dz * nx + dx
            rt = zs(dz) * nx + xs(dx)
            p3send[place] = dot_nt(v3, tile[row_block(rt), :]).astype(LOW)
            send(p3send.at[place], p3recv.at[place], pbase + place, (rt, c))
        total = dot_nt(v3, tile[row_block(r), :])
        for dz, dx in reversed(row_far):
            place = dz * nx + dx
            arrived(p3recv.at[place], pbase + place)
            total = total + p3recv[place].astype(FULL)
    total = total + v3_all[c].astype(FULL)

    place = lax.broadcasted_iota(jnp.int32, (s.cls, own), 0)
    real = place < s.classes
    on_diag = lax.broadcasted_iota(jnp.int32, (s.cls, s.classes), 0) == lax.broadcasted_iota(
        jnp.int32, (s.cls, s.classes), 1
    )
    bias3 = jnp.sum(
        jnp.where(on_diag, bias_ref[2 * width :].reshape(1, s.classes), 0.0), axis=1, keepdims=True
    )
    logits = jnp.where(real, total + bias3, -1e30)
    shifted = logits - jnp.max(logits, axis=0, keepdims=True)
    weight = jnp.where(real, jnp.exp(shifted), 0.0)
    norm = jnp.sum(weight, axis=0, keepdims=True)
    logp = shifted - jnp.log(norm)
    target = jnp.where(place == lab_ref[...], 1.0 - SMOOTH, 0.0) + SMOOTH / s.classes
    target = jnp.where(real, target, 0.0)
    row_loss = -jnp.sum(jnp.where(real, target * logp, 0.0), axis=0, keepdims=True)
    loss = jnp.sum(row_loss * counted, axis=1, keepdims=True)
    number = jnp.sum(counted, axis=1, keepdims=True)
    dlt = ((weight / norm - target) * counted).astype(LOW)

    with jax.named_scope("back3_gather"):
        base = wide[1]
        mine = dl_all.at[r]
        mine[...] = dlt
        for dz, dx in row_far:
            send(mine, mine, base + r, (zs(dz) * nx + xs(dx), c))
        here = dot(dlt, tile[row_block(r), :])
        for dz, dx in reversed(row_far):
            source = zback(dz) * nx + xs(nx - dx)
            arrived(dl_all.at[source], base + source)
            here = here + dot(dl_all[source], tile[row_block(source), :])
        acc[: s.cls, :cols] = here
    with jax.named_scope("back3_sum"):
        qbase = gbase[1]
        for dy, dk in col_far:
            place = dy * nk + dk
            ct = ys(dy) * nk + ks(dk)
            q3send[place] = acc[: s.cls, row_block(ct)].astype(LOW)
            send(q3send.at[place], q3recv.at[place], qbase + place, (r, ct))
        total = dlt.astype(FULL) + acc[: s.cls, row_block(c)]
        for dy, dk in reversed(col_far):
            place = dy * nk + dk
            arrived(q3recv.at[place], qbase + place)
            total = total + q3recv[place].astype(FULL)
    qt = total.astype(LOW)
    dh2t = lax.dot_general(
        w3t[...], qt, (((0,), (0,)), ((), ())), preferred_element_type=FULL
    )
    step_cols = min(cols, 1024)

    def gained(values, block, fresh=False):
        for j in range(0, cols, step_cols):
            here = dot(values, tile[block, j : j + step_cols])
            if fresh:
                acc[:, j : j + step_cols] = here
            else:
                acc[:, j : j + step_cols] += here

    def halves(lane, row):
        return (
            pl.ds(row * (width // 2), width // 2),
            pl.ds(lane * (own // 2), own // 2),
        )

    quarters = [(lane, row) for lane in range(2) for row in range(2)]
    def receive(hop, values, meanwhile=None, late=None):
        base, np = wide[hop], len(quarters)
        first = hop * s.n_row

        def piece(dz, dx, q):
            return pool.at[(first + dx * nz + dz, *halves(*quarters[q]))]

        def to_z(dz, q, when=None, start=True):
            return send(
                piece(0, 0, q),
                piece(dz, 0, q),
                base + dz * np + q,
                at(zs(dz), x, y, k),
                when=when,
                start=start,
            )

        def to_x(dz, q, start=True):
            return [
                send(
                    piece(dz, 0, q),
                    piece(dz, dx, q),
                    base + (dx * nz + dz) * np + q,
                    at(z, xs(dx), y, k),
                    start=start,
                )
                for dx in range(1, nx)
            ]

        own_parts = []
        for lane in range(2):
            mine = values(lane)
            own_parts.append(mine)
            pool[first, :, lane * (own // 2) : (lane + 1) * (own // 2)] = mine
            for q in (2 * lane, 2 * lane + 1):
                if relayed:
                    to_z(2, q)
                    to_z(1, q)
                else:
                    for dz in range(nz - 1, 0, -1):
                        to_z(dz, q)
                to_x(0, q)

        def source(dz, dx):
            return row_block(zback(dz) * nx + xs(nx - dx))

        gained(jnp.concatenate(own_parts, axis=1), row_block(r), fresh=True)
        if meanwhile is not None:
            meanwhile()

        passing = {
            (dz, q): to_x(dz, q, start=False) for q in range(np) for dz in range(1, nz)
        }

        def step(dz, q):
            arrived(piece(dz, 0, q), base + dz * np + q)
            for copy in passing[dz, q]:
                copy.start()

        if relayed:
            relays = [
                send(
                    piece(2, 0, q),
                    piece(3, 0, q),
                    base + 3 * np + q,
                    at(zs(1), x, y, k),
                    when=inner,
                    start=False,
                )
                for q in range(np)
            ]
            paced = [to_z(3, q, inner, start=False) for q in range(np)]

            @pl.when(inner)
            def _():
                for q in range(np):
                    arrived(piece(2, 0, q), base + 2 * np + q)
                    relays[q].start()
                    paced[q].start()
                    for copy in passing[2, q]:
                        copy.start()
                    step(1, q)
                    if q > 1:
                        step(3, q - 2)
                for q in range(np - 2, np):
                    step(3, q)

            @pl.when(outer)
            def _():
                for q in range(np + 2):
                    if q < np:
                        step(1, q)
                    if 0 < q <= np:
                        step(2, q - 1)
                    if q > 2:
                        step(3, q - 3)
                for q in range(np - 1, np):
                    step(3, q)
        else:
            for q in range(np):
                for dz in range(1, nz):
                    step(dz, q)
        for dz in range(1, nz):
            gained(pool[first + dz], source(dz, 0))
        if late is not None:
            late()
        for dz in range(nz):
            for dx in range(1, nx):
                for q in range(np):
                    arrived(piece(dz, dx, q), base + (dx * nz + dz) * np + q)
                gained(pool[first + dx * nz + dz], source(dz, dx))

    dz2t = (dh2t * slope2t).astype(LOW)
    half_own = own // 2

    def features_out():
        for d in range(1, ny):
            send(own_xt, own_xt, xt_base + c, at(z, x, ys(d), k))
        if nk > 1:
            send(own_xt, own_xt, xt_base + c, sibling)

    with jax.named_scope("back2_rows"):
        settle()
        receive(0, lambda lane: dz2t[:, lane * half_own : (lane + 1) * half_own], features_out)
    cbase = gbase[0] + 2 * s.n_col
    ybase = gbase[1] + 2 * s.n_col

    def lane_part(index, lane):
        return pl.ds(pl.multiple_of(index * own + lane * half_own, half_own), half_own)

    def held(place, lane):
        return xsend.at[place, :, pl.ds(lane * half_own, half_own)]

    def crecv(dy, lane):
        return v_all.at[0, dy * own : (dy + 1) * own, pl.ds(lane * half_own, half_own)]

    def yrecv(dy, lane):
        return crecv(dy + (ny if nk > 1 else 0), lane)

    column_totals = [None, None]
    with jax.named_scope("back2_cols"):
        for lane in range(2):
            for dy in range(ny - 1, -1, -1):
                if nk > 1:
                    there = held(dy, lane)
                    there[...] = acc[:, lane_part(ys(dy) * nk + 1 - k, lane)].astype(LOW)
                    send(there, crecv(dy, lane), cbase + 2 * dy + lane, sibling)
        for lane in range(2):
            for dy in range(ny - 1, -1, -1):
                here = acc[:, lane_part(ys(dy) * nk + k, lane)]
                if nk > 1:
                    arrived(crecv(dy, lane), cbase + 2 * dy + lane)
                    here = here + crecv(dy, lane)[...].astype(FULL)
                if dy:
                    there = held(ny + dy, lane)
                    there[...] = here.astype(LOW)
                    send(
                        there, yrecv(dy, lane), ybase + 2 * dy + lane, at(z, x, ys(dy), k)
                    )
                else:
                    column_totals[lane] = here
        for d in range(1, ny):
            source = ys(ny - d) * nk + k
            arrived(xt_all.at[source], xt_base + source)
            if nk > 1:
                send(xt_all.at[source], xt_all.at[source], xt_base + source, sibling)

    dy2_parts, dz1_parts = [], []

    def first_slopes(lane):
        lanes_q = slice(lane * half_own, (lane + 1) * half_own)
        total = column_totals[lane] + dz2t[:, lanes_q].astype(FULL)
        with jax.named_scope("y_wait"):
            for dy in range(1, ny):
                arrived(yrecv(dy, lane), ybase + 2 * dy + lane)
                total = total + yrecv(dy, lane)[...].astype(FULL)
        dy2_parts.append(total.astype(LOW))
        dz1_parts.append((dot(w2, dy2_parts[lane]) * slope1t[:, lanes_q]).astype(LOW))
        return dz1_parts[lane]

    lanes, plane = s.lanes, s.plane
    me = y * nx + x
    others = [(dx, dy) for dx in range(nx) for dy in range(ny) if dx or dy]

    def lane_block(index):
        return pl.ds(pl.multiple_of(index * lanes, lanes), lanes)

    class Total:
        def __init__(self, start, rows):
            self.all = pl.ds(start, rows)
            self.start, self.rows = start, rows
            self.n = rows // plane
            self.short = pl.ds(start // plane, self.n)
            self.base = rslots(1 + 3 * plane + nz)

        def piece(self, index):
            return pl.ds(pl.multiple_of(self.start + index * self.n, 16), self.n)

        def core_send(self, other):
            if nk > 1:
                half_send[self.all, :] = other.astype(LOW)
                send(half_send.at[self.all], half_recv.at[self.all], self.base, sibling)

        def plane_send(self, mine):
            if nk > 1:
                arrived(half_recv.at[self.all], self.base)
                mine = mine + half_recv[self.all, :].astype(FULL)
            half[self.all, :] = mine.astype(LOW)
            base = self.base + 1
            for dx, dy in others:
                there = ys(dy) * nx + xs(dx)
                send(
                    half.at[self.piece(there)],
                    plane_recv.at[me, self.short],
                    base + me,
                    at(z, xs(dx), ys(dy), k),
                )
            plane_recv[me, self.short, :] = half[self.piece(me), :]

        def line_send(self):
            base = self.base + 1
            for dx, dy in others:
                there = ys(dy) * nx + xs(dx)
                arrived(plane_recv.at[there, self.short], base + there)
            total = plane_recv[0, self.short, :].astype(FULL)
            for i in range(1, plane):
                total = total + plane_recv[i, self.short, :].astype(FULL)
            quarter[z, self.short, :] = total.astype(LOW)
            mine = quarter.at[z, self.short]
            base = self.base + 1 + plane
            for dz in range(nz - 1, 0, -1):
                send(mine, mine, base + z, at(zs(dz), x, y, k))

        def back_send(self):
            base = self.base + 1 + plane
            for dz in range(1, nz):
                arrived(quarter.at[zback(dz), self.short], base + zback(dz))
            total = quarter[0, self.short, :].astype(FULL)
            for i in range(1, nz):
                total = total + quarter[i, self.short, :].astype(FULL)
            base = self.base + 1 + plane + nz
            mine = fin.at[k, self.piece(me)]
            mine[...] = total.astype(LOW)
            for dx, dy in others:
                send(mine, mine, base + me, at(z, xs(dx), ys(dy), k))
            if nk > 1:
                send(mine, mine, base + plane + me, sibling)

        def back_forward(self):
            base = self.base + 1 + plane + nz
            for dx, dy in others:
                there = ys(dy) * nx + xs(dx)
                block = fin.at[k, self.piece(there)]
                arrived(block, base + there)
                if nk > 1:
                    send(block, block, base + plane + there, sibling)

        def end(self):
            base = self.base + 1 + plane + nz
            if nk > 1:
                for i in range(plane):
                    arrived(fin.at[1 - k, self.piece(i)], base + plane + i)

    def write(start, count):
        grad_ref[:, start : start + count, :] = fin[:, start : start + count, :]

    one_a = Total(0, s.cut_rows)
    one_b = Total(s.cut_rows, s.one_rows - s.cut_rows)
    two = Total(s.one_rows, s.two_rows)
    tail = s.two_rows - width - s.cls

    ones = jnp.ones((8, own), LOW)
    row = lax.broadcasted_iota(jnp.int32, (8, width), 0)
    lane_of = lax.broadcasted_iota(jnp.int32, (8, width), 1)
    bias_three = jnp.concatenate([dlt, jnp.zeros((width - s.cls, own), LOW)], axis=0)
    misc = jnp.where(row == 1, dot_nt(ones, dz2t), 0.0)
    misc = jnp.where(row == 2, dot_nt(ones, bias_three), misc)
    misc = jnp.where((row == 3) & (lane_of == 0), loss, misc)
    misc = jnp.where((row == 3) & (lane_of == 1), number, misc)
    mbase = rslots(1 + plane + nz)
    plane_base, line_base = mbase + 1, mbase + 1 + plane

    def early():
        misc_k[0] = misc
        if nk > 1:
            send(misc_k.at[0], misc_k.at[1], mbase, sibling)
        grad3t = dot(qt, h2)
        dy2t = jnp.concatenate(dy2_parts, axis=1)
        grad2 = dot_nt(h1t, dy2t)
        acc_two = jnp.concatenate(
            [grad2, grad3t] + ([jnp.zeros((tail, width), FULL)] if tail else []), axis=0
        )
        if nk > 1:
            first, second = acc_two[:, :lanes], acc_two[:, lanes:]
            low_core = (k == 0).astype(FULL)
            two.core_send(second * low_core + first * (1.0 - low_core))
            two.plane_send(first * low_core + second * (1.0 - low_core))
        else:
            two.plane_send(acc_two)
        here = misc_k[0]
        if nk > 1:
            arrived(misc_k.at[1], mbase)
            here = here + misc_k[1]
        misc_p[me] = here
        for dx, dy in others:
            send(misc_p.at[me], misc_p.at[me], plane_base + me, at(z, xs(dx), ys(dy), k))

    def late():
        two.line_send()
        for dx, dy in others:
            there = ys(dy) * nx + xs(dx)
            arrived(misc_p.at[there], plane_base + there)
        here = misc_p[0]
        for i in range(1, plane):
            here = here + misc_p[i]
        misc_z[z] = here
        for dz in range(1, nz):
            send(misc_z.at[z], misc_z.at[z], line_base + z, at(zs(dz), x, y, k))

    with jax.named_scope("back1_rows"):
        receive(1, first_slopes, early, late)
    with jax.named_scope("grad1"):
        dz1t = jnp.concatenate(dz1_parts, axis=1)
        acc[:, row_block(c)] += dz1t.astype(FULL)
        if nk > 1:
            for d in range(ny):
                source = ys(d) * nk + 1 - k
                arrived(xt_all.at[source], xt_base + source)

        low_core = (k == 0).astype(FULL)
        bias_one = dot_nt(ones, dz1t)[0:1, :]

        def grad_one(start, stop):
            total = None
            end = min(stop, s.feat_up)
            for i in range(s.n_col):
                here = acc[:, i * own : (i + 1) * own].astype(LOW)
                here = dot_nt(xt_all[i, start:end, :], here)
                total = here if total is None else total + here
            if end < stop:
                total = jnp.concatenate([total, jnp.zeros((stop - end, width), FULL)], axis=0)
            bias_at = s.feat - start
            if 0 <= bias_at < stop - start:
                places = lax.broadcasted_iota(jnp.int32, (stop - start, width), 0)
                total = jnp.where(places == bias_at, bias_one, total)
            if nk == 1:
                return None, total
            first, second = total[:, :lanes], total[:, lanes:]
            return (
                second * low_core + first * (1.0 - low_core),
                first * low_core + second * (1.0 - low_core),
            )

        other, mine_a = grad_one(0, s.cut_rows)
        one_a.core_send(other)
        other, mine_b = grad_one(s.cut_rows, s.one_rows)
        one_b.core_send(other)
        one_a.plane_send(mine_a)
        one_b.plane_send(mine_b)

    with jax.named_scope("sum_plane"):
        left = len(pending)
        two.back_send()
    with jax.named_scope("sum_line"):
        one_a.line_send()
        one_b.line_send()
    with jax.named_scope("back_line"):
        one_a.back_send()
        one_b.back_send()
        for dz in range(1, nz):
            arrived(misc_z.at[zback(dz)], line_base + zback(dz))
        misc = misc_z[0]
        for i in range(1, nz):
            misc = misc + misc_z[i]
        misc_ref[...] = jnp.where(row == 4, 1.0 / misc[3:4, 1:2], misc)
        settle(len(pending) - left)
    with jax.named_scope("back_plane"):
        one_a.back_forward()
        one_b.back_forward()
        two.back_forward()
        one_a.end()
        write(0, s.cut_rows)
        one_b.end()
        write(s.cut_rows, s.one_rows - s.cut_rows)
        two.end()
        write(s.one_rows, s.two_rows)
    with jax.named_scope("settle"):
        settle()
    assert rcount[0] <= s.arrivals


def update_pieces(s):
    some = up(s.feat // 4, 16)
    cuts = [min(i * some, s.feat) for i in range(5)]
    one = [(0, start, stop - start) for start, stop in zip(cuts, cuts[1:]) if stop > start]
    return (*one, (1, 0, s.width), (2, 0, s.classes))


def adam_kernel(s, grad_ref, misc_ref, *refs):
    ins, outs, scratch = refs[:12], refs[12:26], refs[26:]
    bias_out, ends, *held = scratch[:-1]
    sem_out = scratch[-1]
    width, classes, lanes = s.width, s.classes, s.lanes
    grad_at = (0, s.one_rows, s.one_rows + width)

    stores = []

    def store(source, target):
        copy = pltpu.make_async_copy(source, target, sem_out.at[len(stores)])
        copy.start()
        stores.append(copy)

    total = misc_ref[3:4, 1:2]
    scale = misc_ref[4:5, 0:1]
    for (which, start, rows), target in zip(update_pieces(s), held):
        span = slice(start, start + rows)
        for i in range(s.nk):
            lane = slice(i * lanes, (i + 1) * lanes)
            first = grad_at[which] + start
            grad = grad_ref[i, first : first + up(rows, 16), :].astype(FULL)[:rows]
            weight, one, two = (ins[3 * which + j][span, lane] for j in range(3))
            for j, new in enumerate(adam_update(weight, one, two, grad * scale)):
                target[j, :, lane] = new
        for j in range(3):
            store(target.at[j], outs[3 * which + j].at[pl.ds(start, rows)])
    for i, size in enumerate((width, width, classes)):
        span = slice(i * width, i * width + size)
        weight, first, second = (ins[9 + j][span] for j in range(3))
        grad = misc_ref[i, :size]
        if not i:
            top = s.feat // 16 * 16
            rows = [grad_ref[j, top : top + 16, :].astype(FULL) for j in range(s.nk)]
            grad = jnp.concatenate([a[s.feat - top] for a in rows])
        new = adam_update(weight, first, second, grad * misc_ref[4, :size])
        for j in range(3):
            bias_out[j][span] = new[j]
    for j in range(3):
        store(bias_out[j], outs[9 + j])
    ends[0] = misc_ref[3:4, 0:1]
    ends[1] = total
    for i in range(2):
        store(ends.at[i], outs[12 + i])
    for copy in stores:
        copy.wait()


def shards(
    sizes,
    features,
    adjacency,
    occupancy,
    labels,
    train_mask,
    node_count,
    weight_one,
    weight_two,
    weight_three,
    biases,
    first_one,
    first_two,
    first_three,
    first_bias,
    second_one,
    second_two,
    second_three,
    second_bias,
):
    own, feat = features.shape
    width = weight_two.shape[0]
    classes = weight_three.shape[1]
    s = sizes(own, feat, width, classes)
    rows, cols = adjacency.shape
    lanes = s.lanes
    vmem = pl.BlockSpec(memory_space=pltpu.VMEM)
    smem = pl.BlockSpec(memory_space=pltpu.SMEM)
    anywhere = pl.BlockSpec(memory_space=pl.ANY)
    block = (own, width)
    small = (s.cls, own)
    shapes = [
        ((rows, cols), LOW),
        ((s.feat_up, width), LOW),
        ((s.cls, width), LOW),
        ((s.n_col, s.feat_up, own), LOW),
        ((2, s.n_col * own, width), LOW),
        ((2 * s.n_row, *block), LOW),
        ((max(2 * s.ny, s.n_row - s.nz), *block), LOW),
        ((max(1, s.nz - 1), *block), LOW),
        ((2, s.nz if s.relayed else max(1, s.nz - 1), *block), LOW),
        ((s.n_col, *small), LOW),
        ((s.n_row, *small), LOW),
        ((s.n_row, *small), LOW),
        ((s.n_row, *small), LOW),
        ((s.n_col, *small), LOW),
        ((s.n_col, *small), LOW),
        ((width, max(cols, s.nz * own)), FULL),
        ((s.grad_rows, lanes), LOW),
        ((s.grad_rows, lanes), LOW),
        ((s.grad_rows, lanes), LOW),
        ((s.plane, s.grad_rows // s.plane, lanes), LOW),
        ((s.nz, s.grad_rows // s.plane, lanes), LOW),
        ((s.nk, s.grad_rows, lanes), LOW),
        ((2, 8, width), FULL),
        ((s.plane, 8, width), FULL),
        ((s.nz, 8, width), FULL),
    ]
    bytes_held = sum(math.prod(shape) * jnp.dtype(kind).itemsize for shape, kind in shapes)
    limit = min(62, 16 + bytes_held // 2**20) * 2**20
    grads, misc = pl.pallas_call(
        functools.partial(kernel, s),
        out_shape=(
            pltpu.VMEM((s.nk, s.grad_rows, lanes), LOW),
            pltpu.VMEM((8, width), FULL),
        ),
        in_specs=[
            vmem,
            anywhere,
            smem,
            vmem,
            vmem,
            smem,
            vmem,
            vmem,
            vmem,
            vmem,
        ],
        out_specs=(vmem, vmem),
        scratch_shapes=[
            *[pltpu.VMEM(shape, kind) for shape, kind in shapes],
            pltpu.SemaphoreType.DMA((s.sends,)),
            pltpu.SemaphoreType.DMA((s.arrivals,)),
            pltpu.SemaphoreType.DMA((rows // SUB,)),
        ],
        compiler_params=pltpu.CompilerParams(
            collective_id=0, has_side_effects=True, vmem_limit_bytes=limit
        ),
        cost_estimate=pl.CostEstimate(
            flops=12 * rows * cols * width, bytes_accessed=2 * rows * cols, transcendentals=0
        ),
        name="step",
    )(
        *[
            pltpu.with_memory_space_constraint(a, pltpu.HBM)
            for a in (features.T, adjacency)
        ],
        pltpu.with_memory_space_constraint(occupancy, pltpu.HBM),
        *[
            pltpu.with_memory_space_constraint(a, pltpu.HBM)
            for a in (labels.reshape(1, own), train_mask.reshape(1, own))
        ],
        node_count,
        *[
            pltpu.with_memory_space_constraint(a, pltpu.HBM)
            for a in (weight_one, weight_two, weight_three.T, biases)
        ],
    )
    state = (
        weight_one,
        first_one,
        second_one,
        weight_two,
        first_two,
        second_two,
        weight_three.T,
        first_three.T,
        second_three.T,
        biases,
        first_bias,
        second_bias,
    )
    new = pl.pallas_call(
        functools.partial(adam_kernel, s),
        out_shape=(
            *[jax.ShapeDtypeStruct(a.shape, FULL) for a in state],
            jax.ShapeDtypeStruct((1, 1), FULL),
            jax.ShapeDtypeStruct((1, 1), FULL),
        ),
        in_specs=[vmem] * 14,
        out_specs=(anywhere,) * 14,
        scratch_shapes=[
            [pltpu.VMEM(biases.shape, FULL)] * 3,
            pltpu.VMEM((2, 1, 1), FULL),
            *[pltpu.VMEM((3, rows, width), FULL) for _, _, rows in update_pieces(s)],
            pltpu.SemaphoreType.DMA((3 * len(update_pieces(s)) + 5,)),
        ],
        compiler_params=pltpu.CompilerParams(vmem_limit_bytes=32 * 2**20),
        name="update",
    )(grads, misc, *state)
    return (
        *new[:6],
        *[a.T for a in new[6:9]],
        *new[9:12],
        new[12].reshape(()),
        new[13].reshape(()),
    )


def solution(mesh):
    placed = (
        P(("row", "col"), None),
        P("col", "row"),
        P("col", "row"),
        P(("row", "col")),
        P(("row", "col")),
        P(("row", "col")),
        *[P()] * 12,
    )
    sizes = functools.partial(Sizes, mesh.shape["row"], mesh.shape["col"])
    return jax.shard_map(
        functools.partial(shards, sizes),
        mesh=mesh,
        in_specs=placed,
        out_specs=(P(),) * 14,
        check_vma=False,
    )
```

```python
import functools
import math

import jax
import jax.numpy as jnp
from jax import lax
from jax.experimental import pallas as pl
from jax.experimental.pallas import tpu as pltpu
from jax.sharding import PartitionSpec as P

SUB = 512
STEP = 5


B_ONE = 0.5
B_TWO = 0.5
RATE = 0.05
DECAY = 0.01
EPSILON = 1e-08
SMOOTH = 0.1

MESH = pl.DeviceIdType.MESH
LOW = jnp.bfloat16
FULL = jnp.float32
GELU_A = 0.7978845608028654
GELU_B = 0.044715


def adam_update(weight, first, second, grad):
    first_new = B_ONE * first + (1.0 - B_ONE) * grad
    second_new = B_TWO * second + (1.0 - B_TWO) * grad * grad
    fix_one = 1.0 - B_ONE**STEP
    fix_two = 1.0 - B_TWO**STEP
    scaled = (first_new * (1.0 / fix_one)) / (jnp.sqrt(second_new * (1.0 / fix_two)) + EPSILON)
    return (first_new, second_new, weight - RATE * (scaled + DECAY * weight))


def up(value, unit):
    return -(-value // unit) * unit


def dot(left, right):
    return jnp.dot(left, right, preferred_element_type=FULL)


def dot_nt(left, right):
    return lax.dot_general(left, right, (((1,), (1,)), ((), ())), preferred_element_type=FULL)


def gelu_both(z):
    t = jnp.tanh(GELU_A * (z + GELU_B * z * z * z))
    half = 0.5 * (1.0 + t)
    slope = half + 0.5 * z * (1.0 - t * t) * (GELU_A * (1.0 + 3.0 * GELU_B * z * z))
    return z * half, slope


class Sizes:
    def __init__(self, n_row, n_col, own, feat, width, classes):
        self.n_row, self.n_col = n_row, n_col
        self.nk = 2 if n_col % 2 == 0 else 1
        self.ny = n_col // self.nk
        self.nx = self.ny if n_row % self.ny == 0 else 1
        self.nz = n_row // self.nx
        self.own, self.feat, self.width, self.classes = own, feat, width, classes
        self.feat_up = up(feat, 128)
        self.cls = up(classes, 16)
        self.plane = self.nx * self.ny
        self.one_rows = up(feat + 1, 16 * self.plane)
        self.two_rows = up(width + self.cls, 16 * self.plane)
        self.grad_rows = self.one_rows + self.two_rows
        self.lanes = width // self.nk
        units = self.one_rows // (16 * self.plane)
        chunks = min(3, units)
        cuts = [units * i // chunks * 16 * self.plane for i in range(chunks + 1)]
        self.chunks = list(zip(cuts, cuts[1:]))
        cuts = [own // 4 * i for i in range(5)]
        self.parts = [(start, stop - start) for start, stop in zip(cuts, cuts[1:])]
        self.nh = len(self.parts)
        self.relayed = self.nz == 4
        self.sends = 3 * (n_row + n_col) + 3 * self.plane
        wide = 2 * self.nh * (n_row + n_col)
        self.arrivals = wide + max(1, chunks - 1) * (1 + 3 * self.plane + self.nz) + 1 + self.plane + self.nz


def kernel(
    s,
    xt_ref,
    adj_ref,
    occ_ref,
    lab_ref,
    mask_ref,
    cnt_ref,
    w1_ref,
    w2_ref,
    w3t_ref,
    bias_ref,
    grad_ref,
    misc_ref,
    tile,
    w1b,
    w3t,
    xt_all,
    v_all,
    pool,
    xsend,
    zsend,
    zrecv,
    v3_all,
    p3send,
    p3recv,
    dl_all,
    q3send,
    q3recv,
    acc,
    half_send,
    half_recv,
    half,
    plane_recv,
    quarter,
    fin,
    misc_k,
    misc_p,
    misc_z,
    ssem,
    rsem,
    lsem,
):
    nx, ny, nz, nk = s.nx, s.ny, s.nz, s.nk
    own, width = s.own, s.width
    r, c = lax.axis_index("row"), lax.axis_index("col")
    z, x = r // nx, r % nx
    y, k = c // nk, c % nk

    def at(zz, xx, yy, kk):
        return (zz * nx + xx, yy * nk + kk)

    def xs(d):
        return lax.rem(x + d, nx)

    def ys(d):
        return lax.rem(y + d, ny)

    def zs(d):
        if nz & (nz - 1):
            return lax.rem(z + d, nz)
        there, bit = z, 1
        while bit < nz:
            if d & bit:
                there = there + bit - 2 * bit * lax.rem(there // bit, 2)
            bit *= 2
        return there

    def zback(d):
        return zs(d) if not nz & (nz - 1) else lax.rem(z + nz - d, nz)

    sibling = at(z, x, y, 1 - k)
    relayed = s.relayed
    is_inner = lax.rem((z + 1) // 2, 2)
    inner = is_inner == 1
    outer = is_inner == 0
    line = [dz for dz in range(nz - 1, -1, -1)]
    row_far = [(dz, dx) for dz in line for dx in range(nx - 1, -1, -1) if dz or dx]
    col_far = [(dy, dk) for dy in range(ny - 1, -1, -1) for dk in range(nk - 1, -1, -1) if dy or dk]

    def ks(d):
        return lax.rem(k + d, nk)


    rows, cols = tile.shape
    n_sub = rows // SUB
    loads = [
        pltpu.make_async_copy(
            adj_ref.at[pl.ds(a * SUB, SUB)], tile.at[pl.ds(a * SUB, SUB)], lsem.at[a]
        )
        for a in range(n_sub)
    ]
    for load in loads:
        load.start()

    peers = []
    for d in range(1, s.n_row):
        peers.append((lax.rem(r + d, s.n_row), c))
    for d in range(1, s.n_col):
        peers.append((r, lax.rem(c + d, s.n_col)))
    for dx in range(1, nx):
        for dy in range(1, ny):
            peers.append(at(z, xs(dx), ys(dy), k))
    barrier = pltpu.get_barrier_semaphore()
    for peer in peers:
        pl.semaphore_signal(barrier, inc=1, device_id=peer, device_id_type=MESH)

    free = list(range(s.sends))
    pending = []

    def send(src, dst, recv_slot, device, of=None, when=None, start=True):
        if not free:
            settle(len(pending) - 1)
        copy = pltpu.make_async_remote_copy(
            src_ref=src,
            dst_ref=dst,
            send_sem=ssem.at[free[0]],
            recv_sem=rsem.at[recv_slot],
            device_id=device,
            device_id_type=MESH,
        )
        if start:
            if when is None:
                copy.start()
            else:
                pl.when(when)(copy.start)
        pending.append((copy, free.pop(0), of, when))
        return copy

    def arrived(dst, recv_slot):
        pltpu.make_async_remote_copy(
            src_ref=dst,
            dst_ref=dst,
            send_sem=ssem.at[0],
            recv_sem=rsem.at[recv_slot],
            device_id=sibling,
            device_id_type=MESH,
        ).wait_recv()

    def settle(keep=0, of=None):
        done = [p for p in pending if p[2] == of] if of else pending[: len(pending) - keep]
        for item in done:
            if item[3] is None:
                item[0].wait_send()
            else:
                pl.when(item[3])(item[0].wait_send)
            free.append(item[1])
        left = [p for p in pending if all(p is not q for q in done)]
        pending[:] = left

    rcount = [0]

    def rslots(n):
        rcount[0] += n
        return rcount[0] - n

    def row_block(index):
        return pl.ds(pl.multiple_of(index * own, own), own)

    nh = s.nh

    def row_part(index, q):
        start, count = s.parts[q]
        return pl.ds(pl.multiple_of(index * own + start, count), count)

    def part(q):
        return pl.ds(*s.parts[q])

    def span_of(q):
        start, count = s.parts[q]
        return slice(start, start + count)

    valid_col = (lax.broadcasted_iota(jnp.int32, (own, width), 0) < cnt_ref[0]).astype(FULL)
    valid_low = valid_col.astype(LOW)
    valid_row = (lax.broadcasted_iota(jnp.int32, (1, own), 1) < cnt_ref[0]).astype(FULL)
    counted = mask_ref[...].astype(FULL) * valid_row

    prologue = jax.named_scope("prologue")
    prologue.__enter__()
    pad = s.feat_up - up(s.feat, 16) + 16
    own_xt = xt_all.at[c]
    own_xt[s.feat_up - pad :, :] = jnp.zeros((pad, own), LOW)
    w1b[s.feat_up - pad :, :] = jnp.zeros((pad, width), LOW)
    x_valid = (lax.broadcasted_iota(jnp.int32, (s.feat, own), 1) < cnt_ref[0]).astype(LOW)
    own_xt[: s.feat, :] = xt_ref[...] * x_valid
    w1b[: s.feat, :] = w1_ref[...].astype(LOW)
    y1 = lax.dot_general(
        own_xt[...], w1b[...], (((0,), (0,)), ((), ())), preferred_element_type=FULL
    ).astype(LOW)
    v_all[0, row_block(c), :] = y1

    wide = [rslots(s.n_row * nh) for _ in range(2)]
    gbase = [rslots(s.n_col * nh) for _ in range(2)]
    prologue.__exit__(None, None, None)

    def start_gather(hop, q, values):
        mine = v_all.at[hop, row_part(c, q)]
        if values is not None:
            mine[...] = values
        for d in range(1, ny):
            send(mine, mine, gbase[hop] + c * nh + q, at(z, x, ys(d), k))
        if nk > 1:
            send(mine, mine, gbase[hop] + c * nh + q, sibling)

    def complete_gather(hop):
        for q in range(nh):
            for d in range(1, ny):
                source = ys(ny - d) * nk + k
                block = v_all.at[hop, row_part(source, q)]
                arrived(block, gbase[hop] + source * nh + q)
                if nk > 1:
                    send(block, block, gbase[hop] + source * nh + q, sibling)
        if nk > 1:
            for q in range(nh):
                for d in range(ny):
                    source = ys(d) * nk + 1 - k
                    arrived(
                        v_all.at[hop, row_part(source, q)], gbase[hop] + source * nh + q
                    )

    with jax.named_scope("barrier"):
        pl.semaphore_wait(barrier, len(peers))
    for q in range(nh):
        start_gather(0, q, None)

    if relayed:

        @pl.when(outer)
        def _():
            zrecv[:, 2] = jnp.zeros((2, own, width), LOW)

    w3t[...] = jnp.zeros_like(w3t)
    w3t[: s.classes, :] = w3t_ref[...].astype(LOW)
    w2 = w2_ref[...].astype(LOW)
    for a in range(n_sub):
        loads[a].wait()
        for b in range(cols // own):
            piece = tile[pl.ds(a * SUB, SUB), pl.ds(b * own, own)]
            cover = jnp.full((SUB, own), occ_ref[a, b].astype(FULL), FULL).astype(LOW)
            tile[pl.ds(a * SUB, SUB), pl.ds(b * own, own)] = piece * cover

    def spread(hop, finish):
        settle(of="hop")
        with jax.named_scope("gather_y"):
            complete_gather(hop)
        zbase = wide[hop]
        xbase = zbase + nz * nh
        order = list(range(nz - 1, -1, -1))

        def send_x(dz, dx, q):
            place = (dx - 1) * nz + dz
            send(
                xsend.at[place, part(q)],
                pool.at[hop * s.n_row + place, part(q)],
                xbase + place * nh + q,
                at(z, xs(dx), y, k),
                "hop",
            )

        sequence = []
        if relayed:
            sequence = [(3, 0), (3, 1), (2, 0), (3, 2), (2, 1), (3, 3), (1, 0), (2, 2), (1, 1), (2, 3), (1, 2), (1, 3), (0, 0), (0, 1), (0, 2), (0, 3)]
        else:
            for q in range(nh):
                sequence += [(dz, q) for dz in order if dz]
                if q:
                    sequence.append((0, q - 1))
            sequence.append((0, nh - 1))
        ready = set()
        with jax.named_scope("send_x"):
            for dz, q in sequence:
                for dx in range(1, nx):
                    if (dz, dx) not in ready:
                        ready.add((dz, dx))
                        rt = zs(dz) * nx + xs(dx)
                        xsend[(dx - 1) * nz + dz] = dot(
                            tile[row_block(rt), :], v_all[hop]
                        ).astype(LOW)
                    send_x(dz, dx, q)
            for dz in order:
                acc[:, dz * own : (dz + 1) * own] = dot(
                    tile[row_block(zs(dz) * nx + x), :], v_all[hop]
                )

        def send_z(dz, q):
            rows_q = span_of(q)
            total = acc[rows_q, dz * own : (dz + 1) * own]
            for dx in range(1, nx):
                place = (dx - 1) * nz + dz
                arrived(pool.at[hop * s.n_row + place, part(q)], xbase + place * nh + q)
                total = total + pool[hop * s.n_row + place, rows_q, :].astype(FULL)
            if not dz:
                return total
            there, slot, mark = zs(dz), dz - 1, zbase + dz * nh + q
            if relayed and dz == 3:
                there = is_inner * zs(3) + (1 - is_inner) * zs(1)
                slot, mark = 3 - is_inner, zbase + 3 * nh * is_inner + q
            if relayed and dz == 2:

                @pl.when(inner)
                def _():
                    arrived(zrecv.at[hop, 3, part(q)], zbase + q)
                    handed = zrecv[hop, 3, rows_q, :].astype(FULL)
                    zsend[dz - 1, rows_q, :] = (total + handed).astype(LOW)

                @pl.when(outer)
                def _():
                    zsend[dz - 1, rows_q, :] = total.astype(LOW)

            else:
                zsend[dz - 1, rows_q, :] = total.astype(LOW)
            send(
                zsend.at[dz - 1, part(q)],
                zrecv.at[hop, slot, part(q)],
                mark,
                at(there, x, y, k),
                "hop",
            )
            return total

        totals = [None] * nh

        def sum_z(q):
            total = totals[q]
            rows_q = span_of(q)
            for dz in range(1, nz):
                there, mark = zrecv.at[hop, dz - 1, part(q)], zbase + dz * nh + q
                if relayed and dz == 3:
                    pl.when(inner)(functools.partial(arrived, there, mark))
                else:
                    arrived(there, mark)
                total = total + zrecv[hop, dz - 1, rows_q, :].astype(FULL)
            finish(q, total)

        with jax.named_scope("send_z"):
            for dz, q in sequence[:-1]:
                totals[q] = send_z(dz, q)
                if not dz:
                    with jax.named_scope("sum_z0"):
                        sum_z(q)
        with jax.named_scope("sum_z1"):
            totals[nh - 1] = send_z(0, nh - 1)
            sum_z(nh - 1)

    bias = [bias_ref[i * width : (i + 1) * width].reshape(1, width) for i in range(2)]
    slopes, acts = [None] * nh, [None] * nh

    def first_done(q, total):
        rows_q = span_of(q)
        z1 = total + v_all[0, row_part(c, q), :].astype(FULL) + bias[0]
        act, slope = gelu_both(z1)
        h1 = act.astype(LOW) * valid_low[rows_q]
        start_gather(1, q, dot(h1, w2).astype(LOW))
        acts[q], slopes[q] = h1, slope * valid_col[rows_q]

    spread(0, first_done)
    h1t = jnp.concatenate(acts, axis=0).astype(FULL).T.astype(LOW)
    slope1t = jnp.concatenate(slopes, axis=0).T

    xt_base = gbase[1] + s.n_col

    def second_done(q, total):
        rows_q = span_of(q)
        z2 = total + v_all[1, row_part(c, q), :].astype(FULL) + bias[1]
        act, slope = gelu_both(z2)
        acts[q] = act.astype(LOW) * valid_low[rows_q]
        slopes[q] = slope * valid_col[rows_q]
        ends = span_of(q).stop
        if ends % (own // 2) == 0:
            lane = 2 * ends // own - 1
            some = [act for i, act in enumerate(acts[: q + 1]) if span_of(i).start >= ends - own // 2]
            some = jnp.concatenate(some, axis=0)
            y3t = dot_nt(w3t[...], some).astype(LOW)
            mine = v3_half(c, lane)
            mine[...] = y3t
            for dy, dk in col_far:
                send(mine, mine, gbase[0] + 2 * c + lane, (r, ys(dy) * nk + ks(dk)))

    def v3_half(index, lane):
        return v3_all.at[index, :, pl.ds(lane * (own // 2), own // 2)]

    spread(1, second_done)
    h2 = jnp.concatenate(acts, axis=0)

    with jax.named_scope("hop3_gather"):
        slope2t = jnp.concatenate(slopes, axis=0).T
        settle(s.n_col - 1)
        for lane in range(2):
            for dy, dk in reversed(col_far):
                source = ys(ny - dy) * nk + ks(nk - dk)
                arrived(v3_half(source, lane), gbase[0] + 2 * source + lane)
    with jax.named_scope("hop3_sum"):
        pbase = wide[0]
        v3 = jnp.concatenate([v3_all[i] for i in range(s.n_col)], axis=1)
        for dz, dx in row_far:
            place = dz * nx + dx
            rt = zs(dz) * nx + xs(dx)
            p3send[place] = dot_nt(v3, tile[row_block(rt), :]).astype(LOW)
            send(p3send.at[place], p3recv.at[place], pbase + place, (rt, c))
        total = dot_nt(v3, tile[row_block(r), :])
        for dz, dx in reversed(row_far):
            place = dz * nx + dx
            arrived(p3recv.at[place], pbase + place)
            total = total + p3recv[place].astype(FULL)
    total = total + v3_all[c].astype(FULL)

    place = lax.broadcasted_iota(jnp.int32, (s.cls, own), 0)
    real = place < s.classes
    on_diag = lax.broadcasted_iota(jnp.int32, (s.cls, s.classes), 0) == lax.broadcasted_iota(
        jnp.int32, (s.cls, s.classes), 1
    )
    bias3 = jnp.sum(
        jnp.where(on_diag, bias_ref[2 * width :].reshape(1, s.classes), 0.0), axis=1, keepdims=True
    )
    logits = jnp.where(real, total + bias3, -1e30)
    shifted = logits - jnp.max(logits, axis=0, keepdims=True)
    weight = jnp.where(real, jnp.exp(shifted), 0.0)
    norm = jnp.sum(weight, axis=0, keepdims=True)
    logp = shifted - jnp.log(norm)
    target = jnp.where(place == lab_ref[...], 1.0 - SMOOTH, 0.0) + SMOOTH / s.classes
    target = jnp.where(real, target, 0.0)
    row_loss = -jnp.sum(jnp.where(real, target * logp, 0.0), axis=0, keepdims=True)
    loss = jnp.sum(row_loss * counted, axis=1, keepdims=True)
    number = jnp.sum(counted, axis=1, keepdims=True)
    dlt = ((weight / norm - target) * counted).astype(LOW)

    with jax.named_scope("back3_gather"):
        base = wide[1]
        mine = dl_all.at[r]
        mine[...] = dlt
        for dz, dx in row_far:
            send(mine, mine, base + r, (zs(dz) * nx + xs(dx), c))
        here = dot(dlt, tile[row_block(r), :])
        for dz, dx in reversed(row_far):
            source = zback(dz) * nx + xs(nx - dx)
            arrived(dl_all.at[source], base + source)
            here = here + dot(dl_all[source], tile[row_block(source), :])
        acc[: s.cls, :cols] = here
    with jax.named_scope("back3_sum"):
        qbase = gbase[1]
        for dy, dk in col_far:
            place = dy * nk + dk
            ct = ys(dy) * nk + ks(dk)
            q3send[place] = acc[: s.cls, row_block(ct)].astype(LOW)
            send(q3send.at[place], q3recv.at[place], qbase + place, (r, ct))
        total = dlt.astype(FULL) + acc[: s.cls, row_block(c)]
        for dy, dk in reversed(col_far):
            place = dy * nk + dk
            arrived(q3recv.at[place], qbase + place)
            total = total + q3recv[place].astype(FULL)
    qt = total.astype(LOW)
    dh2t = lax.dot_general(
        w3t[...], qt, (((0,), (0,)), ((), ())), preferred_element_type=FULL
    )
    step_cols = min(cols, 1024)

    def gained(values, block, fresh=False):
        for j in range(0, cols, step_cols):
            here = dot(values, tile[block, j : j + step_cols])
            if fresh:
                acc[:, j : j + step_cols] = here
            else:
                acc[:, j : j + step_cols] += here

    def halves(lane, row):
        return (
            pl.ds(row * (width // 2), width // 2),
            pl.ds(lane * (own // 2), own // 2),
        )

    quarters = [(lane, row) for lane in range(2) for row in range(2)]
    def receive(hop, values, meanwhile=None, late=None):
        base, np = wide[hop], len(quarters)
        first = hop * s.n_row

        def piece(dz, dx, q):
            return pool.at[(first + dx * nz + dz, *halves(*quarters[q]))]

        def to_z(dz, q, when=None, start=True):
            return send(
                piece(0, 0, q),
                piece(dz, 0, q),
                base + dz * np + q,
                at(zs(dz), x, y, k),
                when=when,
                start=start,
            )

        def to_x(dz, q, start=True):
            return [
                send(
                    piece(dz, 0, q),
                    piece(dz, dx, q),
                    base + (dx * nz + dz) * np + q,
                    at(z, xs(dx), y, k),
                    start=start,
                )
                for dx in range(1, nx)
            ]

        own_parts = []
        for lane in range(2):
            mine = values(lane)
            own_parts.append(mine)
            pool[first, :, lane * (own // 2) : (lane + 1) * (own // 2)] = mine
            for q in (2 * lane, 2 * lane + 1):
                if relayed:
                    to_z(2, q)
                    to_z(1, q)
                else:
                    for dz in range(nz - 1, 0, -1):
                        to_z(dz, q)
                to_x(0, q)

        def source(dz, dx):
            return row_block(zback(dz) * nx + xs(nx - dx))

        gained(jnp.concatenate(own_parts, axis=1), row_block(r), fresh=True)
        if meanwhile is not None:
            meanwhile()

        passing = {
            (dz, q): to_x(dz, q, start=False) for q in range(np) for dz in range(1, nz)
        }

        def step(dz, q):
            arrived(piece(dz, 0, q), base + dz * np + q)
            for copy in passing[dz, q]:
                copy.start()

        if relayed:
            relays = [
                send(
                    piece(2, 0, q),
                    piece(3, 0, q),
                    base + 3 * np + q,
                    at(zs(1), x, y, k),
                    when=inner,
                    start=False,
                )
                for q in range(np)
            ]
            paced = [to_z(3, q, inner, start=False) for q in range(np)]

            @pl.when(inner)
            def _():
                for q in range(np):
                    arrived(piece(2, 0, q), base + 2 * np + q)
                    relays[q].start()
                    paced[q].start()
                    for copy in passing[2, q]:
                        copy.start()
                    step(1, q)
                    if q > 1:
                        step(3, q - 2)
                for q in range(np - 2, np):
                    step(3, q)

            @pl.when(outer)
            def _():
                for q in range(np + 2):
                    if q < np:
                        step(1, q)
                    if 0 < q <= np:
                        step(2, q - 1)
                    if q > 2:
                        step(3, q - 3)
                for q in range(np - 1, np):
                    step(3, q)
        else:
            for q in range(np):
                for dz in range(1, nz):
                    step(dz, q)
        for dz in range(1, nz):
            gained(pool[first + dz], source(dz, 0))
        if late is not None:
            late()
        for dz in range(nz):
            for dx in range(1, nx):
                for q in range(np):
                    arrived(piece(dz, dx, q), base + (dx * nz + dz) * np + q)
                gained(pool[first + dx * nz + dz], source(dz, dx))

    dz2t = (dh2t * slope2t).astype(LOW)
    half_own = own // 2

    def features_out():
        for d in range(1, ny):
            send(own_xt, own_xt, xt_base + c, at(z, x, ys(d), k))
        if nk > 1:
            send(own_xt, own_xt, xt_base + c, sibling)

    with jax.named_scope("back2_rows"):
        settle()
        receive(0, lambda lane: dz2t[:, lane * half_own : (lane + 1) * half_own], features_out)
    cbase = gbase[0] + 2 * s.n_col
    ybase = gbase[1] + 2 * s.n_col

    def lane_part(index, lane):
        return pl.ds(pl.multiple_of(index * own + lane * half_own, half_own), half_own)

    def held(place, lane):
        return xsend.at[place, :, pl.ds(lane * half_own, half_own)]

    def crecv(dy, lane):
        return v_all.at[0, dy * own : (dy + 1) * own, pl.ds(lane * half_own, half_own)]

    def yrecv(dy, lane):
        return crecv(dy + (ny if nk > 1 else 0), lane)

    column_totals = [None, None]
    with jax.named_scope("back2_cols"):
        for lane in range(2):
            for dy in range(ny - 1, -1, -1):
                if nk > 1:
                    there = held(dy, lane)
                    there[...] = acc[:, lane_part(ys(dy) * nk + 1 - k, lane)].astype(LOW)
                    send(there, crecv(dy, lane), cbase + 2 * dy + lane, sibling)
        for lane in range(2):
            for dy in range(ny - 1, -1, -1):
                here = acc[:, lane_part(ys(dy) * nk + k, lane)]
                if nk > 1:
                    arrived(crecv(dy, lane), cbase + 2 * dy + lane)
                    here = here + crecv(dy, lane)[...].astype(FULL)
                if dy:
                    there = held(ny + dy, lane)
                    there[...] = here.astype(LOW)
                    send(
                        there, yrecv(dy, lane), ybase + 2 * dy + lane, at(z, x, ys(dy), k)
                    )
                else:
                    column_totals[lane] = here
        for d in range(1, ny):
            source = ys(ny - d) * nk + k
            arrived(xt_all.at[source], xt_base + source)
            if nk > 1:
                send(xt_all.at[source], xt_all.at[source], xt_base + source, sibling)

    dy2_parts, dz1_parts = [], []

    def first_slopes(lane):
        lanes_q = slice(lane * half_own, (lane + 1) * half_own)
        total = column_totals[lane] + dz2t[:, lanes_q].astype(FULL)
        with jax.named_scope("y_wait"):
            for dy in range(1, ny):
                arrived(yrecv(dy, lane), ybase + 2 * dy + lane)
                total = total + yrecv(dy, lane)[...].astype(FULL)
        dy2_parts.append(total.astype(LOW))
        dz1_parts.append((dot(w2, dy2_parts[lane]) * slope1t[:, lanes_q]).astype(LOW))
        return dz1_parts[lane]

    lanes, plane = s.lanes, s.plane
    me = y * nx + x
    others = [(dx, dy) for dx in range(nx) for dy in range(ny) if dx or dy]

    def lane_block(index):
        return pl.ds(pl.multiple_of(index * lanes, lanes), lanes)

    class Total:
        def __init__(self, start, rows, mark=None, base=None):
            self.all = pl.ds(start, rows)
            self.start, self.rows = start, rows
            self.n = rows // plane
            self.short = pl.ds(start // plane, self.n)
            self.mark = rslots(1) if mark is None else mark
            self.base = rslots(3 * plane + nz) if base is None else base

        def piece(self, index):
            return pl.ds(pl.multiple_of(self.start + index * self.n, 16), self.n)

        def core_send(self, other):
            if nk > 1:
                half_send[self.all, :] = other.astype(LOW)
                send(half_send.at[self.all], half_recv.at[self.all], self.mark, sibling)

        def plane_send(self, mine):
            if nk > 1:
                arrived(half_recv.at[self.all], self.mark)
                mine = mine + half_recv[self.all, :].astype(FULL)
            half[self.all, :] = mine.astype(LOW)
            base = self.base
            for dx, dy in others:
                there = ys(dy) * nx + xs(dx)
                send(
                    half.at[self.piece(there)],
                    plane_recv.at[me, self.short],
                    base + me,
                    at(z, xs(dx), ys(dy), k),
                )
            plane_recv[me, self.short, :] = half[self.piece(me), :]

        def line_send(self):
            base = self.base
            for dx, dy in others:
                there = ys(dy) * nx + xs(dx)
                arrived(plane_recv.at[there, self.short], base + there)
            total = plane_recv[0, self.short, :].astype(FULL)
            for i in range(1, plane):
                total = total + plane_recv[i, self.short, :].astype(FULL)
            quarter[z, self.short, :] = total.astype(LOW)
            mine = quarter.at[z, self.short]
            base = self.base + plane
            for dz in range(nz - 1, 0, -1):
                send(mine, mine, base + z, at(zs(dz), x, y, k))

        def back_send(self):
            base = self.base + plane
            for dz in range(1, nz):
                arrived(quarter.at[zback(dz), self.short], base + zback(dz))
            total = quarter[0, self.short, :].astype(FULL)
            for i in range(1, nz):
                total = total + quarter[i, self.short, :].astype(FULL)
            base = self.base + plane + nz
            mine = fin.at[k, self.piece(me)]
            mine[...] = total.astype(LOW)
            for dx, dy in others:
                send(mine, mine, base + me, at(z, xs(dx), ys(dy), k))
            if nk > 1:
                send(mine, mine, base + plane + me, sibling)

        def back_forward(self):
            base = self.base + plane + nz
            for dx, dy in others:
                there = ys(dy) * nx + xs(dx)
                block = fin.at[k, self.piece(there)]
                arrived(block, base + there)
                if nk > 1:
                    send(block, block, base + plane + there, sibling)

        def end(self):
            base = self.base + plane + nz
            if nk > 1:
                for i in range(plane):
                    arrived(fin.at[1 - k, self.piece(i)], base + plane + i)

    def write(start, count):
        grad_ref[:, start : start + count, :] = fin[:, start : start + count, :]

    ones_at = [
        (gbase[i] + 2 * s.n_col + 2 * ny, wide[0] + i * (3 * plane + nz)) for i in range(2)
    ]
    ones_at += [(None, None)] * len(s.chunks)
    assert 2 * (3 * plane + nz) <= s.n_row * nh
    one = [
        Total(start, stop - start, *there) for (start, stop), there in zip(s.chunks, ones_at)
    ]
    two = Total(s.one_rows, s.two_rows)
    tail = s.two_rows - width - s.cls

    ones = jnp.ones((8, own), LOW)
    row = lax.broadcasted_iota(jnp.int32, (8, width), 0)
    lane_of = lax.broadcasted_iota(jnp.int32, (8, width), 1)
    bias_three = jnp.concatenate([dlt, jnp.zeros((width - s.cls, own), LOW)], axis=0)
    misc = jnp.where(row == 1, dot_nt(ones, dz2t), 0.0)
    misc = jnp.where(row == 2, dot_nt(ones, bias_three), misc)
    misc = jnp.where((row == 3) & (lane_of == 0), loss, misc)
    misc = jnp.where((row == 3) & (lane_of == 1), number, misc)
    mbase = rslots(1 + plane + nz)
    plane_base, line_base = mbase + 1, mbase + 1 + plane

    def early():
        misc_k[0] = misc
        if nk > 1:
            send(misc_k.at[0], misc_k.at[1], mbase, sibling)
        grad3t = dot(qt, h2)
        dy2t = jnp.concatenate(dy2_parts, axis=1)
        grad2 = dot_nt(h1t, dy2t)
        acc_two = jnp.concatenate(
            [grad2, grad3t] + ([jnp.zeros((tail, width), FULL)] if tail else []), axis=0
        )
        if nk > 1:
            first, second = acc_two[:, :lanes], acc_two[:, lanes:]
            low_core = (k == 0).astype(FULL)
            two.core_send(second * low_core + first * (1.0 - low_core))
            two.plane_send(first * low_core + second * (1.0 - low_core))
        else:
            two.plane_send(acc_two)
        here = misc_k[0]
        if nk > 1:
            arrived(misc_k.at[1], mbase)
            here = here + misc_k[1]
        misc_p[me] = here
        for dx, dy in others:
            send(misc_p.at[me], misc_p.at[me], plane_base + me, at(z, xs(dx), ys(dy), k))

    def late():
        two.line_send()
        for dx, dy in others:
            there = ys(dy) * nx + xs(dx)
            arrived(misc_p.at[there], plane_base + there)
        here = misc_p[0]
        for i in range(1, plane):
            here = here + misc_p[i]
        misc_z[z] = here
        for dz in range(1, nz):
            send(misc_z.at[z], misc_z.at[z], line_base + z, at(zs(dz), x, y, k))

    with jax.named_scope("back1_rows"):
        receive(1, first_slopes, early, late)
    with jax.named_scope("grad1"):
        dz1t = jnp.concatenate(dz1_parts, axis=1)
        acc[:, row_block(c)] += dz1t.astype(FULL)
        if nk > 1:
            for d in range(ny):
                source = ys(d) * nk + 1 - k
                arrived(xt_all.at[source], xt_base + source)

        low_core = (k == 0).astype(FULL)
        bias_one = dot_nt(ones, dz1t)[0:1, :]

        def grad_one(start, stop):
            total = None
            end = min(stop, s.feat_up)
            for i in range(s.n_col):
                here = acc[:, i * own : (i + 1) * own].astype(LOW)
                here = dot_nt(xt_all[i, start:end, :], here)
                total = here if total is None else total + here
            if end < stop:
                total = jnp.concatenate([total, jnp.zeros((stop - end, width), FULL)], axis=0)
            bias_at = s.feat - start
            if 0 <= bias_at < stop - start:
                places = lax.broadcasted_iota(jnp.int32, (stop - start, width), 0)
                total = jnp.where(places == bias_at, bias_one, total)
            if nk == 1:
                return None, total
            first, second = total[:, :lanes], total[:, lanes:]
            return (
                second * low_core + first * (1.0 - low_core),
                first * low_core + second * (1.0 - low_core),
            )

        waiting = None
        for chunk, (start, stop) in zip(one, s.chunks):
            other, mine = grad_one(start, stop)
            chunk.core_send(other)
            if waiting is not None:
                waiting()
            waiting = functools.partial(chunk.plane_send, mine)
        waiting()

    with jax.named_scope("sum_plane"):
        left = len(pending)
        two.back_send()
    with jax.named_scope("sum_line"):
        for chunk in one:
            chunk.line_send()
    with jax.named_scope("back_line"):
        for chunk in one:
            chunk.back_send()
        for dz in range(1, nz):
            arrived(misc_z.at[zback(dz)], line_base + zback(dz))
        misc = misc_z[0]
        for i in range(1, nz):
            misc = misc + misc_z[i]
        misc_ref[...] = jnp.where(row == 4, 1.0 / misc[3:4, 1:2], misc)
        settle(len(pending) - left)
    with jax.named_scope("back_plane"):
        for chunk in one:
            chunk.back_forward()
        two.back_forward()
        for chunk in one:
            chunk.end()
            write(chunk.start, chunk.rows)
        two.end()
        write(s.one_rows, s.two_rows)
    with jax.named_scope("settle"):
        settle()
    assert rcount[0] <= s.arrivals


def update_pieces(s):
    some = up(s.feat // 4, 16)
    cuts = [min(i * some, s.feat) for i in range(5)]
    one = [(0, start, stop - start) for start, stop in zip(cuts, cuts[1:]) if stop > start]
    return (*one, (1, 0, s.width), (2, 0, s.classes))


def adam_kernel(s, grad_ref, misc_ref, *refs):
    ins, outs, scratch = refs[:12], refs[12:26], refs[26:]
    bias_out, ends, *held = scratch[:-1]
    sem_out = scratch[-1]
    width, classes, lanes = s.width, s.classes, s.lanes
    grad_at = (0, s.one_rows, s.one_rows + width)

    stores = []

    def store(source, target):
        copy = pltpu.make_async_copy(source, target, sem_out.at[len(stores)])
        copy.start()
        stores.append(copy)

    total = misc_ref[3:4, 1:2]
    scale = misc_ref[4:5, 0:1]
    for (which, start, rows), target in zip(update_pieces(s), held):
        span = slice(start, start + rows)
        for i in range(s.nk):
            lane = slice(i * lanes, (i + 1) * lanes)
            first = grad_at[which] + start
            grad = grad_ref[i, first : first + up(rows, 16), :].astype(FULL)[:rows]
            weight, one, two = (ins[3 * which + j][span, lane] for j in range(3))
            for j, new in enumerate(adam_update(weight, one, two, grad * scale)):
                target[j, :, lane] = new
        for j in range(3):
            store(target.at[j], outs[3 * which + j].at[pl.ds(start, rows)])
    for i, size in enumerate((width, width, classes)):
        span = slice(i * width, i * width + size)
        weight, first, second = (ins[9 + j][span] for j in range(3))
        grad = misc_ref[i, :size]
        if not i:
            top = s.feat // 16 * 16
            rows = [grad_ref[j, top : top + 16, :].astype(FULL) for j in range(s.nk)]
            grad = jnp.concatenate([a[s.feat - top] for a in rows])
        new = adam_update(weight, first, second, grad * misc_ref[4, :size])
        for j in range(3):
            bias_out[j][span] = new[j]
    for j in range(3):
        store(bias_out[j], outs[9 + j])
    ends[0] = misc_ref[3:4, 0:1]
    ends[1] = total
    for i in range(2):
        store(ends.at[i], outs[12 + i])
    for copy in stores:
        copy.wait()


def shards(
    sizes,
    features,
    adjacency,
    occupancy,
    labels,
    train_mask,
    node_count,
    weight_one,
    weight_two,
    weight_three,
    biases,
    first_one,
    first_two,
    first_three,
    first_bias,
    second_one,
    second_two,
    second_three,
    second_bias,
):
    own, feat = features.shape
    width = weight_two.shape[0]
    classes = weight_three.shape[1]
    s = sizes(own, feat, width, classes)
    rows, cols = adjacency.shape
    lanes = s.lanes
    vmem = pl.BlockSpec(memory_space=pltpu.VMEM)
    smem = pl.BlockSpec(memory_space=pltpu.SMEM)
    anywhere = pl.BlockSpec(memory_space=pl.ANY)
    block = (own, width)
    small = (s.cls, own)
    shapes = [
        ((rows, cols), LOW),
        ((s.feat_up, width), LOW),
        ((s.cls, width), LOW),
        ((s.n_col, s.feat_up, own), LOW),
        ((2, s.n_col * own, width), LOW),
        ((2 * s.n_row, *block), LOW),
        ((max(2 * s.ny, s.n_row - s.nz), *block), LOW),
        ((max(1, s.nz - 1), *block), LOW),
        ((2, s.nz if s.relayed else max(1, s.nz - 1), *block), LOW),
        ((s.n_col, *small), LOW),
        ((s.n_row, *small), LOW),
        ((s.n_row, *small), LOW),
        ((s.n_row, *small), LOW),
        ((s.n_col, *small), LOW),
        ((s.n_col, *small), LOW),
        ((width, max(cols, s.nz * own)), FULL),
        ((s.grad_rows, lanes), LOW),
        ((s.grad_rows, lanes), LOW),
        ((s.grad_rows, lanes), LOW),
        ((s.plane, s.grad_rows // s.plane, lanes), LOW),
        ((s.nz, s.grad_rows // s.plane, lanes), LOW),
        ((s.nk, s.grad_rows, lanes), LOW),
        ((2, 8, width), FULL),
        ((s.plane, 8, width), FULL),
        ((s.nz, 8, width), FULL),
    ]
    bytes_held = sum(math.prod(shape) * jnp.dtype(kind).itemsize for shape, kind in shapes)
    limit = min(62, 16 + bytes_held // 2**20) * 2**20
    grads, misc = pl.pallas_call(
        functools.partial(kernel, s),
        out_shape=(
            pltpu.VMEM((s.nk, s.grad_rows, lanes), LOW),
            pltpu.VMEM((8, width), FULL),
        ),
        in_specs=[
            vmem,
            anywhere,
            smem,
            vmem,
            vmem,
            smem,
            vmem,
            vmem,
            vmem,
            vmem,
        ],
        out_specs=(vmem, vmem),
        scratch_shapes=[
            *[pltpu.VMEM(shape, kind) for shape, kind in shapes],
            pltpu.SemaphoreType.DMA((s.sends,)),
            pltpu.SemaphoreType.DMA((s.arrivals,)),
            pltpu.SemaphoreType.DMA((rows // SUB,)),
        ],
        compiler_params=pltpu.CompilerParams(
            collective_id=0, has_side_effects=True, vmem_limit_bytes=limit
        ),
        cost_estimate=pl.CostEstimate(
            flops=12 * rows * cols * width, bytes_accessed=2 * rows * cols, transcendentals=0
        ),
        name="step",
    )(
        *[
            pltpu.with_memory_space_constraint(a, pltpu.HBM)
            for a in (features.T, adjacency)
        ],
        pltpu.with_memory_space_constraint(occupancy, pltpu.HBM),
        *[
            pltpu.with_memory_space_constraint(a, pltpu.HBM)
            for a in (labels.reshape(1, own), train_mask.reshape(1, own))
        ],
        node_count,
        *[
            pltpu.with_memory_space_constraint(a, pltpu.HBM)
            for a in (weight_one, weight_two, weight_three.T, biases)
        ],
    )
    state = (
        weight_one,
        first_one,
        second_one,
        weight_two,
        first_two,
        second_two,
        weight_three.T,
        first_three.T,
        second_three.T,
        biases,
        first_bias,
        second_bias,
    )
    new = pl.pallas_call(
        functools.partial(adam_kernel, s),
        out_shape=(
            *[jax.ShapeDtypeStruct(a.shape, FULL) for a in state],
            jax.ShapeDtypeStruct((1, 1), FULL),
            jax.ShapeDtypeStruct((1, 1), FULL),
        ),
        in_specs=[vmem] * 14,
        out_specs=(anywhere,) * 14,
        scratch_shapes=[
            [pltpu.VMEM(biases.shape, FULL)] * 3,
            pltpu.VMEM((2, 1, 1), FULL),
            *[pltpu.VMEM((3, rows, width), FULL) for _, _, rows in update_pieces(s)],
            pltpu.SemaphoreType.DMA((3 * len(update_pieces(s)) + 5,)),
        ],
        compiler_params=pltpu.CompilerParams(vmem_limit_bytes=32 * 2**20),
        name="update",
    )(grads, misc, *state)
    return (
        *new[:6],
        *[a.T for a in new[6:9]],
        *new[9:12],
        new[12].reshape(()),
        new[13].reshape(()),
    )


def solution(mesh):
    placed = (
        P(("row", "col"), None),
        P("col", "row"),
        P("col", "row"),
        P(("row", "col")),
        P(("row", "col")),
        P(("row", "col")),
        *[P()] * 12,
    )
    sizes = functools.partial(Sizes, mesh.shape["row"], mesh.shape["col"])
    return jax.shard_map(
        functools.partial(shards, sizes),
        mesh=mesh,
        in_specs=placed,
        out_specs=(P(),) * 14,
        check_vma=False,
    )
```

```python
import functools
import math

import jax
import jax.numpy as jnp
from jax import lax
from jax.experimental import pallas as pl
from jax.experimental.pallas import tpu as pltpu
from jax.sharding import PartitionSpec as P

SUB = 512
STEP = 5


B_ONE = 0.5
B_TWO = 0.5
RATE = 0.05
DECAY = 0.01
EPSILON = 1e-08
SMOOTH = 0.1

MESH = pl.DeviceIdType.MESH
LOW = jnp.bfloat16
FULL = jnp.float32
GELU_A = 0.7978845608028654
GELU_B = 0.044715


def adam_update(weight, first, second, grad):
    first_new = B_ONE * first + (1.0 - B_ONE) * grad
    second_new = B_TWO * second + (1.0 - B_TWO) * grad * grad
    fix_one = 1.0 - B_ONE**STEP
    fix_two = 1.0 - B_TWO**STEP
    scaled = (first_new * (1.0 / fix_one)) / (jnp.sqrt(second_new * (1.0 / fix_two)) + EPSILON)
    return (first_new, second_new, weight - RATE * (scaled + DECAY * weight))


def up(value, unit):
    return -(-value // unit) * unit


def dot(left, right):
    return jnp.dot(left, right, preferred_element_type=FULL)


def dot_nt(left, right):
    return lax.dot_general(left, right, (((1,), (1,)), ((), ())), preferred_element_type=FULL)


def gelu_both(z):
    t = jnp.tanh(GELU_A * (z + GELU_B * z * z * z))
    half = 0.5 * (1.0 + t)
    slope = half + 0.5 * z * (1.0 - t * t) * (GELU_A * (1.0 + 3.0 * GELU_B * z * z))
    return z * half, slope


class Sizes:
    def __init__(self, n_row, n_col, own, feat, width, classes):
        self.n_row, self.n_col = n_row, n_col
        self.nk = 2 if n_col % 2 == 0 else 1
        self.ny = n_col // self.nk
        self.nx = self.ny if n_row % self.ny == 0 else 1
        self.nz = n_row // self.nx
        self.own, self.feat, self.width, self.classes = own, feat, width, classes
        self.feat_up = up(feat, 128)
        self.cls = up(classes, 16)
        self.plane = self.nx * self.ny
        self.one_rows = up(feat + 1, 16 * self.plane)
        self.two_rows = up(width + self.cls, 16 * self.plane)
        self.grad_rows = self.one_rows + self.two_rows
        self.lanes = width // self.nk
        units = self.one_rows // (16 * self.plane)
        chunks = min(3, units)
        cuts = [units * i // chunks * 16 * self.plane for i in range(chunks + 1)]
        self.chunks = list(zip(cuts, cuts[1:]))
        cuts = [own // 4 * i for i in range(5)]
        self.parts = [(start, stop - start) for start, stop in zip(cuts, cuts[1:])]
        self.nh = len(self.parts)
        self.relayed = self.nz == 4
        self.sends = 3 * (n_row + n_col) + 3 * self.plane
        wide = 2 * self.nh * (n_row + n_col)
        self.arrivals = wide + max(1, chunks - 1) * (1 + 3 * self.plane + self.nz) + 1 + self.plane + self.nz


def kernel(
    s,
    xt_ref,
    adj_ref,
    occ_ref,
    lab_ref,
    mask_ref,
    cnt_ref,
    w1_ref,
    w2_ref,
    w3t_ref,
    bias_ref,
    grad_ref,
    misc_ref,
    tile,
    w1b,
    w3t,
    xt_all,
    v_all,
    pool,
    xsend,
    zsend,
    zrecv,
    v3_all,
    p3send,
    p3recv,
    dl_all,
    q3send,
    q3recv,
    acc,
    half_send,
    half_recv,
    half,
    plane_recv,
    quarter,
    fin,
    misc_k,
    misc_p,
    misc_z,
    ssem,
    rsem,
    lsem,
):
    nx, ny, nz, nk = s.nx, s.ny, s.nz, s.nk
    own, width = s.own, s.width
    r, c = lax.axis_index("row"), lax.axis_index("col")
    z, x = r // nx, r % nx
    y, k = c // nk, c % nk

    def at(zz, xx, yy, kk):
        return (zz * nx + xx, yy * nk + kk)

    def xs(d):
        return lax.rem(x + d, nx)

    def ys(d):
        return lax.rem(y + d, ny)

    def zs(d):
        if nz & (nz - 1):
            return lax.rem(z + d, nz)
        there, bit = z, 1
        while bit < nz:
            if d & bit:
                there = there + bit - 2 * bit * lax.rem(there // bit, 2)
            bit *= 2
        return there

    def zback(d):
        return zs(d) if not nz & (nz - 1) else lax.rem(z + nz - d, nz)

    sibling = at(z, x, y, 1 - k)
    relayed = s.relayed
    is_inner = lax.rem((z + 1) // 2, 2)
    inner = is_inner == 1
    outer = is_inner == 0
    line = [dz for dz in range(nz - 1, -1, -1)]
    row_far = [(dz, dx) for dz in line for dx in range(nx - 1, -1, -1) if dz or dx]
    col_far = [(dy, dk) for dy in range(ny - 1, -1, -1) for dk in range(nk - 1, -1, -1) if dy or dk]

    def ks(d):
        return lax.rem(k + d, nk)


    rows, cols = tile.shape
    n_sub = rows // SUB
    loads = [
        pltpu.make_async_copy(
            adj_ref.at[pl.ds(a * SUB, SUB)], tile.at[pl.ds(a * SUB, SUB)], lsem.at[a]
        )
        for a in range(n_sub)
    ]
    for load in loads:
        load.start()

    peers = []
    for d in range(1, s.n_row):
        peers.append((lax.rem(r + d, s.n_row), c))
    for d in range(1, s.n_col):
        peers.append((r, lax.rem(c + d, s.n_col)))
    for dx in range(1, nx):
        for dy in range(1, ny):
            peers.append(at(z, xs(dx), ys(dy), k))
    barrier = pltpu.get_barrier_semaphore()
    for peer in peers:
        pl.semaphore_signal(barrier, inc=1, device_id=peer, device_id_type=MESH)

    free = list(range(s.sends))
    pending = []

    def send(src, dst, recv_slot, device, of=None, when=None, start=True):
        if not free:
            settle(len(pending) - 1)
        copy = pltpu.make_async_remote_copy(
            src_ref=src,
            dst_ref=dst,
            send_sem=ssem.at[free[0]],
            recv_sem=rsem.at[recv_slot],
            device_id=device,
            device_id_type=MESH,
        )
        if start:
            if when is None:
                copy.start()
            else:
                pl.when(when)(copy.start)
        pending.append((copy, free.pop(0), of, when))
        return copy

    def arrived(dst, recv_slot):
        pltpu.make_async_remote_copy(
            src_ref=dst,
            dst_ref=dst,
            send_sem=ssem.at[0],
            recv_sem=rsem.at[recv_slot],
            device_id=sibling,
            device_id_type=MESH,
        ).wait_recv()

    def settle(keep=0, of=None):
        done = [p for p in pending if p[2] == of] if of else pending[: len(pending) - keep]
        for item in done:
            if item[3] is None:
                item[0].wait_send()
            else:
                pl.when(item[3])(item[0].wait_send)
            free.append(item[1])
        left = [p for p in pending if all(p is not q for q in done)]
        pending[:] = left

    rcount = [0]

    def rslots(n):
        rcount[0] += n
        return rcount[0] - n

    def row_block(index):
        return pl.ds(pl.multiple_of(index * own, own), own)

    nh = s.nh

    def row_part(index, q):
        start, count = s.parts[q]
        return pl.ds(pl.multiple_of(index * own + start, count), count)

    def part(q):
        return pl.ds(*s.parts[q])

    def span_of(q):
        start, count = s.parts[q]
        return slice(start, start + count)

    valid_col = (lax.broadcasted_iota(jnp.int32, (own, width), 0) < cnt_ref[0]).astype(FULL)
    valid_low = valid_col.astype(LOW)
    valid_row = (lax.broadcasted_iota(jnp.int32, (1, own), 1) < cnt_ref[0]).astype(FULL)
    counted = mask_ref[...].astype(FULL) * valid_row

    prologue = jax.named_scope("prologue")
    prologue.__enter__()
    pad = s.feat_up - up(s.feat, 16) + 16
    own_xt = xt_all.at[c]
    own_xt[s.feat_up - pad :, :] = jnp.zeros((pad, own), LOW)
    w1b[s.feat_up - pad :, :] = jnp.zeros((pad, width), LOW)
    x_valid = (lax.broadcasted_iota(jnp.int32, (s.feat, own), 1) < cnt_ref[0]).astype(LOW)
    own_xt[: s.feat, :] = xt_ref[...] * x_valid
    w1b[: s.feat, :] = w1_ref[...].astype(LOW)
    y1 = lax.dot_general(
        own_xt[...], w1b[...], (((0,), (0,)), ((), ())), preferred_element_type=FULL
    ).astype(LOW)
    v_all[0, row_block(c), :] = y1

    wide = [rslots(s.n_row * nh) for _ in range(2)]
    gbase = [rslots(s.n_col * nh) for _ in range(2)]
    prologue.__exit__(None, None, None)

    def start_gather(hop, q, values):
        mine = v_all.at[hop, row_part(c, q)]
        if values is not None:
            mine[...] = values
        for d in range(1, ny):
            send(mine, mine, gbase[hop] + c * nh + q, at(z, x, ys(d), k))
        if nk > 1:
            send(mine, mine, gbase[hop] + c * nh + q, sibling)

    def complete_gather(hop):
        for q in range(nh):
            for d in range(1, ny):
                source = ys(ny - d) * nk + k
                block = v_all.at[hop, row_part(source, q)]
                arrived(block, gbase[hop] + source * nh + q)
                if nk > 1:
                    send(block, block, gbase[hop] + source * nh + q, sibling)
        if nk > 1:
            for q in range(nh):
                for d in range(ny):
                    source = ys(d) * nk + 1 - k
                    arrived(
                        v_all.at[hop, row_part(source, q)], gbase[hop] + source * nh + q
                    )

    with jax.named_scope("barrier"):
        pl.semaphore_wait(barrier, len(peers))
    for q in range(nh):
        start_gather(0, q, None)

    if relayed:

        @pl.when(outer)
        def _():
            zrecv[:, 2] = jnp.zeros((2, own, width), LOW)

    w3t[...] = jnp.zeros_like(w3t)
    w3t[: s.classes, :] = w3t_ref[...].astype(LOW)
    w2 = w2_ref[...].astype(LOW)
    for a in range(n_sub):
        loads[a].wait()
        for b in range(cols // own):
            piece = tile[pl.ds(a * SUB, SUB), pl.ds(b * own, own)]
            cover = jnp.full((SUB, own), occ_ref[a, b].astype(FULL), FULL).astype(LOW)
            tile[pl.ds(a * SUB, SUB), pl.ds(b * own, own)] = piece * cover

    def spread(hop, finish):
        settle(of="hop")
        with jax.named_scope("gather_y"):
            complete_gather(hop)
        zbase = wide[hop]
        xbase = zbase + nz * nh
        order = list(range(nz - 1, -1, -1))

        def send_x(dz, dx, q):
            place = (dx - 1) * nz + dz
            send(
                xsend.at[place, part(q)],
                pool.at[hop * s.n_row + place, part(q)],
                xbase + place * nh + q,
                at(z, xs(dx), y, k),
                "hop",
            )

        sequence = []
        if relayed:
            sequence = [(3, 0), (3, 1), (2, 0), (3, 2), (2, 1), (3, 3), (1, 0), (2, 2), (1, 1), (2, 3), (1, 2), (1, 3), (0, 0), (0, 1), (0, 2), (0, 3)]
        else:
            for q in range(nh):
                sequence += [(dz, q) for dz in order if dz]
                if q:
                    sequence.append((0, q - 1))
            sequence.append((0, nh - 1))
        ready = set()
        with jax.named_scope("send_x"):
            for dz, q in sequence:
                for dx in range(1, nx):
                    if (dz, dx) not in ready:
                        ready.add((dz, dx))
                        rt = zs(dz) * nx + xs(dx)
                        xsend[(dx - 1) * nz + dz] = dot(
                            tile[row_block(rt), :], v_all[hop]
                        ).astype(LOW)
                    send_x(dz, dx, q)
            for dz in order:
                acc[:, dz * own : (dz + 1) * own] = dot(
                    tile[row_block(zs(dz) * nx + x), :], v_all[hop]
                )

        def send_z(dz, q):
            rows_q = span_of(q)
            total = acc[rows_q, dz * own : (dz + 1) * own]
            for dx in range(1, nx):
                place = (dx - 1) * nz + dz
                arrived(pool.at[hop * s.n_row + place, part(q)], xbase + place * nh + q)
                total = total + pool[hop * s.n_row + place, rows_q, :].astype(FULL)
            if not dz:
                return total
            there, slot, mark = zs(dz), dz - 1, zbase + dz * nh + q
            if relayed and dz == 3:
                there = is_inner * zs(3) + (1 - is_inner) * zs(1)
                slot, mark = 3 - is_inner, zbase + 3 * nh * is_inner + q
            if relayed and dz == 2:

                @pl.when(inner)
                def _():
                    arrived(zrecv.at[hop, 3, part(q)], zbase + q)
                    handed = zrecv[hop, 3, rows_q, :].astype(FULL)
                    zsend[dz - 1, rows_q, :] = (total + handed).astype(LOW)

                @pl.when(outer)
                def _():
                    zsend[dz - 1, rows_q, :] = total.astype(LOW)

            else:
                zsend[dz - 1, rows_q, :] = total.astype(LOW)
            send(
                zsend.at[dz - 1, part(q)],
                zrecv.at[hop, slot, part(q)],
                mark,
                at(there, x, y, k),
                "hop",
            )
            return total

        totals = [None] * nh

        def sum_z(q):
            total = totals[q]
            rows_q = span_of(q)
            for dz in range(1, nz):
                there, mark = zrecv.at[hop, dz - 1, part(q)], zbase + dz * nh + q
                if relayed and dz == 3:
                    pl.when(inner)(functools.partial(arrived, there, mark))
                else:
                    arrived(there, mark)
                total = total + zrecv[hop, dz - 1, rows_q, :].astype(FULL)
            finish(q, total)

        with jax.named_scope("send_z"):
            for dz, q in sequence[:-1]:
                totals[q] = send_z(dz, q)
                if not dz:
                    with jax.named_scope("sum_z0"):
                        sum_z(q)
        with jax.named_scope("sum_z1"):
            totals[nh - 1] = send_z(0, nh - 1)
            sum_z(nh - 1)

    bias = [bias_ref[i * width : (i + 1) * width].reshape(1, width) for i in range(2)]
    slopes, acts = [None] * nh, [None] * nh

    def first_done(q, total):
        rows_q = span_of(q)
        z1 = total + v_all[0, row_part(c, q), :].astype(FULL) + bias[0]
        act, slope = gelu_both(z1)
        h1 = act.astype(LOW) * valid_low[rows_q]
        start_gather(1, q, dot(h1, w2).astype(LOW))
        acts[q], slopes[q] = h1, slope * valid_col[rows_q]

    spread(0, first_done)
    h1t = jnp.concatenate(acts, axis=0).astype(FULL).T.astype(LOW)
    slope1t = jnp.concatenate(slopes, axis=0).T

    xt_base = gbase[1] + s.n_col

    def second_done(q, total):
        rows_q = span_of(q)
        z2 = total + v_all[1, row_part(c, q), :].astype(FULL) + bias[1]
        act, slope = gelu_both(z2)
        acts[q] = act.astype(LOW) * valid_low[rows_q]
        slopes[q] = slope * valid_col[rows_q]
        ends = span_of(q).stop
        if ends % (own // 2) == 0:
            lane = 2 * ends // own - 1
            some = [act for i, act in enumerate(acts[: q + 1]) if span_of(i).start >= ends - own // 2]
            some = jnp.concatenate(some, axis=0)
            y3t = dot_nt(w3t[...], some).astype(LOW)
            mine = v3_half(c, lane)
            mine[...] = y3t
            for dy, dk in col_far:
                send(mine, mine, gbase[0] + 2 * c + lane, (r, ys(dy) * nk + ks(dk)))

    def v3_half(index, lane):
        return v3_all.at[index, :, pl.ds(lane * (own // 2), own // 2)]

    spread(1, second_done)
    h2 = jnp.concatenate(acts, axis=0)

    with jax.named_scope("hop3_gather"):
        slope2t = jnp.concatenate(slopes, axis=0).T
        settle(s.n_col - 1)
        for lane in range(2):
            for dy, dk in reversed(col_far):
                source = ys(ny - dy) * nk + ks(nk - dk)
                arrived(v3_half(source, lane), gbase[0] + 2 * source + lane)
    with jax.named_scope("hop3_sum"):
        pbase = wide[0]
        v3 = jnp.concatenate([v3_all[i] for i in range(s.n_col)], axis=1)
        for dz, dx in row_far:
            place = dz * nx + dx
            rt = zs(dz) * nx + xs(dx)
            p3send[place] = dot_nt(v3, tile[row_block(rt), :]).astype(LOW)
            send(p3send.at[place], p3recv.at[place], pbase + place, (rt, c))
        total = dot_nt(v3, tile[row_block(r), :])
        for dz, dx in reversed(row_far):
            place = dz * nx + dx
            arrived(p3recv.at[place], pbase + place)
            total = total + p3recv[place].astype(FULL)
    total = total + v3_all[c].astype(FULL)

    place = lax.broadcasted_iota(jnp.int32, (s.cls, own), 0)
    real = place < s.classes
    on_diag = lax.broadcasted_iota(jnp.int32, (s.cls, s.classes), 0) == lax.broadcasted_iota(
        jnp.int32, (s.cls, s.classes), 1
    )
    bias3 = jnp.sum(
        jnp.where(on_diag, bias_ref[2 * width :].reshape(1, s.classes), 0.0), axis=1, keepdims=True
    )
    logits = jnp.where(real, total + bias3, -1e30)
    shifted = logits - jnp.max(logits, axis=0, keepdims=True)
    weight = jnp.where(real, jnp.exp(shifted), 0.0)
    norm = jnp.sum(weight, axis=0, keepdims=True)
    logp = shifted - jnp.log(norm)
    target = jnp.where(place == lab_ref[...], 1.0 - SMOOTH, 0.0) + SMOOTH / s.classes
    target = jnp.where(real, target, 0.0)
    row_loss = -jnp.sum(jnp.where(real, target * logp, 0.0), axis=0, keepdims=True)
    loss = jnp.sum(row_loss * counted, axis=1, keepdims=True)
    number = jnp.sum(counted, axis=1, keepdims=True)
    dlt = ((weight / norm - target) * counted).astype(LOW)

    with jax.named_scope("back3_gather"):
        base = wide[1]
        mine = dl_all.at[r]
        mine[...] = dlt
        for dz, dx in row_far:
            send(mine, mine, base + r, (zs(dz) * nx + xs(dx), c))
        here = dot(dlt, tile[row_block(r), :])
        for dz, dx in reversed(row_far):
            source = zback(dz) * nx + xs(nx - dx)
            arrived(dl_all.at[source], base + source)
            here = here + dot(dl_all[source], tile[row_block(source), :])
        acc[: s.cls, :cols] = here
    with jax.named_scope("back3_sum"):
        qbase = gbase[1]
        for dy, dk in col_far:
            place = dy * nk + dk
            ct = ys(dy) * nk + ks(dk)
            q3send[place] = acc[: s.cls, row_block(ct)].astype(LOW)
            send(q3send.at[place], q3recv.at[place], qbase + place, (r, ct))
        total = dlt.astype(FULL) + acc[: s.cls, row_block(c)]
        for dy, dk in reversed(col_far):
            place = dy * nk + dk
            arrived(q3recv.at[place], qbase + place)
            total = total + q3recv[place].astype(FULL)
    qt = total.astype(LOW)
    dh2t = lax.dot_general(
        w3t[...], qt, (((0,), (0,)), ((), ())), preferred_element_type=FULL
    )
    step_cols = min(cols, 1024)

    def gained(values, block, fresh=False):
        for j in range(0, cols, step_cols):
            here = dot(values, tile[block, j : j + step_cols])
            if fresh:
                acc[:, j : j + step_cols] = here
            else:
                acc[:, j : j + step_cols] += here

    def halves(lane, row):
        return (
            pl.ds(row * (width // 2), width // 2),
            pl.ds(lane * (own // 2), own // 2),
        )

    quarters = [(lane, row) for lane in range(2) for row in range(2)]
    def receive(hop, values, meanwhile=None, late=None):
        base, np = wide[hop], len(quarters)
        first = hop * s.n_row

        def piece(dz, dx, q):
            return pool.at[(first + dx * nz + dz, *halves(*quarters[q]))]

        def to_z(dz, q, when=None, start=True):
            return send(
                piece(0, 0, q),
                piece(dz, 0, q),
                base + dz * np + q,
                at(zs(dz), x, y, k),
                when=when,
                start=start,
            )

        def to_x(dz, q, start=True):
            return [
                send(
                    piece(dz, 0, q),
                    piece(dz, dx, q),
                    base + (dx * nz + dz) * np + q,
                    at(z, xs(dx), y, k),
                    start=start,
                )
                for dx in range(1, nx)
            ]

        own_parts = []
        for lane in range(2):
            mine = values(lane)
            own_parts.append(mine)
            pool[first, :, lane * (own // 2) : (lane + 1) * (own // 2)] = mine
            for q in (2 * lane, 2 * lane + 1):
                to_x(0, q)
                if relayed:
                    to_z(2, q)
                    to_z(1, q)
                else:
                    for dz in range(nz - 1, 0, -1):
                        to_z(dz, q)

        def source(dz, dx):
            return row_block(zback(dz) * nx + xs(nx - dx))

        gained(jnp.concatenate(own_parts, axis=1), row_block(r), fresh=True)
        if meanwhile is not None:
            meanwhile()

        passing = {
            (dz, q): to_x(dz, q, start=False) for q in range(np) for dz in range(1, nz)
        }

        def step(dz, q):
            arrived(piece(dz, 0, q), base + dz * np + q)
            for copy in passing[dz, q]:
                copy.start()

        if relayed:
            relays = [
                send(
                    piece(2, 0, q),
                    piece(3, 0, q),
                    base + 3 * np + q,
                    at(zs(1), x, y, k),
                    when=inner,
                    start=False,
                )
                for q in range(np)
            ]
            paced = [to_z(3, q, inner, start=False) for q in range(np)]

            @pl.when(inner)
            def _():
                for q in range(np):
                    arrived(piece(2, 0, q), base + 2 * np + q)
                    relays[q].start()
                    paced[q].start()
                    for copy in passing[2, q]:
                        copy.start()
                    step(1, q)
                    if q > 1:
                        step(3, q - 2)
                for q in range(np - 2, np):
                    step(3, q)

            @pl.when(outer)
            def _():
                for q in range(np + 2):
                    if q < np:
                        step(1, q)
                    if 0 < q <= np:
                        step(2, q - 1)
                    if q > 2:
                        step(3, q - 3)
                for q in range(np - 1, np):
                    step(3, q)
        else:
            for q in range(np):
                for dz in range(1, nz):
                    step(dz, q)
        for dz in range(1, nz):
            gained(pool[first + dz], source(dz, 0))
        if late is not None:
            late()
        for dz in range(nz):
            for dx in range(1, nx):
                for q in range(np):
                    arrived(piece(dz, dx, q), base + (dx * nz + dz) * np + q)
                gained(pool[first + dx * nz + dz], source(dz, dx))

    dz2t = (dh2t * slope2t).astype(LOW)
    half_own = own // 2

    def features_out():
        for d in range(1, ny):
            send(own_xt, own_xt, xt_base + c, at(z, x, ys(d), k))
        if nk > 1:
            send(own_xt, own_xt, xt_base + c, sibling)

    with jax.named_scope("back2_rows"):
        settle()
        receive(0, lambda lane: dz2t[:, lane * half_own : (lane + 1) * half_own], features_out)
    cbase = gbase[0] + 2 * s.n_col
    ybase = gbase[1] + 2 * s.n_col

    def lane_part(index, lane):
        return pl.ds(pl.multiple_of(index * own + lane * half_own, half_own), half_own)

    def held(place, lane):
        return xsend.at[place, :, pl.ds(lane * half_own, half_own)]

    def crecv(dy, lane):
        return v_all.at[0, dy * own : (dy + 1) * own, pl.ds(lane * half_own, half_own)]

    def yrecv(dy, lane):
        return crecv(dy + (ny if nk > 1 else 0), lane)

    column_totals = [None, None]
    with jax.named_scope("back2_cols"):
        for lane in range(2):
            for dy in range(ny - 1, -1, -1):
                if nk > 1:
                    there = held(dy, lane)
                    there[...] = acc[:, lane_part(ys(dy) * nk + 1 - k, lane)].astype(LOW)
                    send(there, crecv(dy, lane), cbase + 2 * dy + lane, sibling)
        for lane in range(2):
            for dy in range(ny - 1, -1, -1):
                here = acc[:, lane_part(ys(dy) * nk + k, lane)]
                if nk > 1:
                    arrived(crecv(dy, lane), cbase + 2 * dy + lane)
                    here = here + crecv(dy, lane)[...].astype(FULL)
                if dy:
                    there = held(ny + dy, lane)
                    there[...] = here.astype(LOW)
                    send(
                        there, yrecv(dy, lane), ybase + 2 * dy + lane, at(z, x, ys(dy), k)
                    )
                else:
                    column_totals[lane] = here
        for d in range(1, ny):
            source = ys(ny - d) * nk + k
            arrived(xt_all.at[source], xt_base + source)
            if nk > 1:
                send(xt_all.at[source], xt_all.at[source], xt_base + source, sibling)

    dy2_parts, dz1_parts = [], []

    def first_slopes(lane):
        lanes_q = slice(lane * half_own, (lane + 1) * half_own)
        total = column_totals[lane] + dz2t[:, lanes_q].astype(FULL)
        with jax.named_scope("y_wait"):
            for dy in range(1, ny):
                arrived(yrecv(dy, lane), ybase + 2 * dy + lane)
                total = total + yrecv(dy, lane)[...].astype(FULL)
        dy2_parts.append(total.astype(LOW))
        dz1_parts.append((dot(w2, dy2_parts[lane]) * slope1t[:, lanes_q]).astype(LOW))
        return dz1_parts[lane]

    lanes, plane = s.lanes, s.plane
    me = y * nx + x
    others = [(dx, dy) for dx in range(nx - 1, -1, -1) for dy in range(ny - 1, -1, -1) if dx or dy]

    def lane_block(index):
        return pl.ds(pl.multiple_of(index * lanes, lanes), lanes)

    class Total:
        def __init__(self, start, rows, mark=None, base=None):
            self.all = pl.ds(start, rows)
            self.start, self.rows = start, rows
            self.n = rows // plane
            self.short = pl.ds(start // plane, self.n)
            self.mark = rslots(1) if mark is None else mark
            self.base = rslots(3 * plane + nz) if base is None else base

        def piece(self, index):
            return pl.ds(pl.multiple_of(self.start + index * self.n, 16), self.n)

        def core_send(self, other):
            if nk > 1:
                half_send[self.all, :] = other.astype(LOW)
                send(half_send.at[self.all], half_recv.at[self.all], self.mark, sibling)

        def plane_send(self, mine):
            if nk > 1:
                arrived(half_recv.at[self.all], self.mark)
                mine = mine + half_recv[self.all, :].astype(FULL)
            half[self.all, :] = mine.astype(LOW)
            base = self.base
            for dx, dy in others:
                there = ys(dy) * nx + xs(dx)
                send(
                    half.at[self.piece(there)],
                    plane_recv.at[me, self.short],
                    base + me,
                    at(z, xs(dx), ys(dy), k),
                )
            plane_recv[me, self.short, :] = half[self.piece(me), :]

        def line_send(self):
            base = self.base
            for dx, dy in others:
                there = ys(dy) * nx + xs(dx)
                arrived(plane_recv.at[there, self.short], base + there)
            total = plane_recv[0, self.short, :].astype(FULL)
            for i in range(1, plane):
                total = total + plane_recv[i, self.short, :].astype(FULL)
            quarter[z, self.short, :] = total.astype(LOW)
            mine = quarter.at[z, self.short]
            base = self.base + plane
            for dz in range(nz - 1, 0, -1):
                send(mine, mine, base + z, at(zs(dz), x, y, k))

        def back_send(self):
            base = self.base + plane
            for dz in range(1, nz):
                arrived(quarter.at[zback(dz), self.short], base + zback(dz))
            total = quarter[0, self.short, :].astype(FULL)
            for i in range(1, nz):
                total = total + quarter[i, self.short, :].astype(FULL)
            base = self.base + plane + nz
            mine = fin.at[k, self.piece(me)]
            mine[...] = total.astype(LOW)
            for dx, dy in others:
                send(mine, mine, base + me, at(z, xs(dx), ys(dy), k))
            if nk > 1:
                send(mine, mine, base + plane + me, sibling)

        def back_forward(self):
            base = self.base + plane + nz
            for dx, dy in others:
                there = ys(dy) * nx + xs(dx)
                block = fin.at[k, self.piece(there)]
                arrived(block, base + there)
                if nk > 1:
                    send(block, block, base + plane + there, sibling)

        def end(self):
            base = self.base + plane + nz
            if nk > 1:
                for i in range(plane):
                    arrived(fin.at[1 - k, self.piece(i)], base + plane + i)

    def write(start, count):
        grad_ref[:, start : start + count, :] = fin[:, start : start + count, :]

    ones_at = [
        (gbase[i] + 2 * s.n_col + 2 * ny, wide[0] + i * (3 * plane + nz)) for i in range(2)
    ]
    ones_at += [(None, None)] * len(s.chunks)
    assert 2 * (3 * plane + nz) <= s.n_row * nh
    one = [
        Total(start, stop - start, *there) for (start, stop), there in zip(s.chunks, ones_at)
    ]
    two = Total(s.one_rows, s.two_rows)
    tail = s.two_rows - width - s.cls

    ones = jnp.ones((8, own), LOW)
    row = lax.broadcasted_iota(jnp.int32, (8, width), 0)
    lane_of = lax.broadcasted_iota(jnp.int32, (8, width), 1)
    bias_three = jnp.concatenate([dlt, jnp.zeros((width - s.cls, own), LOW)], axis=0)
    misc = jnp.where(row == 1, dot_nt(ones, dz2t), 0.0)
    misc = jnp.where(row == 2, dot_nt(ones, bias_three), misc)
    misc = jnp.where((row == 3) & (lane_of == 0), loss, misc)
    misc = jnp.where((row == 3) & (lane_of == 1), number, misc)
    mbase = rslots(1 + plane + nz)
    plane_base, line_base = mbase + 1, mbase + 1 + plane

    def early():
        misc_k[0] = misc
        if nk > 1:
            send(misc_k.at[0], misc_k.at[1], mbase, sibling)
        grad3t = dot(qt, h2)
        dy2t = jnp.concatenate(dy2_parts, axis=1)
        grad2 = dot_nt(h1t, dy2t)
        acc_two = jnp.concatenate(
            [grad2, grad3t] + ([jnp.zeros((tail, width), FULL)] if tail else []), axis=0
        )
        if nk > 1:
            first, second = acc_two[:, :lanes], acc_two[:, lanes:]
            low_core = (k == 0).astype(FULL)
            two.core_send(second * low_core + first * (1.0 - low_core))
            two.plane_send(first * low_core + second * (1.0 - low_core))
        else:
            two.plane_send(acc_two)
        here = misc_k[0]
        if nk > 1:
            arrived(misc_k.at[1], mbase)
            here = here + misc_k[1]
        misc_p[me] = here
        for dx, dy in others:
            send(misc_p.at[me], misc_p.at[me], plane_base + me, at(z, xs(dx), ys(dy), k))

    def late():
        two.line_send()
        for dx, dy in others:
            there = ys(dy) * nx + xs(dx)
            arrived(misc_p.at[there], plane_base + there)
        here = misc_p[0]
        for i in range(1, plane):
            here = here + misc_p[i]
        misc_z[z] = here
        for dz in range(1, nz):
            send(misc_z.at[z], misc_z.at[z], line_base + z, at(zs(dz), x, y, k))

    with jax.named_scope("back1_rows"):
        receive(1, first_slopes, early, late)
    with jax.named_scope("grad1"):
        dz1t = jnp.concatenate(dz1_parts, axis=1)
        acc[:, row_block(c)] += dz1t.astype(FULL)
        if nk > 1:
            for d in range(ny):
                source = ys(d) * nk + 1 - k
                arrived(xt_all.at[source], xt_base + source)

        low_core = (k == 0).astype(FULL)
        bias_one = dot_nt(ones, dz1t)[0:1, :]

        def grad_one(start, stop):
            total = None
            end = min(stop, s.feat_up)
            for i in range(s.n_col):
                here = acc[:, i * own : (i + 1) * own].astype(LOW)
                here = dot_nt(xt_all[i, start:end, :], here)
                total = here if total is None else total + here
            if end < stop:
                total = jnp.concatenate([total, jnp.zeros((stop - end, width), FULL)], axis=0)
            bias_at = s.feat - start
            if 0 <= bias_at < stop - start:
                places = lax.broadcasted_iota(jnp.int32, (stop - start, width), 0)
                total = jnp.where(places == bias_at, bias_one, total)
            if nk == 1:
                return None, total
            first, second = total[:, :lanes], total[:, lanes:]
            return (
                second * low_core + first * (1.0 - low_core),
                first * low_core + second * (1.0 - low_core),
            )

        waiting = None
        for chunk, (start, stop) in zip(one, s.chunks):
            other, mine = grad_one(start, stop)
            chunk.core_send(other)
            if waiting is not None:
                waiting()
            waiting = functools.partial(chunk.plane_send, mine)
        waiting()

    with jax.named_scope("sum_plane"):
        left = len(pending)
        two.back_send()
    with jax.named_scope("sum_line"):
        for chunk in one:
            chunk.line_send()
    with jax.named_scope("back_line"):
        for chunk in one:
            chunk.back_send()
        for dz in range(1, nz):
            arrived(misc_z.at[zback(dz)], line_base + zback(dz))
        misc = misc_z[0]
        for i in range(1, nz):
            misc = misc + misc_z[i]
        misc_ref[...] = jnp.where(row == 4, 1.0 / misc[3:4, 1:2], misc)
        settle(len(pending) - left)
    with jax.named_scope("back_plane"):
        for chunk in one:
            chunk.back_forward()
        two.back_forward()
        for chunk in one:
            chunk.end()
            write(chunk.start, chunk.rows)
        two.end()
        write(s.one_rows, s.two_rows)
    with jax.named_scope("settle"):
        settle()
    assert rcount[0] <= s.arrivals


def update_pieces(s):
    some = up(s.feat // 4, 16)
    cuts = [min(i * some, s.feat) for i in range(5)]
    one = [(0, start, stop - start) for start, stop in zip(cuts, cuts[1:]) if stop > start]
    return (*one, (1, 0, s.width), (2, 0, s.classes))


def adam_kernel(s, grad_ref, misc_ref, *refs):
    ins, outs, scratch = refs[:12], refs[12:26], refs[26:]
    bias_out, ends, *held = scratch[:-1]
    sem_out = scratch[-1]
    width, classes, lanes = s.width, s.classes, s.lanes
    grad_at = (0, s.one_rows, s.one_rows + width)

    stores = []

    def store(source, target):
        copy = pltpu.make_async_copy(source, target, sem_out.at[len(stores)])
        copy.start()
        stores.append(copy)

    total = misc_ref[3:4, 1:2]
    scale = misc_ref[4:5, 0:1]
    for (which, start, rows), target in zip(update_pieces(s), held):
        span = slice(start, start + rows)
        for i in range(s.nk):
            lane = slice(i * lanes, (i + 1) * lanes)
            first = grad_at[which] + start
            grad = grad_ref[i, first : first + up(rows, 16), :].astype(FULL)[:rows]
            weight, one, two = (ins[3 * which + j][span, lane] for j in range(3))
            for j, new in enumerate(adam_update(weight, one, two, grad * scale)):
                target[j, :, lane] = new
        for j in range(3):
            store(target.at[j], outs[3 * which + j].at[pl.ds(start, rows)])
    for i, size in enumerate((width, width, classes)):
        span = slice(i * width, i * width + size)
        weight, first, second = (ins[9 + j][span] for j in range(3))
        grad = misc_ref[i, :size]
        if not i:
            top = s.feat // 16 * 16
            rows = [grad_ref[j, top : top + 16, :].astype(FULL) for j in range(s.nk)]
            grad = jnp.concatenate([a[s.feat - top] for a in rows])
        new = adam_update(weight, first, second, grad * misc_ref[4, :size])
        for j in range(3):
            bias_out[j][span] = new[j]
    for j in range(3):
        store(bias_out[j], outs[9 + j])
    ends[0] = misc_ref[3:4, 0:1]
    ends[1] = total
    for i in range(2):
        store(ends.at[i], outs[12 + i])
    for copy in stores:
        copy.wait()


def shards(
    sizes,
    features,
    adjacency,
    occupancy,
    labels,
    train_mask,
    node_count,
    weight_one,
    weight_two,
    weight_three,
    biases,
    first_one,
    first_two,
    first_three,
    first_bias,
    second_one,
    second_two,
    second_three,
    second_bias,
):
    own, feat = features.shape
    width = weight_two.shape[0]
    classes = weight_three.shape[1]
    s = sizes(own, feat, width, classes)
    rows, cols = adjacency.shape
    lanes = s.lanes
    vmem = pl.BlockSpec(memory_space=pltpu.VMEM)
    smem = pl.BlockSpec(memory_space=pltpu.SMEM)
    anywhere = pl.BlockSpec(memory_space=pl.ANY)
    block = (own, width)
    small = (s.cls, own)
    shapes = [
        ((rows, cols), LOW),
        ((s.feat_up, width), LOW),
        ((s.cls, width), LOW),
        ((s.n_col, s.feat_up, own), LOW),
        ((2, s.n_col * own, width), LOW),
        ((2 * s.n_row, *block), LOW),
        ((max(2 * s.ny, s.n_row - s.nz), *block), LOW),
        ((max(1, s.nz - 1), *block), LOW),
        ((2, s.nz if s.relayed else max(1, s.nz - 1), *block), LOW),
        ((s.n_col, *small), LOW),
        ((s.n_row, *small), LOW),
        ((s.n_row, *small), LOW),
        ((s.n_row, *small), LOW),
        ((s.n_col, *small), LOW),
        ((s.n_col, *small), LOW),
        ((width, max(cols, s.nz * own)), FULL),
        ((s.grad_rows, lanes), LOW),
        ((s.grad_rows, lanes), LOW),
        ((s.grad_rows, lanes), LOW),
        ((s.plane, s.grad_rows // s.plane, lanes), LOW),
        ((s.nz, s.grad_rows // s.plane, lanes), LOW),
        ((s.nk, s.grad_rows, lanes), LOW),
        ((2, 8, width), FULL),
        ((s.plane, 8, width), FULL),
        ((s.nz, 8, width), FULL),
    ]
    bytes_held = sum(math.prod(shape) * jnp.dtype(kind).itemsize for shape, kind in shapes)
    limit = min(62, 16 + bytes_held // 2**20) * 2**20
    grads, misc = pl.pallas_call(
        functools.partial(kernel, s),
        out_shape=(
            pltpu.VMEM((s.nk, s.grad_rows, lanes), LOW),
            pltpu.VMEM((8, width), FULL),
        ),
        in_specs=[
            vmem,
            anywhere,
            smem,
            vmem,
            vmem,
            smem,
            vmem,
            vmem,
            vmem,
            vmem,
        ],
        out_specs=(vmem, vmem),
        scratch_shapes=[
            *[pltpu.VMEM(shape, kind) for shape, kind in shapes],
            pltpu.SemaphoreType.DMA((s.sends,)),
            pltpu.SemaphoreType.DMA((s.arrivals,)),
            pltpu.SemaphoreType.DMA((rows // SUB,)),
        ],
        compiler_params=pltpu.CompilerParams(
            collective_id=0, has_side_effects=True, vmem_limit_bytes=limit
        ),
        cost_estimate=pl.CostEstimate(
            flops=12 * rows * cols * width, bytes_accessed=2 * rows * cols, transcendentals=0
        ),
        name="step",
    )(
        *[
            pltpu.with_memory_space_constraint(a, pltpu.HBM)
            for a in (features.T, adjacency)
        ],
        pltpu.with_memory_space_constraint(occupancy, pltpu.HBM),
        *[
            pltpu.with_memory_space_constraint(a, pltpu.HBM)
            for a in (labels.reshape(1, own), train_mask.reshape(1, own))
        ],
        node_count,
        *[
            pltpu.with_memory_space_constraint(a, pltpu.HBM)
            for a in (weight_one, weight_two, weight_three.T, biases)
        ],
    )
    state = (
        weight_one,
        first_one,
        second_one,
        weight_two,
        first_two,
        second_two,
        weight_three.T,
        first_three.T,
        second_three.T,
        biases,
        first_bias,
        second_bias,
    )
    new = pl.pallas_call(
        functools.partial(adam_kernel, s),
        out_shape=(
            *[jax.ShapeDtypeStruct(a.shape, FULL) for a in state],
            jax.ShapeDtypeStruct((1, 1), FULL),
            jax.ShapeDtypeStruct((1, 1), FULL),
        ),
        in_specs=[vmem] * 14,
        out_specs=(anywhere,) * 14,
        scratch_shapes=[
            [pltpu.VMEM(biases.shape, FULL)] * 3,
            pltpu.VMEM((2, 1, 1), FULL),
            *[pltpu.VMEM((3, rows, width), FULL) for _, _, rows in update_pieces(s)],
            pltpu.SemaphoreType.DMA((3 * len(update_pieces(s)) + 5,)),
        ],
        compiler_params=pltpu.CompilerParams(vmem_limit_bytes=32 * 2**20),
        name="update",
    )(grads, misc, *state)
    return (
        *new[:6],
        *[a.T for a in new[6:9]],
        *new[9:12],
        new[12].reshape(()),
        new[13].reshape(()),
    )


def solution(mesh):
    placed = (
        P(("row", "col"), None),
        P("col", "row"),
        P("col", "row"),
        P(("row", "col")),
        P(("row", "col")),
        P(("row", "col")),
        *[P()] * 12,
    )
    sizes = functools.partial(Sizes, mesh.shape["row"], mesh.shape["col"])
    return jax.shard_map(
        functools.partial(shards, sizes),
        mesh=mesh,
        in_specs=placed,
        out_specs=(P(),) * 14,
        check_vma=False,
    )
```

```python
import functools
import math

import jax
import jax.numpy as jnp
from jax import lax
from jax.experimental import pallas as pl
from jax.experimental.pallas import tpu as pltpu
from jax.sharding import PartitionSpec as P

SUB = 512
STEP = 5


B_ONE = 0.5
B_TWO = 0.5
RATE = 0.05
DECAY = 0.01
EPSILON = 1e-08
SMOOTH = 0.1

MESH = pl.DeviceIdType.MESH
LOW = jnp.bfloat16
FULL = jnp.float32
GELU_A = 0.7978845608028654
GELU_B = 0.044715


def adam_update(weight, first, second, grad):
    first_new = B_ONE * first + (1.0 - B_ONE) * grad
    second_new = B_TWO * second + (1.0 - B_TWO) * grad * grad
    fix_one = 1.0 - B_ONE**STEP
    fix_two = 1.0 - B_TWO**STEP
    scaled = (first_new * (1.0 / fix_one)) / (jnp.sqrt(second_new * (1.0 / fix_two)) + EPSILON)
    return (first_new, second_new, weight - RATE * (scaled + DECAY * weight))


def up(value, unit):
    return -(-value // unit) * unit


def dot(left, right):
    return jnp.dot(left, right, preferred_element_type=FULL)


def dot_nt(left, right):
    return lax.dot_general(left, right, (((1,), (1,)), ((), ())), preferred_element_type=FULL)


def gelu_both(z):
    t = jnp.tanh(GELU_A * (z + GELU_B * z * z * z))
    half = 0.5 * (1.0 + t)
    slope = half + 0.5 * z * (1.0 - t * t) * (GELU_A * (1.0 + 3.0 * GELU_B * z * z))
    return z * half, slope


class Sizes:
    def __init__(self, n_row, n_col, own, feat, width, classes):
        self.n_row, self.n_col = n_row, n_col
        self.nk = 2 if n_col % 2 == 0 else 1
        self.ny = n_col // self.nk
        self.nx = self.ny if n_row % self.ny == 0 else 1
        self.nz = n_row // self.nx
        self.own, self.feat, self.width, self.classes = own, feat, width, classes
        self.feat_up = up(feat, 128)
        self.cls = up(classes, 16)
        self.plane = self.nx * self.ny
        self.one_rows = up(feat + 1, 16 * self.plane)
        self.two_rows = up(width + self.cls, 16 * self.plane)
        self.grad_rows = self.one_rows + self.two_rows
        self.lanes = width // self.nk
        units = self.one_rows // (16 * self.plane)
        chunks = min(3, units)
        cuts = [units * i // chunks * 16 * self.plane for i in range(chunks + 1)]
        self.chunks = list(zip(cuts, cuts[1:]))
        cuts = [own // 4 * i for i in range(5)]
        self.parts = [(start, stop - start) for start, stop in zip(cuts, cuts[1:])]
        self.nh = len(self.parts)
        self.relayed = self.nz == 4
        self.sends = 3 * (n_row + n_col) + 3 * self.plane
        wide = 2 * self.nh * (n_row + n_col)
        self.arrivals = wide + max(1, chunks - 1) * (1 + 3 * self.plane + self.nz) + 1 + self.plane + self.nz


def kernel(
    s,
    xt_ref,
    adj_ref,
    occ_ref,
    lab_ref,
    mask_ref,
    cnt_ref,
    w1_ref,
    w2_ref,
    w3t_ref,
    bias_ref,
    grad_ref,
    misc_ref,
    tile,
    w1b,
    w3t,
    xt_all,
    v_all,
    pool,
    xsend,
    zsend,
    zrecv,
    v3_all,
    p3send,
    p3recv,
    dl_all,
    q3send,
    q3recv,
    acc,
    half_send,
    half_recv,
    half,
    plane_recv,
    quarter,
    fin,
    misc_k,
    misc_p,
    misc_z,
    ssem,
    rsem,
    lsem,
):
    nx, ny, nz, nk = s.nx, s.ny, s.nz, s.nk
    own, width = s.own, s.width
    r, c = lax.axis_index("row"), lax.axis_index("col")
    z, x = r // nx, r % nx
    y, k = c // nk, c % nk

    def at(zz, xx, yy, kk):
        return (zz * nx + xx, yy * nk + kk)

    def xs(d):
        return lax.rem(x + d, nx)

    def ys(d):
        return lax.rem(y + d, ny)

    def zs(d):
        if nz & (nz - 1):
            return lax.rem(z + d, nz)
        there, bit = z, 1
        while bit < nz:
            if d & bit:
                there = there + bit - 2 * bit * lax.rem(there // bit, 2)
            bit *= 2
        return there

    def zback(d):
        return zs(d) if not nz & (nz - 1) else lax.rem(z + nz - d, nz)

    sibling = at(z, x, y, 1 - k)
    relayed = s.relayed
    is_inner = lax.rem((z + 1) // 2, 2)
    inner = is_inner == 1
    outer = is_inner == 0
    line = [dz for dz in range(nz - 1, -1, -1)]
    row_far = [(dz, dx) for dz in line for dx in range(nx - 1, -1, -1) if dz or dx]
    col_far = [(dy, dk) for dy in range(ny - 1, -1, -1) for dk in range(nk - 1, -1, -1) if dy or dk]

    def ks(d):
        return lax.rem(k + d, nk)


    rows, cols = tile.shape
    n_sub = rows // SUB
    loads = [
        pltpu.make_async_copy(
            adj_ref.at[pl.ds(a * SUB, SUB)], tile.at[pl.ds(a * SUB, SUB)], lsem.at[a]
        )
        for a in range(n_sub)
    ]
    for load in loads:
        load.start()

    peers = []
    for d in range(1, s.n_row):
        peers.append((lax.rem(r + d, s.n_row), c))
    for d in range(1, s.n_col):
        peers.append((r, lax.rem(c + d, s.n_col)))
    for dx in range(1, nx):
        for dy in range(1, ny):
            peers.append(at(z, xs(dx), ys(dy), k))
    barrier = pltpu.get_barrier_semaphore()
    for peer in peers:
        pl.semaphore_signal(barrier, inc=1, device_id=peer, device_id_type=MESH)

    free = list(range(s.sends))
    pending = []

    def send(src, dst, recv_slot, device, of=None, when=None, start=True):
        if not free:
            settle(len(pending) - 1)
        copy = pltpu.make_async_remote_copy(
            src_ref=src,
            dst_ref=dst,
            send_sem=ssem.at[free[0]],
            recv_sem=rsem.at[recv_slot],
            device_id=device,
            device_id_type=MESH,
        )
        if start:
            if when is None:
                copy.start()
            else:
                pl.when(when)(copy.start)
        pending.append((copy, free.pop(0), of, when))
        return copy

    def arrived(dst, recv_slot):
        pltpu.make_async_remote_copy(
            src_ref=dst,
            dst_ref=dst,
            send_sem=ssem.at[0],
            recv_sem=rsem.at[recv_slot],
            device_id=sibling,
            device_id_type=MESH,
        ).wait_recv()

    def settle(keep=0, of=None):
        done = [p for p in pending if p[2] == of] if of else pending[: len(pending) - keep]
        for item in done:
            if item[3] is None:
                item[0].wait_send()
            else:
                pl.when(item[3])(item[0].wait_send)
            free.append(item[1])
        left = [p for p in pending if all(p is not q for q in done)]
        pending[:] = left

    rcount = [0]

    def rslots(n):
        rcount[0] += n
        return rcount[0] - n

    def row_block(index):
        return pl.ds(pl.multiple_of(index * own, own), own)

    nh = s.nh

    def row_part(index, q):
        start, count = s.parts[q]
        return pl.ds(pl.multiple_of(index * own + start, count), count)

    def part(q):
        return pl.ds(*s.parts[q])

    def span_of(q):
        start, count = s.parts[q]
        return slice(start, start + count)

    valid_col = (lax.broadcasted_iota(jnp.int32, (own, width), 0) < cnt_ref[0]).astype(FULL)
    valid_low = valid_col.astype(LOW)
    valid_row = (lax.broadcasted_iota(jnp.int32, (1, own), 1) < cnt_ref[0]).astype(FULL)
    counted = mask_ref[...].astype(FULL) * valid_row

    prologue = jax.named_scope("prologue")
    prologue.__enter__()
    pad = s.feat_up - up(s.feat, 16) + 16
    own_xt = xt_all.at[c]
    own_xt[s.feat_up - pad :, :] = jnp.zeros((pad, own), LOW)
    w1b[s.feat_up - pad :, :] = jnp.zeros((pad, width), LOW)
    x_valid = (lax.broadcasted_iota(jnp.int32, (s.feat, own), 1) < cnt_ref[0]).astype(LOW)
    own_xt[: s.feat, :] = xt_ref[...] * x_valid
    w1b[: s.feat, :] = w1_ref[...].astype(LOW)
    y1 = lax.dot_general(
        own_xt[...], w1b[...], (((0,), (0,)), ((), ())), preferred_element_type=FULL
    ).astype(LOW)
    v_all[0, row_block(c), :] = y1

    wide = [rslots(s.n_row * nh) for _ in range(2)]
    gbase = [rslots(s.n_col * nh) for _ in range(2)]
    prologue.__exit__(None, None, None)

    def start_gather(hop, q, values):
        mine = v_all.at[hop, row_part(c, q)]
        if values is not None:
            mine[...] = values
        for d in range(1, ny):
            send(mine, mine, gbase[hop] + c * nh + q, at(z, x, ys(d), k))
        if nk > 1:
            send(mine, mine, gbase[hop] + c * nh + q, sibling)

    def complete_gather(hop, meanwhile):
        for q in range(nh):
            for d in range(1, ny):
                source = ys(ny - d) * nk + k
                block = v_all.at[hop, row_part(source, q)]
                arrived(block, gbase[hop] + source * nh + q)
                if nk > 1:
                    send(block, block, gbase[hop] + source * nh + q, sibling)
        for d in range(ny if nk > 1 else 0):
            if d == 1:
                meanwhile()
            source = ys(d) * nk + 1 - k
            for q in range(nh):
                arrived(v_all.at[hop, row_part(source, q)], gbase[hop] + source * nh + q)

    with jax.named_scope("barrier"):
        pl.semaphore_wait(barrier, len(peers))
    for q in range(nh):
        start_gather(0, q, None)

    if relayed:

        @pl.when(outer)
        def _():
            zrecv[:, 2] = jnp.zeros((2, own, width), LOW)

    w3t[...] = jnp.zeros_like(w3t)
    w3t[: s.classes, :] = w3t_ref[...].astype(LOW)
    w2 = w2_ref[...].astype(LOW)
    for a in range(n_sub):
        loads[a].wait()
        for b in range(cols // own):
            piece = tile[pl.ds(a * SUB, SUB), pl.ds(b * own, own)]
            cover = jnp.full((SUB, own), occ_ref[a, b].astype(FULL), FULL).astype(LOW)
            tile[pl.ds(a * SUB, SUB), pl.ds(b * own, own)] = piece * cover

    def spread(hop, finish):
        settle(of="hop")
        start_z = nz - 1
        begun = []
        late = [ys(d) * nk + 1 - k for d in range(1, ny)] if nk > 1 else []
        soon = [ys(d) * nk + k for d in range(ny)] + ([y * nk + 1 - k] if nk > 1 else [])

        def some(sources):
            first_rows = row_block(zs(start_z) * nx + xs(1))
            total = None
            for source in sources:
                here = dot(
                    tile[first_rows, row_block(source)], v_all[hop, row_block(source), :]
                )
                total = here if total is None else total + here
            return total

        split = nx > 1 and nk > 1 and ny > 1
        with jax.named_scope("gather_y"):
            complete_gather(hop, lambda: begun.append(some(soon)) if split else None)
        zbase = wide[hop]
        xbase = zbase + nz * nh
        order = list(range(nz - 1, -1, -1))

        def send_x(dz, dx, q):
            place = (dx - 1) * nz + dz
            send(
                xsend.at[place, part(q)],
                pool.at[hop * s.n_row + place, part(q)],
                xbase + place * nh + q,
                at(z, xs(dx), y, k),
                "hop",
            )

        sequence = []
        if relayed:
            sequence = [(3, 0), (3, 1), (2, 0), (3, 2), (2, 1), (3, 3), (1, 0), (2, 2), (1, 1), (2, 3), (1, 2), (1, 3), (0, 0), (0, 1), (0, 2), (0, 3)]
        else:
            for q in range(nh):
                sequence += [(dz, q) for dz in order if dz]
                if q:
                    sequence.append((0, q - 1))
            sequence.append((0, nh - 1))
        ready = set()
        with jax.named_scope("send_x"):
            for dz, q in sequence:
                for dx in range(1, nx):
                    if (dz, dx) not in ready:
                        ready.add((dz, dx))
                        rt = zs(dz) * nx + xs(dx)
                        if split and (dz, dx) == (start_z, 1):
                            here = begun[0] + some(late)
                        else:
                            here = dot(tile[row_block(rt), :], v_all[hop])
                        xsend[(dx - 1) * nz + dz] = here.astype(LOW)
                    send_x(dz, dx, q)
            for dz in order:
                acc[:, dz * own : (dz + 1) * own] = dot(
                    tile[row_block(zs(dz) * nx + x), :], v_all[hop]
                )

        def send_z(dz, q):
            rows_q = span_of(q)
            total = acc[rows_q, dz * own : (dz + 1) * own]
            for dx in range(1, nx):
                place = (dx - 1) * nz + dz
                arrived(pool.at[hop * s.n_row + place, part(q)], xbase + place * nh + q)
                total = total + pool[hop * s.n_row + place, rows_q, :].astype(FULL)
            if not dz:
                return total
            there, slot, mark = zs(dz), dz - 1, zbase + dz * nh + q
            if relayed and dz == 3:
                there = is_inner * zs(3) + (1 - is_inner) * zs(1)
                slot, mark = 3 - is_inner, zbase + 3 * nh * is_inner + q
            if relayed and dz == 2:

                @pl.when(inner)
                def _():
                    arrived(zrecv.at[hop, 3, part(q)], zbase + q)
                    handed = zrecv[hop, 3, rows_q, :].astype(FULL)
                    zsend[dz - 1, rows_q, :] = (total + handed).astype(LOW)

                @pl.when(outer)
                def _():
                    zsend[dz - 1, rows_q, :] = total.astype(LOW)

            else:
                zsend[dz - 1, rows_q, :] = total.astype(LOW)
            send(
                zsend.at[dz - 1, part(q)],
                zrecv.at[hop, slot, part(q)],
                mark,
                at(there, x, y, k),
                "hop",
            )
            return total

        totals = [None] * nh

        def sum_z(q):
            total = totals[q]
            rows_q = span_of(q)
            for dz in range(1, nz):
                there, mark = zrecv.at[hop, dz - 1, part(q)], zbase + dz * nh + q
                if relayed and dz == 3:
                    pl.when(inner)(functools.partial(arrived, there, mark))
                else:
                    arrived(there, mark)
                total = total + zrecv[hop, dz - 1, rows_q, :].astype(FULL)
            finish(q, total)

        with jax.named_scope("send_z"):
            for dz, q in sequence[:-1]:
                totals[q] = send_z(dz, q)
                if not dz:
                    with jax.named_scope("sum_z0"):
                        sum_z(q)
        with jax.named_scope("sum_z1"):
            totals[nh - 1] = send_z(0, nh - 1)
            sum_z(nh - 1)

    bias = [bias_ref[i * width : (i + 1) * width].reshape(1, width) for i in range(2)]
    slopes, acts = [None] * nh, [None] * nh

    def first_done(q, total):
        rows_q = span_of(q)
        z1 = total + v_all[0, row_part(c, q), :].astype(FULL) + bias[0]
        act, slope = gelu_both(z1)
        h1 = act.astype(LOW) * valid_low[rows_q]
        start_gather(1, q, dot(h1, w2).astype(LOW))
        acts[q], slopes[q] = h1, slope * valid_col[rows_q]

    spread(0, first_done)
    h1t = jnp.concatenate(acts, axis=0).astype(FULL).T.astype(LOW)
    slope1t = jnp.concatenate(slopes, axis=0).T

    xt_base = gbase[1] + s.n_col

    def second_done(q, total):
        rows_q = span_of(q)
        z2 = total + v_all[1, row_part(c, q), :].astype(FULL) + bias[1]
        act, slope = gelu_both(z2)
        acts[q] = act.astype(LOW) * valid_low[rows_q]
        slopes[q] = slope * valid_col[rows_q]
        ends = span_of(q).stop
        if ends % (own // 2) == 0:
            lane = 2 * ends // own - 1
            some = [act for i, act in enumerate(acts[: q + 1]) if span_of(i).start >= ends - own // 2]
            some = jnp.concatenate(some, axis=0)
            y3t = dot_nt(w3t[...], some).astype(LOW)
            mine = v3_half(c, lane)
            mine[...] = y3t
            for dy, dk in col_far:
                send(mine, mine, gbase[0] + 2 * c + lane, (r, ys(dy) * nk + ks(dk)))

    def v3_half(index, lane):
        return v3_all.at[index, :, pl.ds(lane * (own // 2), own // 2)]

    spread(1, second_done)
    h2 = jnp.concatenate(acts, axis=0)

    with jax.named_scope("hop3_gather"):
        slope2t = jnp.concatenate(slopes, axis=0).T
        settle(s.n_col - 1)
        for lane in range(2):
            for dy, dk in reversed(col_far):
                source = ys(ny - dy) * nk + ks(nk - dk)
                arrived(v3_half(source, lane), gbase[0] + 2 * source + lane)
    with jax.named_scope("hop3_sum"):
        pbase = wide[0]
        v3 = jnp.concatenate([v3_all[i] for i in range(s.n_col)], axis=1)
        for dz, dx in row_far:
            place = dz * nx + dx
            rt = zs(dz) * nx + xs(dx)
            p3send[place] = dot_nt(v3, tile[row_block(rt), :]).astype(LOW)
            send(p3send.at[place], p3recv.at[place], pbase + place, (rt, c))
        total = dot_nt(v3, tile[row_block(r), :])
        for dz, dx in reversed(row_far):
            place = dz * nx + dx
            arrived(p3recv.at[place], pbase + place)
            total = total + p3recv[place].astype(FULL)
    total = total + v3_all[c].astype(FULL)

    place = lax.broadcasted_iota(jnp.int32, (s.cls, own), 0)
    real = place < s.classes
    on_diag = lax.broadcasted_iota(jnp.int32, (s.cls, s.classes), 0) == lax.broadcasted_iota(
        jnp.int32, (s.cls, s.classes), 1
    )
    bias3 = jnp.sum(
        jnp.where(on_diag, bias_ref[2 * width :].reshape(1, s.classes), 0.0), axis=1, keepdims=True
    )
    logits = jnp.where(real, total + bias3, -1e30)
    shifted = logits - jnp.max(logits, axis=0, keepdims=True)
    weight = jnp.where(real, jnp.exp(shifted), 0.0)
    norm = jnp.sum(weight, axis=0, keepdims=True)
    logp = shifted - jnp.log(norm)
    target = jnp.where(place == lab_ref[...], 1.0 - SMOOTH, 0.0) + SMOOTH / s.classes
    target = jnp.where(real, target, 0.0)
    row_loss = -jnp.sum(jnp.where(real, target * logp, 0.0), axis=0, keepdims=True)
    loss = jnp.sum(row_loss * counted, axis=1, keepdims=True)
    number = jnp.sum(counted, axis=1, keepdims=True)
    dlt = ((weight / norm - target) * counted).astype(LOW)

    with jax.named_scope("back3_gather"):
        base = wide[1]
        mine = dl_all.at[r]
        mine[...] = dlt
        for dz, dx in row_far:
            send(mine, mine, base + r, (zs(dz) * nx + xs(dx), c))
        here = dot(dlt, tile[row_block(r), :])
        for dz, dx in reversed(row_far):
            source = zback(dz) * nx + xs(nx - dx)
            arrived(dl_all.at[source], base + source)
            here = here + dot(dl_all[source], tile[row_block(source), :])
        acc[: s.cls, :cols] = here
    with jax.named_scope("back3_sum"):
        qbase = gbase[1]
        for dy, dk in col_far:
            place = dy * nk + dk
            ct = ys(dy) * nk + ks(dk)
            q3send[place] = acc[: s.cls, row_block(ct)].astype(LOW)
            send(q3send.at[place], q3recv.at[place], qbase + place, (r, ct))
        total = dlt.astype(FULL) + acc[: s.cls, row_block(c)]
        for dy, dk in reversed(col_far):
            place = dy * nk + dk
            arrived(q3recv.at[place], qbase + place)
            total = total + q3recv[place].astype(FULL)
    qt = total.astype(LOW)
    dh2t = lax.dot_general(
        w3t[...], qt, (((0,), (0,)), ((), ())), preferred_element_type=FULL
    )
    step_cols = min(cols, 1024)

    def gained(values, block, fresh=False):
        for j in range(0, cols, step_cols):
            here = dot(values, tile[block, j : j + step_cols])
            if fresh:
                acc[:, j : j + step_cols] = here
            else:
                acc[:, j : j + step_cols] += here

    def halves(lane, row):
        return (
            pl.ds(row * (width // 2), width // 2),
            pl.ds(lane * (own // 2), own // 2),
        )

    quarters = [(lane, row) for lane in range(2) for row in range(2)]
    def receive(hop, values, meanwhile=None, late=None):
        base, np = wide[hop], len(quarters)
        first = hop * s.n_row

        def piece(dz, dx, q):
            return pool.at[(first + dx * nz + dz, *halves(*quarters[q]))]

        def to_z(dz, q, when=None, start=True):
            return send(
                piece(0, 0, q),
                piece(dz, 0, q),
                base + dz * np + q,
                at(zs(dz), x, y, k),
                when=when,
                start=start,
            )

        def to_x(dz, q, start=True):
            return [
                send(
                    piece(dz, 0, q),
                    piece(dz, dx, q),
                    base + (dx * nz + dz) * np + q,
                    at(z, xs(dx), y, k),
                    start=start,
                )
                for dx in range(1, nx)
            ]

        own_parts = []
        for lane in range(2):
            mine = values(lane)
            own_parts.append(mine)
            pool[first, :, lane * (own // 2) : (lane + 1) * (own // 2)] = mine
            for q in (2 * lane, 2 * lane + 1):
                to_x(0, q)
                if relayed:
                    to_z(2, q)
                    to_z(1, q)
                else:
                    for dz in range(nz - 1, 0, -1):
                        to_z(dz, q)

        def source(dz, dx):
            return row_block(zback(dz) * nx + xs(nx - dx))

        gained(jnp.concatenate(own_parts, axis=1), row_block(r), fresh=True)
        if meanwhile is not None:
            meanwhile()

        passing = {
            (dz, q): to_x(dz, q, start=False) for q in range(np) for dz in range(1, nz)
        }

        def step(dz, q):
            arrived(piece(dz, 0, q), base + dz * np + q)
            for copy in passing[dz, q]:
                copy.start()

        if relayed:
            relays = [
                send(
                    piece(2, 0, q),
                    piece(3, 0, q),
                    base + 3 * np + q,
                    at(zs(1), x, y, k),
                    when=inner,
                    start=False,
                )
                for q in range(np)
            ]
            paced = [to_z(3, q, inner, start=False) for q in range(np)]

            @pl.when(inner)
            def _():
                for q in range(np):
                    arrived(piece(2, 0, q), base + 2 * np + q)
                    relays[q].start()
                    paced[q].start()
                    for copy in passing[2, q]:
                        copy.start()
                    step(1, q)
                    if q > 1:
                        step(3, q - 2)
                for q in range(np - 2, np):
                    step(3, q)

            @pl.when(outer)
            def _():
                for q in range(np + 2):
                    if q < np:
                        step(1, q)
                    if 0 < q <= np:
                        step(2, q - 1)
                    if q > 2:
                        step(3, q - 3)
                for q in range(np - 1, np):
                    step(3, q)
        else:
            for q in range(np):
                for dz in range(1, nz):
                    step(dz, q)
        for dz in range(1, nz):
            gained(pool[first + dz], source(dz, 0))
        if late is not None:
            late()
        for dz in range(nz):
            for dx in range(1, nx):
                for q in range(np):
                    arrived(piece(dz, dx, q), base + (dx * nz + dz) * np + q)
                gained(pool[first + dx * nz + dz], source(dz, dx))

    dz2t = (dh2t * slope2t).astype(LOW)
    half_own = own // 2

    def features_out():
        for d in range(1, ny):
            send(own_xt, own_xt, xt_base + c, at(z, x, ys(d), k))
        if nk > 1:
            send(own_xt, own_xt, xt_base + c, sibling)

    with jax.named_scope("back2_rows"):
        settle()
        receive(0, lambda lane: dz2t[:, lane * half_own : (lane + 1) * half_own], features_out)
    cbase = gbase[0] + 2 * s.n_col
    ybase = gbase[1] + 2 * s.n_col

    def lane_part(index, lane):
        return pl.ds(pl.multiple_of(index * own + lane * half_own, half_own), half_own)

    def held(place, lane):
        return xsend.at[place, :, pl.ds(lane * half_own, half_own)]

    def crecv(dy, lane):
        return v_all.at[0, dy * own : (dy + 1) * own, pl.ds(lane * half_own, half_own)]

    def yrecv(dy, lane):
        return crecv(dy + (ny if nk > 1 else 0), lane)

    column_totals = [None, None]
    with jax.named_scope("back2_cols"):
        for lane in range(2):
            for dy in range(ny - 1, -1, -1):
                if nk > 1:
                    there = held(dy, lane)
                    there[...] = acc[:, lane_part(ys(dy) * nk + 1 - k, lane)].astype(LOW)
                    send(there, crecv(dy, lane), cbase + 2 * dy + lane, sibling)
        for lane in range(2):
            for dy in range(ny - 1, -1, -1):
                here = acc[:, lane_part(ys(dy) * nk + k, lane)]
                if nk > 1:
                    arrived(crecv(dy, lane), cbase + 2 * dy + lane)
                    here = here + crecv(dy, lane)[...].astype(FULL)
                if dy:
                    there = held(ny + dy, lane)
                    there[...] = here.astype(LOW)
                    send(
                        there, yrecv(dy, lane), ybase + 2 * dy + lane, at(z, x, ys(dy), k)
                    )
                else:
                    column_totals[lane] = here
        for d in range(1, ny):
            source = ys(ny - d) * nk + k
            arrived(xt_all.at[source], xt_base + source)
            if nk > 1:
                send(xt_all.at[source], xt_all.at[source], xt_base + source, sibling)

    dy2_parts, dz1_parts = [], []

    def first_slopes(lane):
        lanes_q = slice(lane * half_own, (lane + 1) * half_own)
        total = column_totals[lane] + dz2t[:, lanes_q].astype(FULL)
        with jax.named_scope("y_wait"):
            for dy in range(1, ny):
                arrived(yrecv(dy, lane), ybase + 2 * dy + lane)
                total = total + yrecv(dy, lane)[...].astype(FULL)
        dy2_parts.append(total.astype(LOW))
        dz1_parts.append((dot(w2, dy2_parts[lane]) * slope1t[:, lanes_q]).astype(LOW))
        return dz1_parts[lane]

    lanes, plane = s.lanes, s.plane
    me = y * nx + x
    others = [(dx, dy) for dx in range(nx - 1, -1, -1) for dy in range(ny - 1, -1, -1) if dx or dy]

    def lane_block(index):
        return pl.ds(pl.multiple_of(index * lanes, lanes), lanes)

    class Total:
        def __init__(self, start, rows, mark=None, base=None):
            self.all = pl.ds(start, rows)
            self.start, self.rows = start, rows
            self.n = rows // plane
            self.short = pl.ds(start // plane, self.n)
            self.mark = rslots(1) if mark is None else mark
            self.base = rslots(3 * plane + nz) if base is None else base

        def piece(self, index):
            return pl.ds(pl.multiple_of(self.start + index * self.n, 16), self.n)

        def core_send(self, other):
            if nk > 1:
                half_send[self.all, :] = other.astype(LOW)
                send(half_send.at[self.all], half_recv.at[self.all], self.mark, sibling)

        def plane_send(self, mine):
            if nk > 1:
                arrived(half_recv.at[self.all], self.mark)
                mine = mine + half_recv[self.all, :].astype(FULL)
            half[self.all, :] = mine.astype(LOW)
            base = self.base
            for dx, dy in others:
                there = ys(dy) * nx + xs(dx)
                send(
                    half.at[self.piece(there)],
                    plane_recv.at[me, self.short],
                    base + me,
                    at(z, xs(dx), ys(dy), k),
                )
            plane_recv[me, self.short, :] = half[self.piece(me), :]

        def line_send(self):
            base = self.base
            for dx, dy in others:
                there = ys(dy) * nx + xs(dx)
                arrived(plane_recv.at[there, self.short], base + there)
            total = plane_recv[0, self.short, :].astype(FULL)
            for i in range(1, plane):
                total = total + plane_recv[i, self.short, :].astype(FULL)
            quarter[z, self.short, :] = total.astype(LOW)
            mine = quarter.at[z, self.short]
            base = self.base + plane
            for dz in range(nz - 1, 0, -1):
                send(mine, mine, base + z, at(zs(dz), x, y, k))

        def back_send(self):
            base = self.base + plane
            for dz in range(1, nz):
                arrived(quarter.at[zback(dz), self.short], base + zback(dz))
            total = quarter[0, self.short, :].astype(FULL)
            for i in range(1, nz):
                total = total + quarter[i, self.short, :].astype(FULL)
            base = self.base + plane + nz
            mine = fin.at[k, self.piece(me)]
            mine[...] = total.astype(LOW)
            for dx, dy in others:
                send(mine, mine, base + me, at(z, xs(dx), ys(dy), k))
            if nk > 1:
                send(mine, mine, base + plane + me, sibling)

        def back_forward(self):
            base = self.base + plane + nz
            for dx, dy in others:
                there = ys(dy) * nx + xs(dx)
                block = fin.at[k, self.piece(there)]
                arrived(block, base + there)
                if nk > 1:
                    send(block, block, base + plane + there, sibling)

        def end(self):
            base = self.base + plane + nz
            if nk > 1:
                for i in range(plane):
                    arrived(fin.at[1 - k, self.piece(i)], base + plane + i)

    def write(start, count):
        grad_ref[:, start : start + count, :] = fin[:, start : start + count, :]

    ones_at = [
        (gbase[i] + 2 * s.n_col + 2 * ny, wide[0] + i * (3 * plane + nz)) for i in range(2)
    ]
    ones_at += [(None, None)] * len(s.chunks)
    assert 2 * (3 * plane + nz) <= s.n_row * nh
    one = [
        Total(start, stop - start, *there) for (start, stop), there in zip(s.chunks, ones_at)
    ]
    two = Total(s.one_rows, s.two_rows)
    tail = s.two_rows - width - s.cls

    ones = jnp.ones((8, own), LOW)
    row = lax.broadcasted_iota(jnp.int32, (8, width), 0)
    lane_of = lax.broadcasted_iota(jnp.int32, (8, width), 1)
    bias_three = jnp.concatenate([dlt, jnp.zeros((width - s.cls, own), LOW)], axis=0)
    misc = jnp.where(row == 1, dot_nt(ones, dz2t), 0.0)
    misc = jnp.where(row == 2, dot_nt(ones, bias_three), misc)
    misc = jnp.where((row == 3) & (lane_of == 0), loss, misc)
    misc = jnp.where((row == 3) & (lane_of == 1), number, misc)
    mbase = rslots(1 + plane + nz)
    plane_base, line_base = mbase + 1, mbase + 1 + plane

    def early():
        misc_k[0] = misc
        if nk > 1:
            send(misc_k.at[0], misc_k.at[1], mbase, sibling)
        grad3t = dot(qt, h2)
        dy2t = jnp.concatenate(dy2_parts, axis=1)
        grad2 = dot_nt(h1t, dy2t)
        acc_two = jnp.concatenate(
            [grad2, grad3t] + ([jnp.zeros((tail, width), FULL)] if tail else []), axis=0
        )
        if nk > 1:
            first, second = acc_two[:, :lanes], acc_two[:, lanes:]
            low_core = (k == 0).astype(FULL)
            two.core_send(second * low_core + first * (1.0 - low_core))
            two.plane_send(first * low_core + second * (1.0 - low_core))
        else:
            two.plane_send(acc_two)
        here = misc_k[0]
        if nk > 1:
            arrived(misc_k.at[1], mbase)
            here = here + misc_k[1]
        misc_p[me] = here
        for dx, dy in others:
            send(misc_p.at[me], misc_p.at[me], plane_base + me, at(z, xs(dx), ys(dy), k))

    def late():
        two.line_send()
        for dx, dy in others:
            there = ys(dy) * nx + xs(dx)
            arrived(misc_p.at[there], plane_base + there)
        here = misc_p[0]
        for i in range(1, plane):
            here = here + misc_p[i]
        misc_z[z] = here
        for dz in range(1, nz):
            send(misc_z.at[z], misc_z.at[z], line_base + z, at(zs(dz), x, y, k))

    with jax.named_scope("back1_rows"):
        receive(1, first_slopes, early, late)
    with jax.named_scope("grad1"):
        dz1t = jnp.concatenate(dz1_parts, axis=1)
        acc[:, row_block(c)] += dz1t.astype(FULL)
        if nk > 1:
            for d in range(ny):
                source = ys(d) * nk + 1 - k
                arrived(xt_all.at[source], xt_base + source)

        low_core = (k == 0).astype(FULL)
        bias_one = dot_nt(ones, dz1t)[0:1, :]

        def grad_one(start, stop):
            total = None
            end = min(stop, s.feat_up)
            for i in range(s.n_col):
                here = acc[:, i * own : (i + 1) * own].astype(LOW)
                here = dot_nt(xt_all[i, start:end, :], here)
                total = here if total is None else total + here
            if end < stop:
                total = jnp.concatenate([total, jnp.zeros((stop - end, width), FULL)], axis=0)
            bias_at = s.feat - start
            if 0 <= bias_at < stop - start:
                places = lax.broadcasted_iota(jnp.int32, (stop - start, width), 0)
                total = jnp.where(places == bias_at, bias_one, total)
            if nk == 1:
                return None, total
            first, second = total[:, :lanes], total[:, lanes:]
            return (
                second * low_core + first * (1.0 - low_core),
                first * low_core + second * (1.0 - low_core),
            )

        waiting = None
        for chunk, (start, stop) in zip(one, s.chunks):
            other, mine = grad_one(start, stop)
            chunk.core_send(other)
            if waiting is not None:
                waiting()
            waiting = functools.partial(chunk.plane_send, mine)
        waiting()

    with jax.named_scope("sum_plane"):
        left = len(pending)
        two.back_send()
    with jax.named_scope("sum_line"):
        for chunk in one:
            chunk.line_send()
    with jax.named_scope("back_line"):
        for chunk in one:
            chunk.back_send()
        for dz in range(1, nz):
            arrived(misc_z.at[zback(dz)], line_base + zback(dz))
        misc = misc_z[0]
        for i in range(1, nz):
            misc = misc + misc_z[i]
        misc_ref[...] = jnp.where(row == 4, 1.0 / misc[3:4, 1:2], misc)
        settle(len(pending) - left)
    with jax.named_scope("back_plane"):
        for chunk in one:
            chunk.back_forward()
        two.back_forward()
        for chunk in one:
            chunk.end()
            write(chunk.start, chunk.rows)
        two.end()
        write(s.one_rows, s.two_rows)
    with jax.named_scope("settle"):
        settle()
    assert rcount[0] <= s.arrivals


def update_pieces(s):
    some = up(s.feat // 4, 16)
    cuts = [min(i * some, s.feat) for i in range(5)]
    one = [(0, start, stop - start) for start, stop in zip(cuts, cuts[1:]) if stop > start]
    return (*one, (1, 0, s.width), (2, 0, s.classes))


def adam_kernel(s, grad_ref, misc_ref, *refs):
    ins, outs, scratch = refs[:12], refs[12:26], refs[26:]
    bias_out, ends, *held = scratch[:-1]
    sem_out = scratch[-1]
    width, classes, lanes = s.width, s.classes, s.lanes
    grad_at = (0, s.one_rows, s.one_rows + width)

    stores = []

    def store(source, target):
        copy = pltpu.make_async_copy(source, target, sem_out.at[len(stores)])
        copy.start()
        stores.append(copy)

    total = misc_ref[3:4, 1:2]
    scale = misc_ref[4:5, 0:1]
    for (which, start, rows), target in zip(update_pieces(s), held):
        span = slice(start, start + rows)
        for i in range(s.nk):
            lane = slice(i * lanes, (i + 1) * lanes)
            first = grad_at[which] + start
            grad = grad_ref[i, first : first + up(rows, 16), :].astype(FULL)[:rows]
            weight, one, two = (ins[3 * which + j][span, lane] for j in range(3))
            for j, new in enumerate(adam_update(weight, one, two, grad * scale)):
                target[j, :, lane] = new
        for j in range(3):
            store(target.at[j], outs[3 * which + j].at[pl.ds(start, rows)])
    for i, size in enumerate((width, width, classes)):
        span = slice(i * width, i * width + size)
        weight, first, second = (ins[9 + j][span] for j in range(3))
        grad = misc_ref[i, :size]
        if not i:
            top = s.feat // 16 * 16
            rows = [grad_ref[j, top : top + 16, :].astype(FULL) for j in range(s.nk)]
            grad = jnp.concatenate([a[s.feat - top] for a in rows])
        new = adam_update(weight, first, second, grad * misc_ref[4, :size])
        for j in range(3):
            bias_out[j][span] = new[j]
    for j in range(3):
        store(bias_out[j], outs[9 + j])
    ends[0] = misc_ref[3:4, 0:1]
    ends[1] = total
    for i in range(2):
        store(ends.at[i], outs[12 + i])
    for copy in stores:
        copy.wait()


def shards(
    sizes,
    features,
    adjacency,
    occupancy,
    labels,
    train_mask,
    node_count,
    weight_one,
    weight_two,
    weight_three,
    biases,
    first_one,
    first_two,
    first_three,
    first_bias,
    second_one,
    second_two,
    second_three,
    second_bias,
):
    own, feat = features.shape
    width = weight_two.shape[0]
    classes = weight_three.shape[1]
    s = sizes(own, feat, width, classes)
    rows, cols = adjacency.shape
    lanes = s.lanes
    vmem = pl.BlockSpec(memory_space=pltpu.VMEM)
    smem = pl.BlockSpec(memory_space=pltpu.SMEM)
    anywhere = pl.BlockSpec(memory_space=pl.ANY)
    block = (own, width)
    small = (s.cls, own)
    shapes = [
        ((rows, cols), LOW),
        ((s.feat_up, width), LOW),
        ((s.cls, width), LOW),
        ((s.n_col, s.feat_up, own), LOW),
        ((2, s.n_col * own, width), LOW),
        ((2 * s.n_row, *block), LOW),
        ((max(2 * s.ny, s.n_row - s.nz), *block), LOW),
        ((max(1, s.nz - 1), *block), LOW),
        ((2, s.nz if s.relayed else max(1, s.nz - 1), *block), LOW),
        ((s.n_col, *small), LOW),
        ((s.n_row, *small), LOW),
        ((s.n_row, *small), LOW),
        ((s.n_row, *small), LOW),
        ((s.n_col, *small), LOW),
        ((s.n_col, *small), LOW),
        ((width, max(cols, s.nz * own)), FULL),
        ((s.grad_rows, lanes), LOW),
        ((s.grad_rows, lanes), LOW),
        ((s.grad_rows, lanes), LOW),
        ((s.plane, s.grad_rows // s.plane, lanes), LOW),
        ((s.nz, s.grad_rows // s.plane, lanes), LOW),
        ((s.nk, s.grad_rows, lanes), LOW),
        ((2, 8, width), FULL),
        ((s.plane, 8, width), FULL),
        ((s.nz, 8, width), FULL),
    ]
    bytes_held = sum(math.prod(shape) * jnp.dtype(kind).itemsize for shape, kind in shapes)
    limit = min(62, 16 + bytes_held // 2**20) * 2**20
    grads, misc = pl.pallas_call(
        functools.partial(kernel, s),
        out_shape=(
            pltpu.VMEM((s.nk, s.grad_rows, lanes), LOW),
            pltpu.VMEM((8, width), FULL),
        ),
        in_specs=[
            vmem,
            anywhere,
            smem,
            vmem,
            vmem,
            smem,
            vmem,
            vmem,
            vmem,
            vmem,
        ],
        out_specs=(vmem, vmem),
        scratch_shapes=[
            *[pltpu.VMEM(shape, kind) for shape, kind in shapes],
            pltpu.SemaphoreType.DMA((s.sends,)),
            pltpu.SemaphoreType.DMA((s.arrivals,)),
            pltpu.SemaphoreType.DMA((rows // SUB,)),
        ],
        compiler_params=pltpu.CompilerParams(
            collective_id=0, has_side_effects=True, vmem_limit_bytes=limit
        ),
        cost_estimate=pl.CostEstimate(
            flops=12 * rows * cols * width, bytes_accessed=2 * rows * cols, transcendentals=0
        ),
        name="step",
    )(
        *[
            pltpu.with_memory_space_constraint(a, pltpu.HBM)
            for a in (features.T, adjacency)
        ],
        pltpu.with_memory_space_constraint(occupancy, pltpu.HBM),
        *[
            pltpu.with_memory_space_constraint(a, pltpu.HBM)
            for a in (labels.reshape(1, own), train_mask.reshape(1, own))
        ],
        node_count,
        *[
            pltpu.with_memory_space_constraint(a, pltpu.HBM)
            for a in (weight_one, weight_two, weight_three.T, biases)
        ],
    )
    state = (
        weight_one,
        first_one,
        second_one,
        weight_two,
        first_two,
        second_two,
        weight_three.T,
        first_three.T,
        second_three.T,
        biases,
        first_bias,
        second_bias,
    )
    new = pl.pallas_call(
        functools.partial(adam_kernel, s),
        out_shape=(
            *[jax.ShapeDtypeStruct(a.shape, FULL) for a in state],
            jax.ShapeDtypeStruct((1, 1), FULL),
            jax.ShapeDtypeStruct((1, 1), FULL),
        ),
        in_specs=[vmem] * 14,
        out_specs=(anywhere,) * 14,
        scratch_shapes=[
            [pltpu.VMEM(biases.shape, FULL)] * 3,
            pltpu.VMEM((2, 1, 1), FULL),
            *[pltpu.VMEM((3, rows, width), FULL) for _, _, rows in update_pieces(s)],
            pltpu.SemaphoreType.DMA((3 * len(update_pieces(s)) + 5,)),
        ],
        compiler_params=pltpu.CompilerParams(vmem_limit_bytes=32 * 2**20),
        name="update",
    )(grads, misc, *state)
    return (
        *new[:6],
        *[a.T for a in new[6:9]],
        *new[9:12],
        new[12].reshape(()),
        new[13].reshape(()),
    )


def solution(mesh):
    placed = (
        P(("row", "col"), None),
        P("col", "row"),
        P("col", "row"),
        P(("row", "col")),
        P(("row", "col")),
        P(("row", "col")),
        *[P()] * 12,
    )
    sizes = functools.partial(Sizes, mesh.shape["row"], mesh.shape["col"])
    return jax.shard_map(
        functools.partial(shards, sizes),
        mesh=mesh,
        in_specs=placed,
        out_specs=(P(),) * 14,
        check_vma=False,
    )
```

```python
import functools
import math

import jax
import jax.numpy as jnp
from jax import lax
from jax.experimental import pallas as pl
from jax.experimental.pallas import tpu as pltpu
from jax.sharding import PartitionSpec as P

SUB = 512
STEP = 5


B_ONE = 0.5
B_TWO = 0.5
RATE = 0.05
DECAY = 0.01
EPSILON = 1e-08
SMOOTH = 0.1

MESH = pl.DeviceIdType.MESH
LOW = jnp.bfloat16
FULL = jnp.float32
GELU_A = 0.7978845608028654
GELU_B = 0.044715


def adam_update(weight, first, second, grad):
    first_new = B_ONE * first + (1.0 - B_ONE) * grad
    second_new = B_TWO * second + (1.0 - B_TWO) * grad * grad
    fix_one = 1.0 - B_ONE**STEP
    fix_two = 1.0 - B_TWO**STEP
    scaled = (first_new * (1.0 / fix_one)) / (jnp.sqrt(second_new * (1.0 / fix_two)) + EPSILON)
    return (first_new, second_new, weight - RATE * (scaled + DECAY * weight))


def up(value, unit):
    return -(-value // unit) * unit


def dot(left, right):
    return jnp.dot(left, right, preferred_element_type=FULL)


def dot_nt(left, right):
    return lax.dot_general(left, right, (((1,), (1,)), ((), ())), preferred_element_type=FULL)


def gelu_both(z):
    t = jnp.tanh(GELU_A * (z + GELU_B * z * z * z))
    half = 0.5 * (1.0 + t)
    slope = half + 0.5 * z * (1.0 - t * t) * (GELU_A * (1.0 + 3.0 * GELU_B * z * z))
    return z * half, slope


class Sizes:
    def __init__(self, n_row, n_col, own, feat, width, classes):
        self.n_row, self.n_col = n_row, n_col
        self.nk = 2 if n_col % 2 == 0 else 1
        self.ny = n_col // self.nk
        self.nx = self.ny if n_row % self.ny == 0 else 1
        self.nz = n_row // self.nx
        self.own, self.feat, self.width, self.classes = own, feat, width, classes
        self.feat_up = up(feat, 128)
        self.cls = up(classes, 16)
        self.plane = self.nx * self.ny
        self.one_rows = up(feat + 1, 16 * self.plane)
        self.two_rows = up(width + self.cls, 16 * self.plane)
        self.grad_rows = self.one_rows + self.two_rows
        self.lanes = width // self.nk
        units = self.one_rows // (16 * self.plane)
        chunks = min(3, units)
        cuts = [units * i // chunks * 16 * self.plane for i in range(chunks + 1)]
        self.chunks = list(zip(cuts, cuts[1:]))
        cuts = [own // 4 * i for i in range(5)]
        self.parts = [(start, stop - start) for start, stop in zip(cuts, cuts[1:])]
        self.nh = len(self.parts)
        self.relayed = self.nz == 4
        self.sends = 3 * (n_row + n_col) + 3 * self.plane
        wide = 2 * self.nh * (n_row + n_col)
        self.arrivals = wide + max(1, chunks - 1) * (1 + 3 * self.plane + self.nz) + 1 + self.plane + self.nz


def kernel(
    s,
    xt_ref,
    adj_ref,
    occ_ref,
    lab_ref,
    mask_ref,
    cnt_ref,
    w1_ref,
    w2_ref,
    w3t_ref,
    bias_ref,
    grad_ref,
    misc_ref,
    tile,
    w1b,
    w3t,
    xt_all,
    v_all,
    pool,
    xsend,
    zsend,
    zrecv,
    v3_all,
    p3send,
    p3recv,
    dl_all,
    q3send,
    q3recv,
    acc,
    half_send,
    half_recv,
    half,
    plane_recv,
    quarter,
    fin,
    misc_k,
    misc_p,
    misc_z,
    ssem,
    rsem,
    lsem,
):
    nx, ny, nz, nk = s.nx, s.ny, s.nz, s.nk
    own, width = s.own, s.width
    r, c = lax.axis_index("row"), lax.axis_index("col")
    z, x = r // nx, r % nx
    y, k = c // nk, c % nk

    def at(zz, xx, yy, kk):
        return (zz * nx + xx, yy * nk + kk)

    def xs(d):
        return lax.rem(x + d, nx)

    def ys(d):
        return lax.rem(y + d, ny)

    def zs(d):
        if nz & (nz - 1):
            return lax.rem(z + d, nz)
        there, bit = z, 1
        while bit < nz:
            if d & bit:
                there = there + bit - 2 * bit * lax.rem(there // bit, 2)
            bit *= 2
        return there

    def zback(d):
        return zs(d) if not nz & (nz - 1) else lax.rem(z + nz - d, nz)

    sibling = at(z, x, y, 1 - k)
    relayed = s.relayed
    is_inner = lax.rem((z + 1) // 2, 2)
    inner = is_inner == 1
    outer = is_inner == 0
    line = [dz for dz in range(nz - 1, -1, -1)]
    row_far = [(dz, dx) for dz in line for dx in range(nx - 1, -1, -1) if dz or dx]
    col_far = [(dy, dk) for dy in range(ny - 1, -1, -1) for dk in range(nk - 1, -1, -1) if dy or dk]

    def ks(d):
        return lax.rem(k + d, nk)


    rows, cols = tile.shape
    n_sub = rows // SUB
    loads = [
        pltpu.make_async_copy(
            adj_ref.at[pl.ds(a * SUB, SUB)], tile.at[pl.ds(a * SUB, SUB)], lsem.at[a]
        )
        for a in range(n_sub)
    ]
    for load in loads:
        load.start()

    peers = []
    for d in range(1, s.n_row):
        peers.append((lax.rem(r + d, s.n_row), c))
    for d in range(1, s.n_col):
        peers.append((r, lax.rem(c + d, s.n_col)))
    for dx in range(1, nx):
        for dy in range(1, ny):
            peers.append(at(z, xs(dx), ys(dy), k))
    barrier = pltpu.get_barrier_semaphore()
    for peer in peers:
        pl.semaphore_signal(barrier, inc=1, device_id=peer, device_id_type=MESH)

    free = list(range(s.sends))
    pending = []

    def send(src, dst, recv_slot, device, of=None, when=None, start=True):
        if not free:
            settle(len(pending) - 1)
        copy = pltpu.make_async_remote_copy(
            src_ref=src,
            dst_ref=dst,
            send_sem=ssem.at[free[0]],
            recv_sem=rsem.at[recv_slot],
            device_id=device,
            device_id_type=MESH,
        )
        if start:
            if when is None:
                copy.start()
            else:
                pl.when(when)(copy.start)
        pending.append((copy, free.pop(0), of, when))
        return copy

    def arrived(dst, recv_slot):
        pltpu.make_async_remote_copy(
            src_ref=dst,
            dst_ref=dst,
            send_sem=ssem.at[0],
            recv_sem=rsem.at[recv_slot],
            device_id=sibling,
            device_id_type=MESH,
        ).wait_recv()

    def settle(keep=0, of=None):
        done = [p for p in pending if p[2] == of] if of else pending[: len(pending) - keep]
        for item in done:
            if item[3] is None:
                item[0].wait_send()
            else:
                pl.when(item[3])(item[0].wait_send)
            free.append(item[1])
        left = [p for p in pending if all(p is not q for q in done)]
        pending[:] = left

    rcount = [0]

    def rslots(n):
        rcount[0] += n
        return rcount[0] - n

    def row_block(index):
        return pl.ds(pl.multiple_of(index * own, own), own)

    nh = s.nh

    def row_part(index, q):
        start, count = s.parts[q]
        return pl.ds(pl.multiple_of(index * own + start, count), count)

    def part(q):
        return pl.ds(*s.parts[q])

    def span_of(q):
        start, count = s.parts[q]
        return slice(start, start + count)

    valid_col = (lax.broadcasted_iota(jnp.int32, (own, width), 0) < cnt_ref[0]).astype(FULL)
    valid_low = valid_col.astype(LOW)
    valid_row = (lax.broadcasted_iota(jnp.int32, (1, own), 1) < cnt_ref[0]).astype(FULL)
    counted = mask_ref[...].astype(FULL) * valid_row

    prologue = jax.named_scope("prologue")
    prologue.__enter__()
    pad = s.feat_up - up(s.feat, 16) + 16
    own_xt = xt_all.at[c]
    own_xt[s.feat_up - pad :, :] = jnp.zeros((pad, own), LOW)
    w1b[s.feat_up - pad :, :] = jnp.zeros((pad, width), LOW)
    x_valid = (lax.broadcasted_iota(jnp.int32, (s.feat, own), 1) < cnt_ref[0]).astype(LOW)
    own_xt[: s.feat, :] = xt_ref[...] * x_valid
    w1b[: s.feat, :] = w1_ref[...].astype(LOW)
    y1 = lax.dot_general(
        own_xt[...], w1b[...], (((0,), (0,)), ((), ())), preferred_element_type=FULL
    ).astype(LOW)
    v_all[0, row_block(c), :] = y1

    wide = [rslots(s.n_row * nh) for _ in range(2)]
    gbase = [rslots(s.n_col * nh) for _ in range(2)]
    prologue.__exit__(None, None, None)

    def start_gather(hop, q, values):
        mine = v_all.at[hop, row_part(c, q)]
        if values is not None:
            mine[...] = values
        for d in range(1, ny):
            send(mine, mine, gbase[hop] + c * nh + q, at(z, x, ys(d), k))
        if nk > 1:
            send(mine, mine, gbase[hop] + c * nh + q, sibling)

    def complete_gather(hop, meanwhile):
        for q in range(nh):
            for d in range(1, ny):
                source = ys(ny - d) * nk + k
                block = v_all.at[hop, row_part(source, q)]
                arrived(block, gbase[hop] + source * nh + q)
                if nk > 1:
                    send(block, block, gbase[hop] + source * nh + q, sibling)
        for d in range(ny if nk > 1 else 0):
            if d == 1:
                meanwhile()
            source = ys(d) * nk + 1 - k
            for q in range(nh):
                arrived(v_all.at[hop, row_part(source, q)], gbase[hop] + source * nh + q)

    with jax.named_scope("barrier"):
        pl.semaphore_wait(barrier, len(peers))
    for q in range(nh):
        start_gather(0, q, None)

    if relayed:

        @pl.when(outer)
        def _():
            zrecv[:, 2] = jnp.zeros((2, own, width), LOW)

    w3t[...] = jnp.zeros_like(w3t)
    w3t[: s.classes, :] = w3t_ref[...].astype(LOW)
    w2 = w2_ref[...].astype(LOW)
    for a in range(n_sub):
        loads[a].wait()
        for b in range(cols // own):
            piece = tile[pl.ds(a * SUB, SUB), pl.ds(b * own, own)]
            cover = jnp.full((SUB, own), occ_ref[a, b].astype(FULL), FULL).astype(LOW)
            tile[pl.ds(a * SUB, SUB), pl.ds(b * own, own)] = piece * cover

    def spread(hop, finish):
        settle(of="hop")
        start_z = nz - 1
        begun = []
        late = [ys(d) * nk + 1 - k for d in range(1, ny)] if nk > 1 else []
        soon = [ys(d) * nk + k for d in range(ny)] + ([y * nk + 1 - k] if nk > 1 else [])

        def some(sources):
            first_rows = row_block(zs(start_z) * nx + xs(1))
            total = None
            for source in sources:
                here = dot(
                    tile[first_rows, row_block(source)], v_all[hop, row_block(source), :]
                )
                total = here if total is None else total + here
            return total

        split = nx > 1 and nk > 1 and ny > 1
        with jax.named_scope("gather_y"):
            complete_gather(hop, lambda: begun.append(some(soon)) if split else None)
        zbase = wide[hop]
        xbase = zbase + nz * nh
        order = list(range(nz - 1, -1, -1))

        def send_x(dz, dx, q):
            place = (dx - 1) * nz + dz
            send(
                xsend.at[place, part(q)],
                pool.at[hop * s.n_row + place, part(q)],
                xbase + place * nh + q,
                at(z, xs(dx), y, k),
                "hop",
            )

        sequence = []
        if relayed:
            sequence = [(3, 0), (3, 1), (2, 0), (3, 2), (2, 1), (3, 3), (1, 0), (2, 2), (1, 1), (2, 3), (1, 2), (1, 3), (0, 0), (0, 1), (0, 2), (0, 3)]
        else:
            for q in range(nh):
                sequence += [(dz, q) for dz in order if dz]
                if q:
                    sequence.append((0, q - 1))
            sequence.append((0, nh - 1))
        ready = set()
        with jax.named_scope("send_x"):
            for dz, q in sequence:
                for dx in range(1, nx):
                    if (dz, dx) not in ready:
                        ready.add((dz, dx))
                        rt = zs(dz) * nx + xs(dx)
                        if split and (dz, dx) == (start_z, 1):
                            here = begun[0] + some(late)
                        else:
                            here = dot(tile[row_block(rt), :], v_all[hop])
                        xsend[(dx - 1) * nz + dz] = here.astype(LOW)
                    send_x(dz, dx, q)
            for dz in order:
                acc[:, dz * own : (dz + 1) * own] = dot(
                    tile[row_block(zs(dz) * nx + x), :], v_all[hop]
                )

        def send_z(dz, q):
            rows_q = span_of(q)
            total = acc[rows_q, dz * own : (dz + 1) * own]
            for dx in range(1, nx):
                place = (dx - 1) * nz + dz
                arrived(pool.at[hop * s.n_row + place, part(q)], xbase + place * nh + q)
                total = total + pool[hop * s.n_row + place, rows_q, :].astype(FULL)
            if not dz:
                return total
            there, slot, mark = zs(dz), dz - 1, zbase + dz * nh + q
            if relayed and dz == 3:
                there = is_inner * zs(3) + (1 - is_inner) * zs(1)
                slot, mark = 3 - is_inner, zbase + 3 * nh * is_inner + q
            if relayed and dz == 2:

                @pl.when(inner)
                def _():
                    arrived(zrecv.at[hop, 3, part(q)], zbase + q)
                    handed = zrecv[hop, 3, rows_q, :].astype(FULL)
                    zsend[dz - 1, rows_q, :] = (total + handed).astype(LOW)

                @pl.when(outer)
                def _():
                    zsend[dz - 1, rows_q, :] = total.astype(LOW)

            else:
                zsend[dz - 1, rows_q, :] = total.astype(LOW)
            send(
                zsend.at[dz - 1, part(q)],
                zrecv.at[hop, slot, part(q)],
                mark,
                at(there, x, y, k),
                "hop",
            )
            return total

        totals = [None] * nh

        def sum_z(q):
            total = totals[q]
            rows_q = span_of(q)
            for dz in range(1, nz):
                there, mark = zrecv.at[hop, dz - 1, part(q)], zbase + dz * nh + q
                if relayed and dz == 3:
                    pl.when(inner)(functools.partial(arrived, there, mark))
                else:
                    arrived(there, mark)
                total = total + zrecv[hop, dz - 1, rows_q, :].astype(FULL)
            finish(q, total)

        with jax.named_scope("send_z"):
            for dz, q in sequence[:-1]:
                totals[q] = send_z(dz, q)
                if not dz:
                    with jax.named_scope("sum_z0"):
                        sum_z(q)
        with jax.named_scope("sum_z1"):
            totals[nh - 1] = send_z(0, nh - 1)
            sum_z(nh - 1)

    bias = [bias_ref[i * width : (i + 1) * width].reshape(1, width) for i in range(2)]
    acts = [None] * nh

    def first_done(q, total):
        rows_q = span_of(q)
        z1 = total + v_all[0, row_part(c, q), :].astype(FULL) + bias[0]
        h1 = gelu_both(z1)[0].astype(LOW) * valid_low[rows_q]
        start_gather(1, q, dot(h1, w2).astype(LOW))
        acts[q] = h1
        acc[rows_q, :width] = z1

    spread(0, first_done)
    h1t = jnp.concatenate(acts, axis=0).astype(FULL).T.astype(LOW)
    slope1t = (gelu_both(acc[:, :width])[1] * valid_col).T

    xt_base = gbase[1] + s.n_col

    def second_done(q, total):
        rows_q = span_of(q)
        z2 = total + v_all[1, row_part(c, q), :].astype(FULL) + bias[1]
        acts[q] = gelu_both(z2)[0].astype(LOW) * valid_low[rows_q]
        acc[rows_q, :width] = z2
        ends = span_of(q).stop
        if ends % (own // 2) == 0:
            lane = 2 * ends // own - 1
            some = [act for i, act in enumerate(acts[: q + 1]) if span_of(i).start >= ends - own // 2]
            some = jnp.concatenate(some, axis=0)
            y3t = dot_nt(w3t[...], some).astype(LOW)
            mine = v3_half(c, lane)
            mine[...] = y3t
            for dy, dk in col_far:
                send(mine, mine, gbase[0] + 2 * c + lane, (r, ys(dy) * nk + ks(dk)))

    def v3_half(index, lane):
        return v3_all.at[index, :, pl.ds(lane * (own // 2), own // 2)]

    spread(1, second_done)
    h2 = jnp.concatenate(acts, axis=0)

    with jax.named_scope("hop3_gather"):
        slope2t = (gelu_both(acc[:, :width])[1] * valid_col).T
        settle(s.n_col - 1)
        for lane in range(2):
            for dy, dk in reversed(col_far):
                source = ys(ny - dy) * nk + ks(nk - dk)
                arrived(v3_half(source, lane), gbase[0] + 2 * source + lane)
    with jax.named_scope("hop3_sum"):
        pbase = wide[0]
        v3 = jnp.concatenate([v3_all[i] for i in range(s.n_col)], axis=1)
        for dz, dx in row_far:
            place = dz * nx + dx
            rt = zs(dz) * nx + xs(dx)
            p3send[place] = dot_nt(v3, tile[row_block(rt), :]).astype(LOW)
            send(p3send.at[place], p3recv.at[place], pbase + place, (rt, c))
        total = dot_nt(v3, tile[row_block(r), :])
        for dz, dx in reversed(row_far):
            place = dz * nx + dx
            arrived(p3recv.at[place], pbase + place)
            total = total + p3recv[place].astype(FULL)
    total = total + v3_all[c].astype(FULL)

    place = lax.broadcasted_iota(jnp.int32, (s.cls, own), 0)
    real = place < s.classes
    on_diag = lax.broadcasted_iota(jnp.int32, (s.cls, s.classes), 0) == lax.broadcasted_iota(
        jnp.int32, (s.cls, s.classes), 1
    )
    bias3 = jnp.sum(
        jnp.where(on_diag, bias_ref[2 * width :].reshape(1, s.classes), 0.0), axis=1, keepdims=True
    )
    logits = jnp.where(real, total + bias3, -1e30)
    shifted = logits - jnp.max(logits, axis=0, keepdims=True)
    weight = jnp.where(real, jnp.exp(shifted), 0.0)
    norm = jnp.sum(weight, axis=0, keepdims=True)
    logp = shifted - jnp.log(norm)
    target = jnp.where(place == lab_ref[...], 1.0 - SMOOTH, 0.0) + SMOOTH / s.classes
    target = jnp.where(real, target, 0.0)
    row_loss = -jnp.sum(jnp.where(real, target * logp, 0.0), axis=0, keepdims=True)
    loss = jnp.sum(row_loss * counted, axis=1, keepdims=True)
    number = jnp.sum(counted, axis=1, keepdims=True)
    dlt = ((weight / norm - target) * counted).astype(LOW)

    with jax.named_scope("back3_gather"):
        base = wide[1]
        mine = dl_all.at[r]
        mine[...] = dlt
        for dz, dx in row_far:
            send(mine, mine, base + r, (zs(dz) * nx + xs(dx), c))
        here = dot(dlt, tile[row_block(r), :])
        for dz, dx in reversed(row_far):
            source = zback(dz) * nx + xs(nx - dx)
            arrived(dl_all.at[source], base + source)
            here = here + dot(dl_all[source], tile[row_block(source), :])
        acc[: s.cls, :cols] = here
    with jax.named_scope("back3_sum"):
        qbase = gbase[1]
        for dy, dk in col_far:
            place = dy * nk + dk
            ct = ys(dy) * nk + ks(dk)
            q3send[place] = acc[: s.cls, row_block(ct)].astype(LOW)
            send(q3send.at[place], q3recv.at[place], qbase + place, (r, ct))
        total = dlt.astype(FULL) + acc[: s.cls, row_block(c)]
        for dy, dk in reversed(col_far):
            place = dy * nk + dk
            arrived(q3recv.at[place], qbase + place)
            total = total + q3recv[place].astype(FULL)
    qt = total.astype(LOW)
    dh2t = lax.dot_general(
        w3t[...], qt, (((0,), (0,)), ((), ())), preferred_element_type=FULL
    )
    step_cols = min(cols, 1024)

    def gained(values, block, fresh=False):
        for j in range(0, cols, step_cols):
            here = dot(values, tile[block, j : j + step_cols])
            if fresh:
                acc[:, j : j + step_cols] = here
            else:
                acc[:, j : j + step_cols] += here

    def halves(lane, row):
        return (
            pl.ds(row * (width // 2), width // 2),
            pl.ds(lane * (own // 2), own // 2),
        )

    quarters = [(lane, row) for lane in range(2) for row in range(2)]
    def receive(hop, values, meanwhile=None, late=None):
        base, np = wide[hop], len(quarters)
        first = hop * s.n_row

        def piece(dz, dx, q):
            return pool.at[(first + dx * nz + dz, *halves(*quarters[q]))]

        def to_z(dz, q, when=None, start=True):
            return send(
                piece(0, 0, q),
                piece(dz, 0, q),
                base + dz * np + q,
                at(zs(dz), x, y, k),
                when=when,
                start=start,
            )

        def to_x(dz, q, start=True):
            return [
                send(
                    piece(dz, 0, q),
                    piece(dz, dx, q),
                    base + (dx * nz + dz) * np + q,
                    at(z, xs(dx), y, k),
                    start=start,
                )
                for dx in range(1, nx)
            ]

        own_parts = []
        for lane in range(2):
            mine = values(lane)
            own_parts.append(mine)
            pool[first, :, lane * (own // 2) : (lane + 1) * (own // 2)] = mine
            for q in (2 * lane, 2 * lane + 1):
                to_x(0, q)
                if relayed:
                    to_z(2, q)
                    to_z(1, q)
                else:
                    for dz in range(nz - 1, 0, -1):
                        to_z(dz, q)

        def source(dz, dx):
            return row_block(zback(dz) * nx + xs(nx - dx))

        gained(jnp.concatenate(own_parts, axis=1), row_block(r), fresh=True)
        if meanwhile is not None:
            meanwhile()

        passing = {
            (dz, q): to_x(dz, q, start=False) for q in range(np) for dz in range(1, nz)
        }

        def step(dz, q):
            arrived(piece(dz, 0, q), base + dz * np + q)
            for copy in passing[dz, q]:
                copy.start()

        if relayed:
            relays = [
                send(
                    piece(2, 0, q),
                    piece(3, 0, q),
                    base + 3 * np + q,
                    at(zs(1), x, y, k),
                    when=inner,
                    start=False,
                )
                for q in range(np)
            ]
            paced = [to_z(3, q, inner, start=False) for q in range(np)]

            @pl.when(inner)
            def _():
                for q in range(np):
                    arrived(piece(2, 0, q), base + 2 * np + q)
                    relays[q].start()
                    paced[q].start()
                    for copy in passing[2, q]:
                        copy.start()
                    step(1, q)
                    if q > 1:
                        step(3, q - 2)
                for q in range(np - 2, np):
                    step(3, q)

            @pl.when(outer)
            def _():
                for q in range(np + 2):
                    if q < np:
                        step(1, q)
                    if 0 < q <= np:
                        step(2, q - 1)
                    if q > 2:
                        step(3, q - 3)
                for q in range(np - 1, np):
                    step(3, q)
        else:
            for q in range(np):
                for dz in range(1, nz):
                    step(dz, q)
        for dz in range(1, nz):
            gained(pool[first + dz], source(dz, 0))
        if late is not None:
            late()
        for dz in range(nz):
            for dx in range(1, nx):
                for q in range(np):
                    arrived(piece(dz, dx, q), base + (dx * nz + dz) * np + q)
                gained(pool[first + dx * nz + dz], source(dz, dx))

    dz2t = (dh2t * slope2t).astype(LOW)
    half_own = own // 2

    def features_out():
        for d in range(1, ny):
            send(own_xt, own_xt, xt_base + c, at(z, x, ys(d), k))
        if nk > 1:
            send(own_xt, own_xt, xt_base + c, sibling)

    with jax.named_scope("back2_rows"):
        settle()
        receive(0, lambda lane: dz2t[:, lane * half_own : (lane + 1) * half_own], features_out)
    cbase = gbase[0] + 2 * s.n_col
    ybase = gbase[1] + 2 * s.n_col

    def lane_part(index, lane):
        return pl.ds(pl.multiple_of(index * own + lane * half_own, half_own), half_own)

    def held(place, lane):
        return xsend.at[place, :, pl.ds(lane * half_own, half_own)]

    def crecv(dy, lane):
        return v_all.at[0, dy * own : (dy + 1) * own, pl.ds(lane * half_own, half_own)]

    def yrecv(dy, lane):
        return crecv(dy + (ny if nk > 1 else 0), lane)

    column_totals = [None, None]
    with jax.named_scope("back2_cols"):
        for lane in range(2):
            for dy in range(ny - 1, -1, -1):
                if nk > 1:
                    there = held(dy, lane)
                    there[...] = acc[:, lane_part(ys(dy) * nk + 1 - k, lane)].astype(LOW)
                    send(there, crecv(dy, lane), cbase + 2 * dy + lane, sibling)
        for lane in range(2):
            for dy in range(ny - 1, -1, -1):
                here = acc[:, lane_part(ys(dy) * nk + k, lane)]
                if nk > 1:
                    arrived(crecv(dy, lane), cbase + 2 * dy + lane)
                    here = here + crecv(dy, lane)[...].astype(FULL)
                if dy:
                    there = held(ny + dy, lane)
                    there[...] = here.astype(LOW)
                    send(
                        there, yrecv(dy, lane), ybase + 2 * dy + lane, at(z, x, ys(dy), k)
                    )
                else:
                    column_totals[lane] = here
        for d in range(1, ny):
            source = ys(ny - d) * nk + k
            arrived(xt_all.at[source], xt_base + source)
            if nk > 1:
                send(xt_all.at[source], xt_all.at[source], xt_base + source, sibling)

    dy2_parts, dz1_parts = [], []

    def first_slopes(lane):
        lanes_q = slice(lane * half_own, (lane + 1) * half_own)
        total = column_totals[lane] + dz2t[:, lanes_q].astype(FULL)
        with jax.named_scope("y_wait"):
            for dy in range(1, ny):
                arrived(yrecv(dy, lane), ybase + 2 * dy + lane)
                total = total + yrecv(dy, lane)[...].astype(FULL)
        dy2_parts.append(total.astype(LOW))
        dz1_parts.append((dot(w2, dy2_parts[lane]) * slope1t[:, lanes_q]).astype(LOW))
        return dz1_parts[lane]

    lanes, plane = s.lanes, s.plane
    me = y * nx + x
    others = [(dx, dy) for dx in range(nx - 1, -1, -1) for dy in range(ny - 1, -1, -1) if dx or dy]

    def lane_block(index):
        return pl.ds(pl.multiple_of(index * lanes, lanes), lanes)

    class Total:
        def __init__(self, start, rows, mark=None, base=None):
            self.all = pl.ds(start, rows)
            self.start, self.rows = start, rows
            self.n = rows // plane
            self.short = pl.ds(start // plane, self.n)
            self.mark = rslots(1) if mark is None else mark
            self.base = rslots(3 * plane + nz) if base is None else base

        def piece(self, index):
            return pl.ds(pl.multiple_of(self.start + index * self.n, 16), self.n)

        def core_send(self, other):
            if nk > 1:
                half_send[self.all, :] = other.astype(LOW)
                send(half_send.at[self.all], half_recv.at[self.all], self.mark, sibling)

        def plane_send(self, mine):
            if nk > 1:
                arrived(half_recv.at[self.all], self.mark)
                mine = mine + half_recv[self.all, :].astype(FULL)
            half[self.all, :] = mine.astype(LOW)
            base = self.base
            for dx, dy in others:
                there = ys(dy) * nx + xs(dx)
                send(
                    half.at[self.piece(there)],
                    plane_recv.at[me, self.short],
                    base + me,
                    at(z, xs(dx), ys(dy), k),
                )
            plane_recv[me, self.short, :] = half[self.piece(me), :]

        def line_send(self):
            base = self.base
            for dx, dy in others:
                there = ys(dy) * nx + xs(dx)
                arrived(plane_recv.at[there, self.short], base + there)
            total = plane_recv[0, self.short, :].astype(FULL)
            for i in range(1, plane):
                total = total + plane_recv[i, self.short, :].astype(FULL)
            quarter[z, self.short, :] = total.astype(LOW)
            mine = quarter.at[z, self.short]
            base = self.base + plane
            for dz in range(nz - 1, 0, -1):
                send(mine, mine, base + z, at(zs(dz), x, y, k))

        def back_send(self):
            base = self.base + plane
            for dz in range(1, nz):
                arrived(quarter.at[zback(dz), self.short], base + zback(dz))
            total = quarter[0, self.short, :].astype(FULL)
            for i in range(1, nz):
                total = total + quarter[i, self.short, :].astype(FULL)
            base = self.base + plane + nz
            mine = fin.at[k, self.piece(me)]
            mine[...] = total.astype(LOW)
            for dx, dy in others:
                send(mine, mine, base + me, at(z, xs(dx), ys(dy), k))
            if nk > 1:
                send(mine, mine, base + plane + me, sibling)

        def back_forward(self):
            base = self.base + plane + nz
            for dx, dy in others:
                there = ys(dy) * nx + xs(dx)
                block = fin.at[k, self.piece(there)]
                arrived(block, base + there)
                if nk > 1:
                    send(block, block, base + plane + there, sibling)

        def end(self):
            base = self.base + plane + nz
            if nk > 1:
                for i in range(plane):
                    arrived(fin.at[1 - k, self.piece(i)], base + plane + i)

    def write(start, count):
        grad_ref[:, start : start + count, :] = fin[:, start : start + count, :]

    ones_at = [
        (gbase[i] + 2 * s.n_col + 2 * ny, wide[0] + i * (3 * plane + nz)) for i in range(2)
    ]
    ones_at += [(None, None)] * len(s.chunks)
    assert 2 * (3 * plane + nz) <= s.n_row * nh
    one = [
        Total(start, stop - start, *there) for (start, stop), there in zip(s.chunks, ones_at)
    ]
    two = Total(s.one_rows, s.two_rows)
    tail = s.two_rows - width - s.cls

    ones = jnp.ones((8, own), LOW)
    row = lax.broadcasted_iota(jnp.int32, (8, width), 0)
    lane_of = lax.broadcasted_iota(jnp.int32, (8, width), 1)
    bias_three = jnp.concatenate([dlt, jnp.zeros((width - s.cls, own), LOW)], axis=0)
    misc = jnp.where(row == 1, dot_nt(ones, dz2t), 0.0)
    misc = jnp.where(row == 2, dot_nt(ones, bias_three), misc)
    misc = jnp.where((row == 3) & (lane_of == 0), loss, misc)
    misc = jnp.where((row == 3) & (lane_of == 1), number, misc)
    mbase = rslots(1 + plane + nz)
    plane_base, line_base = mbase + 1, mbase + 1 + plane

    def early():
        misc_k[0] = misc
        if nk > 1:
            send(misc_k.at[0], misc_k.at[1], mbase, sibling)
        grad3t = dot(qt, h2)
        dy2t = jnp.concatenate(dy2_parts, axis=1)
        grad2 = dot_nt(h1t, dy2t)
        acc_two = jnp.concatenate(
            [grad2, grad3t] + ([jnp.zeros((tail, width), FULL)] if tail else []), axis=0
        )
        if nk > 1:
            first, second = acc_two[:, :lanes], acc_two[:, lanes:]
            low_core = (k == 0).astype(FULL)
            two.core_send(second * low_core + first * (1.0 - low_core))
            two.plane_send(first * low_core + second * (1.0 - low_core))
        else:
            two.plane_send(acc_two)
        here = misc_k[0]
        if nk > 1:
            arrived(misc_k.at[1], mbase)
            here = here + misc_k[1]
        misc_p[me] = here
        for dx, dy in others:
            send(misc_p.at[me], misc_p.at[me], plane_base + me, at(z, xs(dx), ys(dy), k))

    def late():
        two.line_send()
        for dx, dy in others:
            there = ys(dy) * nx + xs(dx)
            arrived(misc_p.at[there], plane_base + there)
        here = misc_p[0]
        for i in range(1, plane):
            here = here + misc_p[i]
        misc_z[z] = here
        for dz in range(1, nz):
            send(misc_z.at[z], misc_z.at[z], line_base + z, at(zs(dz), x, y, k))

    with jax.named_scope("back1_rows"):
        receive(1, first_slopes, early, late)
    with jax.named_scope("grad1"):
        dz1t = jnp.concatenate(dz1_parts, axis=1)
        acc[:, row_block(c)] += dz1t.astype(FULL)
        if nk > 1:
            for d in range(ny):
                source = ys(d) * nk + 1 - k
                arrived(xt_all.at[source], xt_base + source)

        low_core = (k == 0).astype(FULL)
        bias_one = dot_nt(ones, dz1t)[0:1, :]

        def grad_one(start, stop):
            total = None
            end = min(stop, s.feat_up)
            for i in range(s.n_col):
                here = acc[:, i * own : (i + 1) * own].astype(LOW)
                here = dot_nt(xt_all[i, start:end, :], here)
                total = here if total is None else total + here
            if end < stop:
                total = jnp.concatenate([total, jnp.zeros((stop - end, width), FULL)], axis=0)
            bias_at = s.feat - start
            if 0 <= bias_at < stop - start:
                places = lax.broadcasted_iota(jnp.int32, (stop - start, width), 0)
                total = jnp.where(places == bias_at, bias_one, total)
            if nk == 1:
                return None, total
            first, second = total[:, :lanes], total[:, lanes:]
            return (
                second * low_core + first * (1.0 - low_core),
                first * low_core + second * (1.0 - low_core),
            )

        waiting = None
        for chunk, (start, stop) in zip(one, s.chunks):
            other, mine = grad_one(start, stop)
            chunk.core_send(other)
            if waiting is not None:
                waiting()
            waiting = functools.partial(chunk.plane_send, mine)
        waiting()

    with jax.named_scope("sum_plane"):
        left = len(pending)
        two.back_send()
    with jax.named_scope("sum_line"):
        for chunk in one:
            chunk.line_send()
    with jax.named_scope("back_line"):
        for chunk in one:
            chunk.back_send()
        for dz in range(1, nz):
            arrived(misc_z.at[zback(dz)], line_base + zback(dz))
        misc = misc_z[0]
        for i in range(1, nz):
            misc = misc + misc_z[i]
        misc_ref[...] = jnp.where(row == 4, 1.0 / misc[3:4, 1:2], misc)
        settle(len(pending) - left)
    with jax.named_scope("back_plane"):
        for chunk in one:
            chunk.back_forward()
        two.back_forward()
        for chunk in one:
            chunk.end()
            write(chunk.start, chunk.rows)
        two.end()
        write(s.one_rows, s.two_rows)
    with jax.named_scope("settle"):
        settle()
    assert rcount[0] <= s.arrivals


def update_pieces(s):
    some = up(s.feat // 4, 16)
    cuts = [min(i * some, s.feat) for i in range(5)]
    one = [(0, start, stop - start) for start, stop in zip(cuts, cuts[1:]) if stop > start]
    return (*one, (1, 0, s.width), (2, 0, s.classes))


def adam_kernel(s, grad_ref, misc_ref, *refs):
    ins, outs, scratch = refs[:12], refs[12:26], refs[26:]
    bias_out, ends, *held = scratch[:-1]
    sem_out = scratch[-1]
    width, classes, lanes = s.width, s.classes, s.lanes
    grad_at = (0, s.one_rows, s.one_rows + width)

    stores = []

    def store(source, target):
        copy = pltpu.make_async_copy(source, target, sem_out.at[len(stores)])
        copy.start()
        stores.append(copy)

    total = misc_ref[3:4, 1:2]
    scale = misc_ref[4:5, 0:1]
    for (which, start, rows), target in zip(update_pieces(s), held):
        span = slice(start, start + rows)
        for i in range(s.nk):
            lane = slice(i * lanes, (i + 1) * lanes)
            first = grad_at[which] + start
            grad = grad_ref[i, first : first + up(rows, 16), :].astype(FULL)[:rows]
            weight, one, two = (ins[3 * which + j][span, lane] for j in range(3))
            for j, new in enumerate(adam_update(weight, one, two, grad * scale)):
                target[j, :, lane] = new
        for j in range(3):
            store(target.at[j], outs[3 * which + j].at[pl.ds(start, rows)])
    for i, size in enumerate((width, width, classes)):
        span = slice(i * width, i * width + size)
        weight, first, second = (ins[9 + j][span] for j in range(3))
        grad = misc_ref[i, :size]
        if not i:
            top = s.feat // 16 * 16
            rows = [grad_ref[j, top : top + 16, :].astype(FULL) for j in range(s.nk)]
            grad = jnp.concatenate([a[s.feat - top] for a in rows])
        new = adam_update(weight, first, second, grad * misc_ref[4, :size])
        for j in range(3):
            bias_out[j][span] = new[j]
    for j in range(3):
        store(bias_out[j], outs[9 + j])
    ends[0] = misc_ref[3:4, 0:1]
    ends[1] = total
    for i in range(2):
        store(ends.at[i], outs[12 + i])
    for copy in stores:
        copy.wait()


def shards(
    sizes,
    features,
    adjacency,
    occupancy,
    labels,
    train_mask,
    node_count,
    weight_one,
    weight_two,
    weight_three,
    biases,
    first_one,
    first_two,
    first_three,
    first_bias,
    second_one,
    second_two,
    second_three,
    second_bias,
):
    own, feat = features.shape
    width = weight_two.shape[0]
    classes = weight_three.shape[1]
    s = sizes(own, feat, width, classes)
    rows, cols = adjacency.shape
    lanes = s.lanes
    vmem = pl.BlockSpec(memory_space=pltpu.VMEM)
    smem = pl.BlockSpec(memory_space=pltpu.SMEM)
    anywhere = pl.BlockSpec(memory_space=pl.ANY)
    block = (own, width)
    small = (s.cls, own)
    shapes = [
        ((rows, cols), LOW),
        ((s.feat_up, width), LOW),
        ((s.cls, width), LOW),
        ((s.n_col, s.feat_up, own), LOW),
        ((2, s.n_col * own, width), LOW),
        ((2 * s.n_row, *block), LOW),
        ((max(2 * s.ny, s.n_row - s.nz), *block), LOW),
        ((max(1, s.nz - 1), *block), LOW),
        ((2, s.nz if s.relayed else max(1, s.nz - 1), *block), LOW),
        ((s.n_col, *small), LOW),
        ((s.n_row, *small), LOW),
        ((s.n_row, *small), LOW),
        ((s.n_row, *small), LOW),
        ((s.n_col, *small), LOW),
        ((s.n_col, *small), LOW),
        ((width, max(cols, s.nz * own)), FULL),
        ((s.grad_rows, lanes), LOW),
        ((s.grad_rows, lanes), LOW),
        ((s.grad_rows, lanes), LOW),
        ((s.plane, s.grad_rows // s.plane, lanes), LOW),
        ((s.nz, s.grad_rows // s.plane, lanes), LOW),
        ((s.nk, s.grad_rows, lanes), LOW),
        ((2, 8, width), FULL),
        ((s.plane, 8, width), FULL),
        ((s.nz, 8, width), FULL),
    ]
    bytes_held = sum(math.prod(shape) * jnp.dtype(kind).itemsize for shape, kind in shapes)
    limit = min(62, 16 + bytes_held // 2**20) * 2**20
    grads, misc = pl.pallas_call(
        functools.partial(kernel, s),
        out_shape=(
            pltpu.VMEM((s.nk, s.grad_rows, lanes), LOW),
            pltpu.VMEM((8, width), FULL),
        ),
        in_specs=[
            vmem,
            anywhere,
            smem,
            vmem,
            vmem,
            smem,
            vmem,
            vmem,
            vmem,
            vmem,
        ],
        out_specs=(vmem, vmem),
        scratch_shapes=[
            *[pltpu.VMEM(shape, kind) for shape, kind in shapes],
            pltpu.SemaphoreType.DMA((s.sends,)),
            pltpu.SemaphoreType.DMA((s.arrivals,)),
            pltpu.SemaphoreType.DMA((rows // SUB,)),
        ],
        compiler_params=pltpu.CompilerParams(
            collective_id=0, has_side_effects=True, vmem_limit_bytes=limit
        ),
        cost_estimate=pl.CostEstimate(
            flops=12 * rows * cols * width, bytes_accessed=2 * rows * cols, transcendentals=0
        ),
        name="step",
    )(
        *[
            pltpu.with_memory_space_constraint(a, pltpu.HBM)
            for a in (features.T, adjacency)
        ],
        pltpu.with_memory_space_constraint(occupancy, pltpu.HBM),
        *[
            pltpu.with_memory_space_constraint(a, pltpu.HBM)
            for a in (labels.reshape(1, own), train_mask.reshape(1, own))
        ],
        node_count,
        *[
            pltpu.with_memory_space_constraint(a, pltpu.HBM)
            for a in (weight_one, weight_two, weight_three.T, biases)
        ],
    )
    state = (
        weight_one,
        first_one,
        second_one,
        weight_two,
        first_two,
        second_two,
        weight_three.T,
        first_three.T,
        second_three.T,
        biases,
        first_bias,
        second_bias,
    )
    new = pl.pallas_call(
        functools.partial(adam_kernel, s),
        out_shape=(
            *[jax.ShapeDtypeStruct(a.shape, FULL) for a in state],
            jax.ShapeDtypeStruct((1, 1), FULL),
            jax.ShapeDtypeStruct((1, 1), FULL),
        ),
        in_specs=[vmem] * 14,
        out_specs=(anywhere,) * 14,
        scratch_shapes=[
            [pltpu.VMEM(biases.shape, FULL)] * 3,
            pltpu.VMEM((2, 1, 1), FULL),
            *[pltpu.VMEM((3, rows, width), FULL) for _, _, rows in update_pieces(s)],
            pltpu.SemaphoreType.DMA((3 * len(update_pieces(s)) + 5,)),
        ],
        compiler_params=pltpu.CompilerParams(vmem_limit_bytes=32 * 2**20),
        name="update",
    )(grads, misc, *state)
    return (
        *new[:6],
        *[a.T for a in new[6:9]],
        *new[9:12],
        new[12].reshape(()),
        new[13].reshape(()),
    )


def solution(mesh):
    placed = (
        P(("row", "col"), None),
        P("col", "row"),
        P("col", "row"),
        P(("row", "col")),
        P(("row", "col")),
        P(("row", "col")),
        *[P()] * 12,
    )
    sizes = functools.partial(Sizes, mesh.shape["row"], mesh.shape["col"])
    return jax.shard_map(
        functools.partial(shards, sizes),
        mesh=mesh,
        in_specs=placed,
        out_specs=(P(),) * 14,
        check_vma=False,
    )
```
